128 devices in a mesh: dp: 8 (over z, core), dom: 16 (over x, y).
Axes of the slice: x: 4, y: 4, z: 4, core: 2. Of those that a mesh axis runs over, the one named last changes fastest.
Arguments:
- hidden: bfloat16 [2048, 16, 1024], P(('dp', 'dom')), may hold values from -6 to 6
- desc_len: int32 [2048], P(('dp', 'dom')), may hold values from 1 to 16
- w_in: bfloat16 [1024, 4096], P(None, 'dom'), may hold values from -0.1875 to 0.1875
- w_out: bfloat16 [4096, 1024], P('dom'), may hold values from -0.09375 to 0.09375
- send_order: int32 [128, 16], P(('dp', 'dom')), may hold values from 0 to 15, each once within a row
- place_order: int32 [128, 16], P(('dp', 'dom')), may hold values from 0 to 15, each once within a row
- cache: bfloat16 [30720, 1024], P(('dp', 'dom')), may hold values from -6 to 6
- halo_rows: int32 [128, 128], P(('dp', 'dom')), may hold values from 0 to 255
- edge_src: int32 [128, 2048], P(('dp', 'dom')), may hold values from 0 to 383
- edge_dst: int32 [128, 2048], P(('dp', 'dom')), may hold values from 0 to 255
- edge_rel: int32 [128, 16], P(('dp', 'dom')), may hold values from 0 to 831
- rel_table: bfloat16 [832, 1024], P('dom'), may hold values from -6 to 6
- w_msg: bfloat16 [1024, 1024], replicated, may hold values from -0.1875 to 0.1875
- w_self: bfloat16 [1024, 1024], replicated, may hold values from -0.1875 to 0.1875
- d_out: bfloat16 [32768, 1024], P(('dp', 'dom')), may hold values from -0.0625 to 0.0625
Outputs:
- graph_out: bfloat16 [32768, 1024], P(('dp', 'dom'))
- grad_w_in: float32 [1024, 4096], P(None, 'dom')
- grad_w_out: float32 [4096, 1024], P('dom')
- grad_rel: float32 [832, 1024], P('dom')
- grad_msg: float32 [1024, 1024], P(('dp', 'dom'))
- grad_self: float32 [1024, 1024], P(('dp', 'dom'))
The draws below stay inside these ranges and needn't reach their ends.
All inputs are finite; a program needn't handle non-finite values.
Results may differ from the reference program's by a relative error of at most 0.022.
Values may be sent and summed in bfloat16 or wider, within the bound.
No kernel may reach another device: no remote copies, remote signals or barrier semaphores. Data moves between devices by JAX's collectives and lax.ppermute only.
A program may use at most 128 MiB of HBM per device.

```python
import jax
import jax.numpy as jnp
from jax import lax

D = 1024
FF = 4096
NREL = 832
K = 1
HALO = 64
BLOCK = 128
LEN = 16
CACHE_DEV = 240
EDGE_BLOCKS = 16
E_DEV = 16
ENTITIES = 2048
NODE_DEV = 256
NODES = 32768
EDGES_DEV = 2048
N_DP = 8
N_DOM = 16


def with_ends(drawn, stream_key, least, largest):
    index_at = [jax.random.randint(jax.random.fold_in(stream_key, axis), (), 0, length) for axis, length in enumerate(drawn.shape)]
    longest = drawn.shape.index(max(drawn.shape))
    next_to = index_at[:longest] + [(index_at[longest] + 1) % drawn.shape[longest]] + index_at[longest + 1:]
    return drawn.at[tuple(index_at)].set(least).at[tuple(next_to)].set(largest)


def level_of(key, extent, pieces, smallest, top_value):
    level = 1.0
    for axis_at, blocks in pieces:
        heights = jax.random.uniform(jax.random.fold_in(jax.random.fold_in(key, 6), axis_at), (blocks,), jnp.float32, smallest / len(pieces), top_value / len(pieces))
        level = level * jnp.repeat(jnp.exp(heights), extent[axis_at] // blocks).reshape((-1,) + (1,) * (len(extent) - 1 - axis_at))
    return level


def scatter_about(key, shape, deviation, limit, pieces=(), kind=jnp.bfloat16):
    result = jax.random.normal(key, shape, jnp.float32) * deviation
    if len(pieces) > 0:
        result = level_of(key, shape, pieces, -0.22, 0.18) * result
    return jnp.clip(result, min=-limit, max=limit).astype(kind)


def setup_inputs(seed: int = 0) -> dict:
    key_list = jax.random.split(jax.random.key(seed), 16)
    hidden = scatter_about(key_list[0], (ENTITIES, LEN, D), 1.0, 6.0, ((0, 128),))
    desc_len = with_ends(jax.random.randint(key_list[1], (ENTITIES,), 1, LEN + 1), jax.random.fold_in(key_list[1], 1), 1, LEN).astype(jnp.int32)
    w_in = scatter_about(key_list[2], (D, FF), D ** -0.5, 0.1875, ((1, 16),))
    w_out = scatter_about(key_list[3], (FF, D), FF ** -0.5, 0.09375, ((0, 16),))
    send_order = jax.vmap(lambda own: jax.random.permutation(own, E_DEV))(jax.random.split(key_list[4], (N_DP * N_DOM))).reshape((N_DP * N_DOM, E_DEV)).astype(jnp.int32)
    place_order = jax.vmap(lambda own: jax.random.permutation(own, E_DEV))(jax.random.split(key_list[5], (N_DP * N_DOM))).reshape((N_DP * N_DOM, E_DEV)).astype(jnp.int32)
    cache = scatter_about(key_list[6], (N_DP * N_DOM * CACHE_DEV, D), 1.0, 6.0, ((0, 128),))
    halo_rows = with_ends(jax.random.randint(key_list[7], (N_DP * N_DOM, 2 * HALO), 0, NODE_DEV), jax.random.fold_in(key_list[7], 1), 0, NODE_DEV - 1).astype(jnp.int32)
    edge_src = with_ends(jax.random.randint(key_list[8], (N_DP * N_DOM, EDGES_DEV), 0, NODE_DEV + 2 * HALO), jax.random.fold_in(key_list[8], 1), 0, (NODE_DEV + 2 * HALO) - 1).astype(jnp.int32)
    edge_dst = with_ends(jax.random.randint(key_list[9], (N_DP * N_DOM, EDGES_DEV), 0, NODE_DEV), jax.random.fold_in(key_list[9], 1), 0, NODE_DEV - 1).astype(jnp.int32)
    edge_rel = with_ends(jax.random.randint(key_list[10], (N_DP * N_DOM, EDGE_BLOCKS), 0, NREL), jax.random.fold_in(key_list[10], 1), 0, NREL - 1).astype(jnp.int32)
    rel_table = scatter_about(key_list[11], (NREL, D), 1.0, 6.0, ((0, 16),))
    w_msg = scatter_about(key_list[12], (D, D), D ** -0.5, 0.1875)
    w_self = scatter_about(key_list[13], (D, D), D ** -0.5, 0.1875)
    d_out = scatter_about(key_list[14], (NODES, D), 0.01, 0.0625, ((0, 128),))
    return {"hidden": hidden, "desc_len": desc_len, "w_in": w_in, "w_out": w_out, "send_order": send_order, "place_order": place_order, "cache": cache, "halo_rows": halo_rows, "edge_src": edge_src, "edge_dst": edge_dst, "edge_rel": edge_rel, "rel_table": rel_table, "w_msg": w_msg, "w_self": w_self, "d_out": d_out}


def layer_norm(hidden):
    values = hidden.astype(jnp.float32)
    center = values - lax.optimization_barrier(jnp.mean(values, axis=-1, keepdims=True))
    spread = lax.optimization_barrier(jnp.mean(center * center, axis=-1, keepdims=True))
    return (center * lax.rsqrt(spread + 1e-05)).astype(jnp.bfloat16)

def local_graph(extended, nodes, src_one, dst_one, rel_rows, cot_one, w_msg, w_self):
    node_count = nodes.shape[0]
    edge_count = src_one.shape[0]
    scale_factor = (node_count / edge_count) ** 0.5
    rel_edges = jnp.repeat(rel_rows, BLOCK, axis=0).astype(jnp.float32)
    sources = jnp.take(extended, src_one, axis=0).astype(jnp.float32)
    messages = (sources * rel_edges).astype(jnp.bfloat16)
    summed = jax.ops.segment_sum(messages.astype(jnp.float32), dst_one, num_segments=node_count)
    aggregate = (scale_factor * summed).astype(jnp.bfloat16)
    out_pre = jnp.dot(aggregate, w_msg, preferred_element_type=jnp.float32) + jnp.dot(nodes, w_self, preferred_element_type=jnp.float32)
    squashed = jnp.tanh(out_pre)
    graph_out = squashed.astype(jnp.bfloat16)
    grad_pre = (cot_one.astype(jnp.float32) * (1.0 - squashed * squashed)).astype(jnp.bfloat16)
    grad_agg = (scale_factor * jnp.dot(grad_pre, w_msg.T, preferred_element_type=jnp.float32)).astype(jnp.bfloat16)
    at_dest = jnp.take(grad_agg, dst_one, axis=0).astype(jnp.float32)
    grad_src = (at_dest * rel_edges).astype(jnp.bfloat16)
    grad_blocks = lax.optimization_barrier(jnp.sum((at_dest * sources).reshape(-1, BLOCK, D), axis=1))
    grad_ext = jax.ops.segment_sum(grad_src.astype(jnp.float32), src_one, num_segments=extended.shape[0])
    grad_fresh = jnp.dot(grad_pre[:E_DEV], w_self.T, preferred_element_type=jnp.float32) + grad_ext[:E_DEV]
    return (graph_out, aggregate, grad_pre, grad_blocks, grad_ext, grad_fresh)

def reference(hidden, desc_len, w_in, w_out, send_order, place_order, cache, halo_rows, edge_src, edge_dst, edge_rel, rel_table, w_msg, w_self, d_out):
    groups = N_DP
    domains = N_DOM
    device_count = groups * domains
    normed = layer_norm(hidden)
    flat_normed = normed.reshape(ENTITIES * LEN, D)
    pre_act = jnp.dot(flat_normed, w_in, preferred_element_type=jnp.float32)
    activation = jax.nn.gelu(pre_act).astype(jnp.bfloat16)
    positions = jnp.arange(LEN, dtype=jnp.int32)
    token_mask = (positions[None, :] < desc_len[:, None]).astype(jnp.float32)
    inv_len = 1.0 / desc_len.astype(jnp.float32)
    pooled_act = jnp.einsum('etf,et->ef', activation.reshape(ENTITIES, LEN, FF).astype(jnp.float32), token_mask).astype(jnp.bfloat16)
    token_sum = jnp.dot(pooled_act, w_out, preferred_element_type=jnp.float32)
    hidden_sum = jnp.einsum('etd,et->ed', hidden.astype(jnp.float32), token_mask)
    pooled = ((hidden_sum + token_sum) * inv_len[:, None]).astype(jnp.bfloat16)
    pooled_grid = pooled.reshape(groups, domains, E_DEV, D)
    send_grid = send_order.reshape(groups, domains, E_DEV)
    place_grid = place_order.reshape(groups, domains, E_DEV)
    outgoing = jnp.take_along_axis(pooled_grid, send_grid[..., None], axis=2)
    arrived = outgoing.reshape(groups, domains, domains, K, D).transpose(0, 2, 1, 3, 4).reshape(groups, domains, E_DEV, D)
    fresh = jnp.take_along_axis(arrived, place_grid[..., None], axis=2)
    nodes = jnp.concatenate([fresh, cache.reshape(groups, domains, CACHE_DEV, D)], axis=2)
    halo_grid = halo_rows.reshape(groups, domains, 2 * HALO)
    boundary = jnp.take_along_axis(nodes, halo_grid[..., None], axis=2)
    from_left = jnp.roll(boundary[:, :, HALO:], 1, axis=1)
    from_right = jnp.roll(boundary[:, :, :HALO], -1, axis=1)
    extended = jnp.concatenate([nodes, from_left, from_right], axis=2)
    rel_rows_all = jnp.take(rel_table, edge_rel.reshape(-1), axis=0).reshape(device_count, EDGE_BLOCKS, D)

    def per_device(items):
        ext_one, nodes_one, src_one, dst_one, rel_one, cot_one = items
        return local_graph(ext_one, nodes_one, src_one, dst_one, rel_one, cot_one, w_msg, w_self)
    graph_out, aggregate, grad_pre, grad_blocks, grad_ext, grad_fresh = lax.map(per_device, (extended.reshape(device_count, NODE_DEV + 2 * HALO, D), nodes.reshape(device_count, NODE_DEV, D), edge_src, edge_dst, rel_rows_all, d_out.reshape(device_count, NODE_DEV, D)))
    all_pre = grad_pre.reshape(NODES, D)
    grad_msg = jnp.dot(aggregate.reshape(NODES, D).T, all_pre, preferred_element_type=jnp.float32)
    grad_self = jnp.dot(nodes.reshape(NODES, D).T, all_pre, preferred_element_type=jnp.float32)
    grad_rel = jax.ops.segment_sum(grad_blocks.reshape(-1, D), edge_rel.reshape(-1), num_segments=NREL)
    ext_grid = grad_ext.reshape(groups, domains, NODE_DEV + 2 * HALO, D)
    back_first = jnp.roll(ext_grid[:, :, NODE_DEV + HALO:], 1, axis=1)
    back_second = jnp.roll(ext_grid[:, :, NODE_DEV:NODE_DEV + HALO], -1, axis=1)
    returned = jnp.concatenate([back_first, back_second], axis=2).reshape(device_count, 2 * HALO, D)

    def fold_back(items):
        rows_one, values_one = items
        return jax.ops.segment_sum(values_one, rows_one, num_segments=NODE_DEV)[:E_DEV]
    grad_fresh = grad_fresh + lax.map(fold_back, (halo_rows, returned))

    def unplace(items):
        order_one, values_one = items
        return jnp.zeros((E_DEV, D), jnp.float32).at[order_one].set(values_one)
    grad_arrived = lax.map(unplace, (place_order, grad_fresh)).reshape(groups, domains, domains, K, D)
    grad_outgoing = grad_arrived.transpose(0, 2, 1, 3, 4).reshape(device_count, E_DEV, D)
    grad_pooled = lax.map(unplace, (send_order, grad_outgoing)).reshape(ENTITIES, D)
    scaled = (grad_pooled * inv_len[:, None]).astype(jnp.bfloat16)
    upstream = jnp.dot(scaled, w_out.T, preferred_element_type=jnp.float32)
    grad_act = token_mask[:, :, None] * upstream[:, None, :]
    grad_pre_act = jax.vjp(jax.nn.gelu, pre_act)[1](grad_act.reshape(ENTITIES * LEN, FF))[0].astype(jnp.bfloat16)
    grad_w_in = jnp.dot(flat_normed.T, grad_pre_act, preferred_element_type=jnp.float32)
    grad_w_out = jnp.dot(pooled_act.T, scaled, preferred_element_type=jnp.float32)
    return (graph_out.reshape(NODES, D), grad_w_in, grad_w_out, grad_rel, grad_msg, grad_self)
```

```python
import jax
import jax.numpy as jnp
from jax import lax
from jax.sharding import Mesh
from jax.sharding import PartitionSpec as P

BF = jnp.bfloat16
F32 = jnp.float32
I32 = jnp.int32
GROUP = ("x", "y")
SHIFTS = (1, 3, 2)


def shift_by(value, axis, shift):
    count = lax.axis_size(axis)
    return lax.ppermute(value, axis, [(i, (i + shift) % count) for i in range(count)])


def dot(a, b):
    return jnp.dot(a, b, preferred_element_type=F32)


def dot_t(a, b):
    return lax.dot_general(a, b, (((0,), (0,)), ((), ())), preferred_element_type=F32)


def dot_bt(a, b):
    return lax.dot_general(a, b, (((1,), (1,)), ((), ())), preferred_element_type=F32)


def one_hot(index, count):
    return (index[:, None] == jnp.arange(count, dtype=I32)[None, :]).astype(BF)


def layer_norm(hidden):
    values = hidden.astype(F32)
    center = values - jnp.mean(values, axis=-1, keepdims=True)
    spread = jnp.mean(center * center, axis=-1, keepdims=True)
    return (center * lax.rsqrt(spread + 1e-05)).astype(BF)


def row_of(values, width):
    return jnp.pad(values.astype(BF), (0, width - values.shape[0]))[None, :]


def pick(stack, index):
    return lax.dynamic_index_in_dim(stack, index, 0, keepdims=False)


def scatter_four(chunks, axis):
    me = lax.axis_index(axis)
    total = pick(chunks, me).astype(F32)
    for shift in SHIFTS:
        total = total + shift_by(pick(chunks, (me + shift) % 4), axis, shift).astype(F32)
    return total


def fresh_row(side, place):
    return (place % 4) * 16 + (side + 1) * 4 + place // 4


def shards(
    hidden,
    desc_len,
    w_in,
    w_out,
    send_order,
    place_order,
    cache,
    halo_rows,
    edge_src,
    edge_dst,
    edge_rel,
    rel_table,
    w_msg,
    w_self,
    d_out,
):
    entities, length, width = hidden.shape
    tokens = entities * length
    units = w_in.shape[1]
    my_z, my_core = lax.axis_index("z"), lax.axis_index("core")
    my_x = lax.axis_index("x")

    full_table = lax.all_gather(rel_table, GROUP, axis=0, tiled=True)

    normed = layer_norm(hidden).reshape(tokens, width)
    extra = row_of(jnp.concatenate([desc_len, send_order[0]]), width)
    block = jnp.concatenate([normed, jnp.pad(extra, ((0, 15), (0, 0)))], axis=0)
    blocks = [block] + [shift_by(block, "x", s) for s in SHIFTS]

    half_k, half_u = width // 2, units // 2
    in_half = lax.dynamic_slice_in_dim(w_in, my_core * half_k, half_k, 0)
    in_wide = jnp.concatenate([in_half[i * half_u : (i + 1) * half_u] for i in range(4)], axis=1)
    out_half = lax.dynamic_slice_in_dim(w_out, my_core * half_u, half_u, 0)
    weights = jnp.concatenate([in_wide, out_half], axis=0)
    mine = jnp.stack([shift_by(weights, "y", s) for s in SHIFTS])
    other = shift_by(mine, "core", 1)
    low = jnp.where(my_core == 0, mine, other)
    high = jnp.where(my_core == 0, other, mine)

    def in_block(half):
        return jnp.concatenate([half[:half_u, i * units : (i + 1) * units] for i in range(4)], axis=0)

    all_in = jnp.concatenate(
        [w_in] + [jnp.concatenate([in_block(low[t]), in_block(high[t])], axis=0) for t in range(3)], axis=1
    )
    all_out = jnp.concatenate(
        [w_out] + [part for t in range(3) for part in (low[t, half_u:], high[t, half_u:])], axis=0
    )

    halo = halo_rows[0]
    place = place_order[0]
    side = halo.shape[0] // 2
    cache_count = cache.shape[0]
    boundary = dot(one_hot(halo - entities, cache_count), cache).astype(BF)
    halo_hot = halo[:, None] == jnp.arange(entities, dtype=I32)[None, :]
    halo_place = jnp.where(halo < entities, jnp.sum(jnp.where(halo_hot, place[None, :], 0), axis=1), 16)

    def edge_of(rows, places):
        return jnp.concatenate([rows, jnp.pad(row_of(places, width), ((0, 15), (0, 0)))], axis=0)

    from_low = shift_by(edge_of(boundary[side:], halo_place[side:]), GROUP, 1)
    from_high = shift_by(edge_of(boundary[:side], halo_place[:side]), GROUP, 15)
    low_place = from_low[side, :side].astype(I32)
    high_place = from_high[side, :side].astype(I32)
    own_row = fresh_row(0, place)
    low_row = jnp.where(low_place < 16, fresh_row(-1, low_place), -1)
    high_row = jnp.where(high_place < 16, fresh_row(1, high_place), -1)
    own_hot = one_hot(own_row, 64)
    low_hot = one_hot(low_row, 64)
    high_hot = one_hot(high_row, 64)
    row_hot = jnp.concatenate([own_hot, jnp.zeros((cache_count, 64), BF), low_hot, high_hot], axis=0)
    src = edge_src[0]
    dst = edge_dst[0]
    rel = edge_rel[0]
    node_count = entities + cache_count
    extended_count = node_count + 2 * side
    edge_count = src.shape[0]
    block_count = rel.shape[0]
    block_size = edge_count // block_count
    scale_factor = (node_count / edge_count) ** 0.5
    src_hot = one_hot(src, extended_count)
    dst_hot = one_hot(dst, node_count)
    src_row_hot = dot(src_hot, row_hot).astype(BF)

    all_normed = jnp.concatenate([b[:tokens] for b in blocks], axis=0)
    lens = jnp.concatenate([b[tokens, :entities] for b in blocks]).astype(F32)
    sends = jnp.stack([b[tokens, entities : 2 * entities] for b in blocks]).astype(F32)
    group_rows = lens.shape[0]
    mask = (jnp.arange(length, dtype=F32)[None, :] < lens[:, None]).astype(F32)
    inv_len = 1.0 / lens
    pre_act = dot(all_normed, all_in)
    all_units = pre_act.shape[1]
    activation = jax.nn.gelu(pre_act).astype(BF)
    pooled_act = jnp.einsum(
        "etf,et->ef",
        activation.reshape(group_rows, length, all_units),
        mask.astype(BF),
        preferred_element_type=F32,
    ).astype(BF)
    partial_out = dot(pooled_act, all_out)
    own_mask = (jnp.arange(length, dtype=I32)[None, :] < desc_len[:, None]).astype(BF)
    hidden_sum = jnp.einsum("etd,et->ed", hidden, own_mask, preferred_element_type=F32)
    partial_out = jnp.concatenate([partial_out[:entities] + hidden_sum, partial_out[entities:]], axis=0)
    partial_rows = (partial_out * inv_len[:, None]).astype(BF)

    line = jnp.arange(256, dtype=I32)
    slot = line % 16
    bound = (line // 16 + slot // 4 + 15) % 16
    column = jnp.arange(group_rows, dtype=I32)
    column_x = (my_x + jnp.array([0, 3, 1, 2], I32)[column // 16]) % 4
    sent_index = dot(one_hot(bound, 16), jnp.repeat(sends.T, entities, axis=1).astype(BF)).astype(I32)
    route = (
        (sent_index == (column % 16)[None, :])
        & ((slot % 4)[:, None] == column_x[None, :])
        & (slot < 12)[:, None]
    ).astype(BF)
    shard_rows = rel_table.shape[0]
    rel_row = row_of(jnp.concatenate([rel // shard_rows, rel % shard_rows]), width)
    outgoing = dot(route, partial_rows).astype(BF).reshape(16, 16, width)
    outgoing = jnp.where((jnp.arange(16) == 12)[None, :, None], rel_row[None], outgoing)
    arrived = lax.all_to_all(outgoing, GROUP, 0, 0, tiled=True)
    group_rel = arrived[:, 12, : 2 * block_count].astype(I32)
    table = jnp.sum(arrived.reshape(4, 64, width).astype(F32), axis=0).astype(BF)

    fresh = dot(own_hot, table).astype(BF)
    nodes = jnp.concatenate([fresh, cache], axis=0)
    low_halo = from_low[:side] + dot(low_hot, table).astype(BF)
    high_halo = from_high[:side] + dot(high_hot, table).astype(BF)
    extended = jnp.concatenate([nodes, low_halo, high_halo], axis=0)
    rel_rows = dot(one_hot(rel, full_table.shape[0]), full_table)
    rel_edges = rel_rows[:, None, :]
    sources = dot(src_hot, extended).astype(BF).astype(F32).reshape(block_count, block_size, width)
    messages = (sources * rel_edges).astype(BF).reshape(edge_count, width)
    aggregate = (scale_factor * dot_t(dst_hot, messages)).astype(BF)
    out_pre = dot(aggregate, w_msg) + dot(nodes, w_self)
    squashed = jnp.tanh(out_pre)
    graph_out = squashed.astype(BF)
    grad_pre = (d_out.astype(F32) * (1.0 - squashed * squashed)).astype(BF)
    grad_agg = (scale_factor * dot_bt(grad_pre, w_msg)).astype(BF)
    at_dest = dot(dst_hot, grad_agg).astype(BF).astype(F32).reshape(block_count, block_size, width)
    grad_src = (at_dest * rel_edges).astype(BF).reshape(edge_count, width)
    grad_blocks = jnp.sum(at_dest * sources, axis=1).astype(BF)
    own_pre = dot_t(own_hot, grad_pre[:entities]).astype(BF)
    grad_table = dot_t(src_row_hot, grad_src) + dot_bt(own_pre, w_self)

    back = jnp.broadcast_to(grad_table.astype(BF).reshape(1, 4, 16, width), (4, 4, 16, width))
    returned = lax.all_to_all(back.reshape(16, 16, width), GROUP, 0, 0, tiled=True).reshape(256, width)
    scaled = (dot_t(route, returned) * inv_len[:, None]).astype(BF)

    blocks_out = jnp.broadcast_to(grad_blocks[None], (16, block_count, width))
    group_blocks = lax.all_to_all(blocks_out, GROUP, 0, 0, tiled=True).reshape(16 * block_count, width)
    my_b = lax.axis_index(GROUP)
    rel_owner = group_rel[:, :block_count].reshape(-1)
    rel_index = group_rel[:, block_count:].reshape(-1)
    rel_hot = one_hot(jnp.where(rel_owner == my_b, rel_index, -1), 64)
    rel_shard = dot_t(rel_hot, group_blocks).astype(BF)

    graph_grads = jnp.stack([dot_t(aggregate, grad_pre).astype(BF), dot_t(nodes, grad_pre).astype(BF)])
    graph_grads = graph_grads.reshape(2, 4, 2, 128, width)
    kept = lax.dynamic_index_in_dim(graph_grads, my_core, 2, keepdims=False)
    given = lax.dynamic_index_in_dim(graph_grads, 1 - my_core, 2, keepdims=False)
    chip = (kept.astype(F32) + shift_by(given, "core", 1).astype(F32)).astype(BF)
    line_sum = scatter_four(chip.transpose(1, 0, 2, 3), "z").astype(BF)
    plane = line_sum.reshape(2, 16, 8, width).transpose(1, 0, 2, 3).reshape(16, 16, width)
    plane = lax.all_to_all(plane, GROUP, 0, 0, tiled=True)
    weight_rows = jnp.sum(plane.astype(F32), axis=0)
    grad_msg, grad_self = weight_rows[:8], weight_rows[8:]

    upstream = dot_bt(scaled, all_out)
    grad_act = mask[:, :, None] * upstream[:, None, :]
    grad_pre_act = jax.vjp(jax.nn.gelu, pre_act)[1](grad_act.reshape(group_rows * length, all_units))[0].astype(BF)
    grad_out = dot_t(pooled_act, scaled).astype(BF).reshape(4, 2, half_u, width)
    grad_in = dot_t(all_normed, grad_pre_act).astype(BF)
    grad_in = grad_in.reshape(2, half_k, 4, units).transpose(2, 0, 1, 3)

    def over_core_and_y(grads):
        kept = lax.dynamic_index_in_dim(grads, my_core, 1, keepdims=False)
        given = lax.dynamic_index_in_dim(grads, 1 - my_core, 1, keepdims=False)
        chip = (kept.astype(F32) + shift_by(given, "core", 1).astype(F32)).astype(BF)
        total = chip[0].astype(F32)
        for t, shift in enumerate(SHIFTS):
            total = total + shift_by(chip[t + 1], "y", (4 - shift) % 4).astype(F32)
        return total.astype(BF)

    sum_out = over_core_and_y(grad_out)
    sum_in = over_core_and_y(grad_in)
    rel_halves = rel_shard.reshape(2, 32, width)
    rel_kept = pick(rel_halves, my_core).astype(F32)
    rel_given = shift_by(pick(rel_halves, 1 - my_core), "core", 1).astype(F32)
    sum_rel = (rel_kept + rel_given).astype(BF)
    in_wide = jnp.concatenate([sum_in[i * half_u : (i + 1) * half_u] for i in range(4)], axis=1)
    columns = jnp.concatenate(
        [in_wide.reshape(4, 32, width), sum_out.reshape(4, 32, width), sum_rel.reshape(4, 8, width)], axis=1
    )
    part = scatter_four(columns, "z").astype(BF)
    parts = jnp.zeros_like(columns)
    parts = lax.dynamic_update_index_in_dim(parts, part, my_z, 0)
    for shift in SHIFTS:
        parts = lax.dynamic_update_index_in_dim(parts, shift_by(part, "z", shift), (my_z + 4 - shift) % 4, 0)
    others = shift_by(parts, "core", 1)
    first = jnp.where(my_core == 0, parts, others)
    second = jnp.where(my_core == 0, others, parts)

    def in_rows(half):
        wide = half[:, :32].reshape(128, width)
        return jnp.concatenate([wide[:, i * units : (i + 1) * units] for i in range(4)], axis=0)

    grad_w_in = jnp.concatenate([in_rows(first), in_rows(second)], axis=0).astype(F32)
    grad_w_out = jnp.concatenate(
        [first[:, 32:64].reshape(128, width), second[:, 32:64].reshape(128, width)], axis=0
    ).astype(F32)
    grad_rel = jnp.concatenate([first[:, 64:].reshape(32, width), second[:, 64:].reshape(32, width)], axis=0)
    grad_rel = grad_rel[:shard_rows].astype(F32)
    return (graph_out, grad_w_in, grad_w_out, grad_rel, grad_msg, grad_self)


def solution(mesh):
    fine = Mesh(mesh.devices.reshape(4, 2, 4, 4), ("z", "core", "x", "y"))
    every = ("z", "core", "x", "y")
    placed = (
        P(every, None, None),
        P(every),
        P(None, GROUP),
        P(GROUP, None),
        P(every, None),
        P(every, None),
        P(every, None),
        P(every, None),
        P(every, None),
        P(every, None),
        P(every, None),
        P(GROUP, None),
        P(),
        P(),
        P(every, None),
    )
    return jax.shard_map(
        shards,
        mesh=fine,
        in_specs=placed,
        out_specs=(
            P(every, None),
            P(None, GROUP),
            P(GROUP, None),
            P(GROUP, None),
            P(every, None),
            P(every, None),
        ),
        check_vma=False,
    )
```

```python
import jax
import jax.numpy as jnp
import numpy as np
from jax import lax
from jax.experimental import pallas as pl
from jax.experimental.pallas import tpu as pltpu
from jax.sharding import Mesh
from jax.sharding import PartitionSpec as P

BF = jnp.bfloat16
F32 = jnp.float32
I32 = jnp.int32
GROUP = ("x", "y")
SHIFTS = (1, 3, 2)
ORIGINS = (0, 3, 1, 2)
GELU_SCALE = float(np.sqrt(2.0 / np.pi))
GELU_CUBE = 0.044715


def shift_by(value, axis, shift):
    count = lax.axis_size(axis)
    return lax.ppermute(value, axis, [(i, (i + shift) % count) for i in range(count)])


def dot(a, b):
    return jnp.dot(a, b, preferred_element_type=F32)


def dot_t(a, b):
    return lax.dot_general(a, b, (((0,), (0,)), ((), ())), preferred_element_type=F32)


def dot_bt(a, b):
    return lax.dot_general(a, b, (((1,), (1,)), ((), ())), preferred_element_type=F32)


def one_hot(index, count):
    return (index[:, None] == jnp.arange(count, dtype=I32)[None, :]).astype(BF)


def one_hot_t(index, count):
    return (index[None, :] == jnp.arange(count, dtype=I32)[:, None]).astype(BF)


def lanes(shape):
    return lax.broadcasted_iota(I32, shape, 1)


def sublanes(shape):
    return lax.broadcasted_iota(I32, shape, 0)


def row_of(values, width):
    return jnp.pad(values.astype(BF), (0, width - values.shape[0]))[None, :]


def fresh_row(side, place):
    return (place % 4) * 16 + (side + 1) * 4 + place // 4


def local_call(body, outs, operands, scratch=(), flops=0, limit=48):
    return pl.pallas_call(
        body,
        out_shape=[jax.ShapeDtypeStruct(shape, kind) for shape, kind in outs],
        in_specs=[pl.BlockSpec(memory_space=pltpu.SMEM)]
        + [pl.BlockSpec(memory_space=pltpu.VMEM)] * (len(operands) - 1),
        out_specs=[pl.BlockSpec(memory_space=pltpu.VMEM)] * len(outs),
        scratch_shapes=list(scratch),
        compiler_params=pltpu.CompilerParams(vmem_limit_bytes=limit * 1024 * 1024),
        cost_estimate=pl.CostEstimate(flops=flops, bytes_accessed=1024 * 1024, transcendentals=0),
    )(*operands)


def length_column(meta):
    shape = meta.shape
    return jnp.sum(jnp.where(lanes(shape) == sublanes(shape), meta, 0.0), axis=1, keepdims=True)


def pool_rows(length, tokens):
    shape = (16, tokens)
    line = lanes(shape)
    inside = (line // 16 == sublanes(shape)) & ((line % 16).astype(F32) < length)
    return inside.astype(F32).astype(BF)


def norm_kernel(where_ref, hidden_ref, meta_ref, block_ref, sum_ref):
    values = hidden_ref[...].astype(F32)
    center = values - jnp.mean(values, axis=-1, keepdims=True)
    spread = jnp.mean(center * center, axis=-1, keepdims=True)
    tokens = values.shape[0]
    block_ref[0:tokens, :] = (center * lax.rsqrt(spread + 1e-05)).astype(BF)
    block_ref[tokens : tokens + 16, :] = meta_ref[...]
    pool = pool_rows(length_column(meta_ref[:, 0:128].astype(F32)), tokens)
    sum_ref[...] = dot(pool, hidden_ref[...])


def encode_kernel(
    where_ref,
    b0, b1, b2, b3,
    own_in, own_out,
    m1, m2, m3,
    o1, o2, o3,
    hidden_sum_ref,
    outgoing_ref, normed_ref, slope_ref, pooled_ref, all_out_ref, route_ref, length_ref, rel_hot_ref,
    in_ref, pool_ref,
):
    core, my_x = where_ref[1], where_ref[2]
    for s, block in enumerate((b0, b1, b2, b3)):
        normed_ref[s * 256 : (s + 1) * 256, :] = block[0:256, :]
    in_ref[:, 0:256] = own_in[...]
    all_out_ref[0:256, :] = own_out[...]
    for t, (mine, other) in enumerate(((m1, o1), (m2, o2), (m3, o3)), 1):
        for part, half in ((mine, core), (other, 1 - core)):
            for i in range(2):
                rows = pl.ds(pl.multiple_of(half * 512 + i * 256, 256), 256)
                in_ref[rows, t * 256 : (t + 1) * 256] = part[0:256, i * 256 : (i + 1) * 256]
                rows = pl.ds(pl.multiple_of(t * 256 + half * 128, 128), 128)
                all_out_ref[rows, i * 512 : (i + 1) * 512] = part[256 + i * 128 : 384 + i * 128, :]

    wide = (16, 256)
    slot = lanes(wide) % 16
    bound = lanes((128, 256))
    bound = (bound // 16 + (bound % 16) // 4 + 15) % 16
    bound_hot = (sublanes((128, 256)) == bound + 16).astype(F32).astype(BF)
    ids = jnp.zeros((16, 64), F32)
    for s, block in enumerate((b0, b1, b2, b3)):
        meta = block[256:272, 0:128]
        length = length_column(meta.astype(F32))
        length_ref[s * 16 : (s + 1) * 16, :] = jnp.broadcast_to(1.0 / length, (16, 128))
        pool_ref[s * 16 : (s + 1) * 16, :] = pool_rows(length, 256)
        sent = dot(meta, bound_hot)
        encoder = lax.rem(my_x + ORIGINS[s], 4)
        chosen = (sent == sublanes(wide).astype(F32)) & (slot % 4 == encoder) & (slot < 12)
        route_ref[s * 16 : (s + 1) * 16, :] = chosen.astype(F32).astype(BF)
        at, to = sublanes((128, 64)), lanes((128, 64)) - s * 16
        inside = (to >= 0) & (to < 16)
        select = jnp.where(inside & (at == 32 + to), 32.0, jnp.where(inside & (at == 48 + to), 1.0, 0.0))
        ids = ids + dot(meta, select.astype(BF))
    line = sublanes((512, 64))
    local = (line // 64) % 2 * 32 + (line // 16) % 4 * 8 + line % 16
    name = (my_x * 4 + line // 128) * 52 + local
    good = (line % 16 < 8) & (local < 52)
    rel_hot_ref[...] = ((name.astype(F32) == ids[0:1, :]) & good).astype(F32).astype(BF)

    @pl.loop(0, 16)
    def _(step):
        s, t = step // 4, step % 4
        rows = pl.ds(pl.multiple_of(s * 256, 256), 256)
        cols = pl.ds(pl.multiple_of(t * 256, 256), 256)
        few = pl.ds(pl.multiple_of(s * 16, 16), 16)
        pre = dot(normed_ref[rows, :], in_ref[:, cols])
        square = pre * pre
        tanh = jnp.tanh(GELU_SCALE * pre * (1.0 + GELU_CUBE * square))
        upper = 0.5 + 0.5 * tanh
        slope = upper + (0.5 * GELU_SCALE) * pre * (1.0 - tanh * tanh) * (1.0 + 3.0 * GELU_CUBE * square)
        slope_ref[rows, cols] = slope.astype(BF)
        pooled_ref[few, cols] = dot(pool_ref[few, :], (pre * upper).astype(BF)).astype(BF)

    partial = dot(pooled_ref[...], all_out_ref[...])
    partial = jnp.concatenate([partial[0:16] + hidden_sum_ref[...], partial[16:64]], axis=0)
    partial = (partial * length_ref[:, 0:1]).astype(BF)
    outgoing_ref[...] = dot_t(route_ref[...], partial).astype(BF)


def graph_kernel(
    where_ref,
    arrived_ref, base_ref, row_hot_ref, own_hot_t_ref, rel_ref,
    src_hot_ref, dst_hot_ref, dst_hot_t_ref, src_row_hot_ref,
    w_msg_ref, w_self_ref, d_out_ref,
    table_out_ref, blocks_ref, graph_out_ref, aggregate_ref, nodes_ref, pre_ref,
    ext_ref, sources_ref, edges_ref, agg_grad_ref, sums_ref,
):
    scale = (256 / 2048) ** 0.5
    total = arrived_ref[0:64, :].astype(F32)
    for i in range(1, 4):
        total = total + arrived_ref[i * 64 : (i + 1) * 64, :].astype(F32)
    table = total.astype(BF)
    ext_ref[...] = (base_ref[...].astype(F32) + dot(row_hot_ref[...], table)).astype(BF)
    nodes_ref[...] = ext_ref[0:256, :]

    @pl.loop(0, 16)
    def _(j):
        rows = pl.ds(pl.multiple_of(j * 128, 128), 128)
        taken = dot(src_hot_ref[rows, :], ext_ref[...])
        sources_ref[rows, :] = taken.astype(BF)
        edges_ref[rows, :] = (taken * rel_ref[j]).astype(BF)

    @pl.loop(0, 4)
    def _(n):
        cols = pl.ds(pl.multiple_of(n * 256, 256), 256)
        aggregate_ref[:, cols] = (scale * dot(dst_hot_t_ref[...], edges_ref[:, cols])).astype(BF)

    @pl.loop(0, 4)
    def _(n):
        cols = pl.ds(pl.multiple_of(n * 256, 256), 256)
        out_pre = dot(aggregate_ref[...], w_msg_ref[:, cols]) + dot(nodes_ref[...], w_self_ref[:, cols])
        squashed = jnp.tanh(out_pre)
        graph_out_ref[:, cols] = squashed.astype(BF)
        pre_ref[:, cols] = (d_out_ref[:, cols].astype(F32) * (1.0 - squashed * squashed)).astype(BF)

    @pl.loop(0, 4)
    def _(n):
        cols = pl.ds(pl.multiple_of(n * 256, 256), 256)
        agg_grad_ref[:, cols] = (scale * dot_bt(pre_ref[...], w_msg_ref[cols, :])).astype(BF)

    @pl.loop(0, 16)
    def _(j):
        rows = pl.ds(pl.multiple_of(j * 128, 128), 128)
        at_dest = dot(dst_hot_ref[rows, :], agg_grad_ref[...])
        edges_ref[rows, :] = (at_dest * rel_ref[j]).astype(BF)
        sums_ref[j] = jnp.sum(at_dest * sources_ref[rows, :].astype(F32), axis=0, keepdims=True)

    blocks_ref[...] = jnp.concatenate([sums_ref[j] for j in range(16)], axis=0).astype(BF)
    own_pre = dot(own_hot_t_ref[...], pre_ref[0:16, :]).astype(BF)

    @pl.loop(0, 4)
    def _(n):
        cols = pl.ds(pl.multiple_of(n * 256, 256), 256)
        grad = dot(src_row_hot_ref[...], edges_ref[:, cols]) + dot_bt(own_pre, w_self_ref[cols, :])
        table_out_ref[:, cols] = grad.astype(BF)


def back_kernel(
    where_ref,
    returned_ref, route_ref, length_ref, all_out_ref, slope_ref, pooled_ref, normed_t_ref,
    rel_hot_ref, r0, r1, r2, r3,
    kept_ref, given_ref,
    scaled_ref, grad_ref,
):
    core, my_y = where_ref[1], where_ref[3]
    scaled_ref[...] = (dot(route_ref[...], returned_ref[...]) * length_ref[:, 0:1]).astype(BF)
    blocks = jnp.concatenate([r0[...], r1[...], r2[...], r3[...]], axis=0)
    for half, chunk_ref in ((core, kept_ref), (1 - core, given_ref)):
        for y in range(4):
            rows = pl.ds(pl.multiple_of(y * 128 + half * 64, 64), 64)
            rel = dot(rel_hot_ref[rows, :], blocks).astype(BF)
            for z in range(4):
                chunk_ref[z, y, 64:80, :] = rel[z * 16 : (z + 1) * 16]

    @pl.loop(0, 4)
    def _(t):
        cols = pl.ds(pl.multiple_of(t * 256, 256), 256)
        origin = jnp.where(t == 0, 0, jnp.where(t == 1, 3, t - 1))
        owner = lax.rem(my_y + origin, 4)
        upstream = dot_bt(scaled_ref[...], all_out_ref[cols, :]).astype(BF)
        for s in range(4):
            rows = slice(s * 256, (s + 1) * 256)
            shape = (16, 256)
            line = lanes(shape)
            length = 1.0 / length_ref[s * 16 : (s + 1) * 16, 0:1]
            inside = (line // 16 == sublanes(shape)) & ((line % 16).astype(F32) + 0.5 < length)
            pool = inside.astype(F32).astype(BF)
            at_tokens = dot_t(pool, upstream[s * 16 : (s + 1) * 16])
            grad_ref[rows, :] = (slope_ref[rows, cols].astype(F32) * at_tokens).astype(BF)
        for half, chunk_ref in ((1 - core, given_ref), (core, kept_ref)):
            units = pl.ds(pl.multiple_of(t * 256 + half * 128, 128), 128)
            out = dot_t(pooled_ref[:, units], scaled_ref[...]).astype(BF)
            inner = dot(normed_t_ref[pl.ds(pl.multiple_of(half * 512, 512), 512), :], grad_ref[...]).astype(BF)
            for z in range(4):
                chunk_ref[z, owner, 32:64, :] = out[z * 32 : (z + 1) * 32]
                for i in range(4):
                    piece = inner[z * 128 + i * 32 : z * 128 + (i + 1) * 32]
                    chunk_ref[z, owner, 0:32, i * 256 : (i + 1) * 256] = piece


def place_kernel(where_ref, a0, a1, a2, a3, c0, c1, c2, c3, in_ref, out_ref, rel_ref):
    my_z, core = where_ref[0], where_ref[1]
    for pieces, half in (((a0, a1, a2, a3), core), ((c0, c1, c2, c3), 1 - core)):
        for piece, origin in zip(pieces, ORIGINS):
            z = lax.rem(my_z + origin, 4)
            values = piece[...].astype(F32)
            for i in range(4):
                rows = pl.ds(pl.multiple_of(half * 512 + z * 128 + i * 32, 32), 32)
                in_ref[rows, :] = values[0:32, i * 256 : (i + 1) * 256]
            out_ref[pl.ds(pl.multiple_of(half * 128 + z * 32, 32), 32), :] = values[32:64]
            rel_ref[pl.ds(pl.multiple_of(half * 32 + z * 8, 8), 8), :] = values[64:72]


def scatter_four(chunks, axis):
    me = lax.axis_index(axis)
    total = lax.dynamic_index_in_dim(chunks, me, 0, keepdims=False).astype(F32)
    for shift in SHIFTS:
        chunk = lax.dynamic_index_in_dim(chunks, (me + shift) % 4, 0, keepdims=False)
        total = total + shift_by(chunk, axis, shift).astype(F32)
    return total


def shards(
    hidden,
    desc_len,
    w_in,
    w_out,
    send_order,
    place_order,
    cache,
    halo_rows,
    edge_src,
    edge_dst,
    edge_rel,
    rel_table,
    w_msg,
    w_self,
    d_out,
):
    entities, length, width = hidden.shape
    tokens = entities * length
    units = w_in.shape[1]
    my_core = lax.axis_index("core")
    where = jnp.stack([lax.axis_index(name) for name in ("z", "core", "x", "y")]).astype(I32)
    src, dst, rel = edge_src[0], edge_dst[0], edge_rel[0]
    shard_rows = rel_table.shape[0]

    full_table = lax.all_gather(rel_table, GROUP, axis=0, tiled=True)

    meta = row_of(jnp.concatenate([desc_len, send_order[0], rel // 32, rel % 32]), width)
    block, hidden_sum = local_call(
        norm_kernel,
        [((tokens + 16, width), BF), ((entities, width), F32)],
        [where, hidden.reshape(tokens, width), jnp.broadcast_to(meta, (16, width))],
    )
    blocks = [block] + [shift_by(block, "x", s) for s in SHIFTS]

    half_k, half_u = width // 2, units // 2
    in_half = lax.dynamic_slice_in_dim(w_in, my_core * half_k, half_k, 0)
    out_half = lax.dynamic_slice_in_dim(w_out, my_core * half_u, half_u, 0)
    weights = jnp.concatenate(
        [
            jnp.concatenate([in_half[:units], in_half[units:]], axis=1),
            out_half[:, : 2 * units],
            out_half[:, 2 * units :],
        ],
        axis=0,
    )
    mine = [shift_by(weights, "y", s) for s in SHIFTS]
    other = [shift_by(part, "core", 1) for part in mine]

    halo = halo_rows[0]
    place = place_order[0]
    side = halo.shape[0] // 2
    cache_count = cache.shape[0]
    boundary = dot(one_hot(halo - entities, cache_count), cache).astype(BF)
    halo_hot = halo[:, None] == jnp.arange(entities, dtype=I32)[None, :]
    halo_place = jnp.where(halo < entities, jnp.sum(jnp.where(halo_hot, place[None, :], 0), axis=1), 16)

    def edge_of(rows, places):
        return jnp.concatenate([rows, jnp.pad(row_of(places, width), ((0, 15), (0, 0)))], axis=0)

    from_low = shift_by(edge_of(boundary[side:], halo_place[side:]), GROUP, 1)
    from_high = shift_by(edge_of(boundary[:side], halo_place[:side]), GROUP, 15)
    low_place = from_low[side, :side].astype(I32)
    high_place = from_high[side, :side].astype(I32)
    own_row = fresh_row(0, place)
    low_row = jnp.where(low_place < 16, fresh_row(-1, low_place), -1)
    high_row = jnp.where(high_place < 16, fresh_row(1, high_place), -1)
    table_row = jnp.concatenate([own_row, jnp.full((cache_count,), -1, I32), low_row, high_row])
    row_hot = one_hot(table_row, 64)
    base = jnp.concatenate([jnp.zeros((entities, width), BF), cache, from_low[:side], from_high[:side]], axis=0)
    node_count = entities + cache_count
    extended_count = node_count + 2 * side
    edge_count = src.shape[0]
    block_count = rel.shape[0]
    src_hot = one_hot(src, extended_count)
    src_row_hot = dot_bt(one_hot_t(table_row, 64), src_hot).astype(BF)
    rel_rows = dot(one_hot(rel, full_table.shape[0]), full_table).reshape(block_count, 1, width)

    outgoing, normed, slope, pooled, all_out, route, inverse, rel_hot = local_call(
        encode_kernel,
        [
            ((256, width), BF),
            ((4 * tokens, width), BF),
            ((4 * tokens, 4 * units), BF),
            ((4 * entities, 4 * units), BF),
            ((4 * units, width), BF),
            ((4 * entities, 256), BF),
            ((4 * entities, 128), F32),
            ((512, 64), BF),
        ],
        [where, *blocks, w_in, w_out, *mine, *other, hidden_sum],
        [pltpu.VMEM((width, 4 * units), BF), pltpu.VMEM((4 * entities, tokens), BF)],
        flops=2 * 4 * tokens * width * 4 * units,
    )
    arrived = lax.all_to_all(outgoing.reshape(16, 16, width), GROUP, 0, 0, tiled=True).reshape(256, width)
    normed_t = normed.T

    grad_table, grad_blocks, graph_out, aggregate, nodes, grad_pre = local_call(
        graph_kernel,
        [
            ((64, width), BF),
            ((block_count, width), BF),
            ((node_count, width), BF),
            ((node_count, width), BF),
            ((node_count, width), BF),
            ((node_count, width), BF),
        ],
        [
            where,
            arrived,
            base,
            row_hot,
            one_hot_t(own_row, 64),
            rel_rows,
            src_hot,
            one_hot(dst, node_count),
            one_hot_t(dst, node_count),
            src_row_hot,
            w_msg,
            w_self,
            d_out,
        ],
        [
            pltpu.VMEM((extended_count, width), BF),
            pltpu.VMEM((edge_count, width), BF),
            pltpu.VMEM((edge_count, width), BF),
            pltpu.VMEM((node_count, width), BF),
            pltpu.VMEM((block_count, 1, width), F32),
        ],
        flops=6 * 10**9,
    )

    back = jnp.broadcast_to(grad_table.reshape(1, 4, 16, width), (4, 4, 16, width))
    returned = lax.all_to_all(back.reshape(16, 16, width), GROUP, 0, 0, tiled=True).reshape(256, width)
    rel_blocks = [grad_blocks] + [shift_by(grad_blocks, "x", s) for s in SHIFTS]

    graph_grads = jnp.stack([dot_t(aggregate, grad_pre).astype(BF), dot_t(nodes, grad_pre).astype(BF)])
    graph_grads = graph_grads.reshape(2, 4, 2, 128, width)
    graph_kept = lax.dynamic_index_in_dim(graph_grads, my_core, 2, keepdims=False)
    graph_given = lax.dynamic_index_in_dim(graph_grads, 1 - my_core, 2, keepdims=False)
    chip = (graph_kept.astype(F32) + shift_by(graph_given, "core", 1).astype(F32)).astype(BF)
    line_sum = scatter_four(chip.transpose(1, 0, 2, 3), "z").astype(BF)
    plane = line_sum.reshape(2, 16, 8, width).transpose(1, 0, 2, 3).reshape(16, 16, width)
    plane = lax.all_to_all(plane, GROUP, 0, 0, tiled=True)
    weight_rows = jnp.sum(plane.astype(F32), axis=0)
    grad_msg, grad_self = weight_rows[:8], weight_rows[8:]

    kept, given = local_call(
        back_kernel,
        [((4, 4, 80, width), BF), ((4, 4, 80, width), BF)],
        [where, returned, route, inverse, all_out, slope, pooled, normed_t, rel_hot, *rel_blocks],
        [pltpu.VMEM((4 * entities, width), BF), pltpu.VMEM((4 * tokens, units), BF)],
        flops=2 * 4 * tokens * width * 4 * units,
    )
    chunks = (kept.astype(F32) + shift_by(given, "core", 1).astype(F32)).astype(BF)
    chunks = lax.all_to_all(chunks.reshape(16, 80, width), ("z", "y"), 0, 0, tiled=True)
    part = jnp.sum(chunks.astype(F32), axis=0).astype(BF)
    parts = [part] + [shift_by(part, "z", s) for s in SHIFTS]
    others = [shift_by(piece, "core", 1) for piece in parts]
    grad_w_in, grad_w_out, grad_rel = local_call(
        place_kernel,
        [((width, units), F32), ((units, width), F32), ((64, width), F32)],
        [where, *parts, *others],
    )
    return (graph_out, grad_w_in, grad_w_out, grad_rel[:shard_rows], grad_msg, grad_self)


def solution(mesh):
    fine = Mesh(mesh.devices.reshape(4, 2, 4, 4), ("z", "core", "x", "y"))
    every = ("z", "core", "x", "y")
    placed = (
        P(every, None, None),
        P(every),
        P(None, GROUP),
        P(GROUP, None),
        P(every, None),
        P(every, None),
        P(every, None),
        P(every, None),
        P(every, None),
        P(every, None),
        P(every, None),
        P(GROUP, None),
        P(),
        P(),
        P(every, None),
    )
    return jax.shard_map(
        shards,
        mesh=fine,
        in_specs=placed,
        out_specs=(
            P(every, None),
            P(None, GROUP),
            P(GROUP, None),
            P(GROUP, None),
            P(every, None),
            P(every, None),
        ),
        check_vma=False,
    )
```

```python
import jax
import jax.numpy as jnp
import numpy as np
from jax import lax
from jax.experimental import pallas as pl
from jax.experimental.pallas import tpu as pltpu
from jax.sharding import Mesh
from jax.sharding import PartitionSpec as P

BF = jnp.bfloat16
F32 = jnp.float32
I32 = jnp.int32
GROUP = ("x", "y")
SHIFTS = (1, 3, 2)
ORIGINS = (0, 3, 1, 2)
GELU_SCALE = float(np.sqrt(2.0 / np.pi))
GELU_CUBE = 0.044715


def shift_by(value, axis, shift):
    count = lax.axis_size(axis)
    return lax.ppermute(value, axis, [(i, (i + shift) % count) for i in range(count)])


def dot(a, b):
    return jnp.dot(a, b, preferred_element_type=F32)


def dot_t(a, b):
    return lax.dot_general(a, b, (((0,), (0,)), ((), ())), preferred_element_type=F32)


def dot_bt(a, b):
    return lax.dot_general(a, b, (((1,), (1,)), ((), ())), preferred_element_type=F32)


def one_hot(index, count):
    return (index[:, None] == jnp.arange(count, dtype=I32)[None, :]).astype(BF)


def one_hot_t(index, count):
    return (index[None, :] == jnp.arange(count, dtype=I32)[:, None]).astype(BF)


def lanes(shape):
    return lax.broadcasted_iota(I32, shape, 1)


def sublanes(shape):
    return lax.broadcasted_iota(I32, shape, 0)


def row_of(values, width):
    return jnp.pad(values.astype(BF), (0, width - values.shape[0]))[None, :]


def fresh_row(side, place):
    return (place % 4) * 16 + (side + 1) * 4 + place // 4


def local_call(body, outs, operands, scratch=(), flops=0, limit=24):
    return pl.pallas_call(
        body,
        out_shape=[jax.ShapeDtypeStruct(shape, kind) for shape, kind in outs],
        in_specs=[pl.BlockSpec(memory_space=pltpu.SMEM)]
        + [pl.BlockSpec(memory_space=pltpu.VMEM)] * (len(operands) - 1),
        out_specs=[pl.BlockSpec(memory_space=pltpu.VMEM)] * len(outs),
        scratch_shapes=list(scratch),
        compiler_params=pltpu.CompilerParams(vmem_limit_bytes=limit * 1024 * 1024),
        cost_estimate=pl.CostEstimate(flops=flops, bytes_accessed=1024 * 1024, transcendentals=0),
    )(*operands)


def length_column(meta):
    shape = meta.shape
    return jnp.sum(jnp.where(lanes(shape) == sublanes(shape), meta, 0.0), axis=1, keepdims=True)


def pool_rows(length, tokens):
    shape = (16, tokens)
    line = lanes(shape)
    inside = (line // 16 == sublanes(shape)) & ((line % 16).astype(F32) < length)
    return inside.astype(F32).astype(BF)


def norm_kernel(where_ref, hidden_ref, meta_ref, block_ref, sum_ref):
    values = hidden_ref[...].astype(F32)
    center = values - jnp.mean(values, axis=-1, keepdims=True)
    spread = jnp.mean(center * center, axis=-1, keepdims=True)
    tokens = values.shape[0]
    block_ref[0:tokens, :] = (center * lax.rsqrt(spread + 1e-05)).astype(BF)
    block_ref[tokens : tokens + 16, :] = meta_ref[...]
    pool = pool_rows(length_column(meta_ref[:, 0:128].astype(F32)), tokens)
    sum_ref[...] = dot(pool, hidden_ref[...])


def encode_kernel(
    where_ref,
    b0, b1, b2, b3,
    own_in, own_out,
    m1, m2, m3,
    o1, o2, o3,
    own_rel, hidden_sum_ref,
    outgoing_ref, normed_ref, slope_ref, pooled_ref, all_out_ref, route_ref, length_ref, rel_hot_ref,
    rel0_ref, rel1_ref, rel2_ref, rel3_ref,
    in_ref, pool_ref, rel_ref,
):
    core, my_x, my_y = where_ref[1], where_ref[2], where_ref[3]
    rel_ref[0:64, :] = own_rel[...]
    for s, block in enumerate((b0, b1, b2, b3)):
        normed_ref[s * 256 : (s + 1) * 256, :] = block[0:256, :]
    in_ref[:, 0:256] = own_in[...]
    all_out_ref[0:256, :] = own_out[...]
    for t, (mine, other) in enumerate(((m1, o1), (m2, o2), (m3, o3)), 1):
        for part, half in ((mine, core), (other, 1 - core)):
            for i in range(2):
                rows = pl.ds(pl.multiple_of(half * 512 + i * 256, 256), 256)
                in_ref[rows, t * 256 : (t + 1) * 256] = part[0:256, i * 256 : (i + 1) * 256]
                rows = pl.ds(pl.multiple_of(t * 256 + half * 128, 128), 128)
                all_out_ref[rows, i * 512 : (i + 1) * 512] = part[256 + i * 128 : 384 + i * 128, :]
                rows = pl.ds(pl.multiple_of(t * 64 + half * 32, 32), 32)
                rel_ref[rows, i * 512 : (i + 1) * 512] = part[512 + i * 32 : 544 + i * 32, :]

    wide = (16, 256)
    slot = lanes(wide) % 16
    bound = lanes((128, 256))
    bound = (bound // 16 + (bound % 16) // 4 + 15) % 16
    bound_hot = (sublanes((128, 256)) == bound + 16).astype(F32).astype(BF)
    ids = jnp.zeros((16, 64), F32)
    asked = (rel0_ref, rel1_ref, rel2_ref, rel3_ref)
    for s, block in enumerate((b0, b1, b2, b3)):
        meta = block[256:272, 0:128]
        values = meta.astype(F32)
        apart = lanes(meta.shape) - sublanes(meta.shape)
        wanted = jnp.where(apart == 32, 32.0 * values, jnp.where(apart == 48, values, 0.0))
        wanted = jnp.sum(wanted, axis=1, keepdims=True)
        line = lanes(wide)
        owner_y = (my_y + jnp.where(line < 64, 0, jnp.where(line < 128, 3, line // 64 - 1))) % 4
        name = (my_x * 4 + owner_y) * 52 + line // 32 % 2 * 26 + line % 32
        pick = (name.astype(F32) == wanted) & (line % 32 < 26)
        asked[s][...] = dot(pick.astype(F32).astype(BF), rel_ref[...]).astype(BF)
        length = length_column(values)
        length_ref[s * 16 : (s + 1) * 16, :] = jnp.broadcast_to(1.0 / length, (16, 128))
        pool_ref[s * 16 : (s + 1) * 16, :] = pool_rows(length, 256)
        sent = dot(meta, bound_hot)
        encoder = lax.rem(my_x + ORIGINS[s], 4)
        chosen = (sent == sublanes(wide).astype(F32)) & (slot % 4 == encoder) & (slot < 12)
        route_ref[s * 16 : (s + 1) * 16, :] = chosen.astype(F32).astype(BF)
        at, to = sublanes((128, 64)), lanes((128, 64)) - s * 16
        inside = (to >= 0) & (to < 16)
        select = jnp.where(inside & (at == 32 + to), 32.0, jnp.where(inside & (at == 48 + to), 1.0, 0.0))
        ids = ids + dot(meta, select.astype(BF))
    line = sublanes((512, 64))
    local = (line // 64) % 2 * 32 + (line // 16) % 4 * 8 + line % 16
    name = (my_x * 4 + line // 128) * 52 + local
    good = (line % 16 < 8) & (local < 52)
    rel_hot_ref[...] = ((name.astype(F32) == ids[0:1, :]) & good).astype(F32).astype(BF)

    @pl.loop(0, 16)
    def _(step):
        s, t = step // 4, step % 4
        rows = pl.ds(pl.multiple_of(s * 256, 256), 256)
        cols = pl.ds(pl.multiple_of(t * 256, 256), 256)
        few = pl.ds(pl.multiple_of(s * 16, 16), 16)
        pre = dot(normed_ref[rows, :], in_ref[:, cols])
        square = pre * pre
        tanh = jnp.tanh(GELU_SCALE * pre * (1.0 + GELU_CUBE * square))
        upper = 0.5 + 0.5 * tanh
        slope = upper + (0.5 * GELU_SCALE) * pre * (1.0 - tanh * tanh) * (1.0 + 3.0 * GELU_CUBE * square)
        slope_ref[rows, cols] = slope.astype(BF)
        pooled_ref[few, cols] = dot(pool_ref[few, :], (pre * upper).astype(BF)).astype(BF)

    partial = dot(pooled_ref[...], all_out_ref[...])
    partial = jnp.concatenate([partial[0:16] + hidden_sum_ref[...], partial[16:64]], axis=0)
    partial = (partial * length_ref[:, 0:1]).astype(BF)
    outgoing_ref[...] = dot_t(route_ref[...], partial).astype(BF)


def graph_kernel(
    where_ref,
    arrived_ref, base_ref, row_hot_ref, own_hot_t_ref, e0, e1, e2, e3,
    src_hot_ref, dst_hot_ref, dst_hot_t_ref, src_row_hot_ref,
    w_msg_ref, w_self_ref, d_out_ref,
    table_out_ref, blocks_ref, graph_out_ref, aggregate_ref, nodes_ref, pre_ref,
    ext_ref, sources_ref, edges_ref, agg_grad_ref, sums_ref, rel_ref,
):
    scale = (256 / 2048) ** 0.5
    rel = e0[...].astype(F32) + e1[...].astype(F32) + e2[...].astype(F32) + e3[...].astype(F32)
    for j in range(16):
        rel_ref[j] = rel[j : j + 1]
    total = arrived_ref[0:64, :].astype(F32)
    for i in range(1, 4):
        total = total + arrived_ref[i * 64 : (i + 1) * 64, :].astype(F32)
    table = total.astype(BF)
    ext_ref[...] = (base_ref[...].astype(F32) + dot(row_hot_ref[...], table)).astype(BF)
    nodes_ref[...] = ext_ref[0:256, :]

    @pl.loop(0, 16)
    def _(j):
        rows = pl.ds(pl.multiple_of(j * 128, 128), 128)
        taken = dot(src_hot_ref[rows, :], ext_ref[...])
        sources_ref[rows, :] = taken.astype(BF)
        edges_ref[rows, :] = (taken * rel_ref[j]).astype(BF)

    @pl.loop(0, 4)
    def _(n):
        cols = pl.ds(pl.multiple_of(n * 256, 256), 256)
        aggregate_ref[:, cols] = (scale * dot(dst_hot_t_ref[...], edges_ref[:, cols])).astype(BF)

    @pl.loop(0, 4)
    def _(n):
        cols = pl.ds(pl.multiple_of(n * 256, 256), 256)
        out_pre = dot(aggregate_ref[...], w_msg_ref[:, cols]) + dot(nodes_ref[...], w_self_ref[:, cols])
        squashed = jnp.tanh(out_pre)
        graph_out_ref[:, cols] = squashed.astype(BF)
        pre_ref[:, cols] = (d_out_ref[:, cols].astype(F32) * (1.0 - squashed * squashed)).astype(BF)

    @pl.loop(0, 4)
    def _(n):
        cols = pl.ds(pl.multiple_of(n * 256, 256), 256)
        agg_grad_ref[:, cols] = (scale * dot_bt(pre_ref[...], w_msg_ref[cols, :])).astype(BF)

    @pl.loop(0, 16)
    def _(j):
        rows = pl.ds(pl.multiple_of(j * 128, 128), 128)
        at_dest = dot(dst_hot_ref[rows, :], agg_grad_ref[...])
        edges_ref[rows, :] = (at_dest * rel_ref[j]).astype(BF)
        sums_ref[j] = jnp.sum(at_dest * sources_ref[rows, :].astype(F32), axis=0, keepdims=True)

    blocks_ref[...] = jnp.concatenate([sums_ref[j] for j in range(16)], axis=0).astype(BF)
    own_pre = dot(own_hot_t_ref[...], pre_ref[0:16, :]).astype(BF)

    @pl.loop(0, 4)
    def _(n):
        cols = pl.ds(pl.multiple_of(n * 256, 256), 256)
        grad = dot(src_row_hot_ref[...], edges_ref[:, cols]) + dot_bt(own_pre, w_self_ref[cols, :])
        table_out_ref[:, cols] = grad.astype(BF)


def back_kernel(
    where_ref,
    returned_ref, route_ref, length_ref, all_out_ref, slope_ref, pooled_ref, normed_t_ref,
    rel_hot_ref, r0, r1, r2, r3,
    kept_ref, given_ref,
    scaled_ref, grad_ref,
):
    core, my_y = where_ref[1], where_ref[3]
    scaled_ref[...] = (dot(route_ref[...], returned_ref[...]) * length_ref[:, 0:1]).astype(BF)
    blocks = jnp.concatenate([r0[...], r1[...], r2[...], r3[...]], axis=0)
    for half, chunk_ref in ((core, kept_ref), (1 - core, given_ref)):
        for y in range(4):
            rows = pl.ds(pl.multiple_of(y * 128 + half * 64, 64), 64)
            rel = dot(rel_hot_ref[rows, :], blocks).astype(BF)
            for z in range(4):
                chunk_ref[z, y, 64:80, :] = rel[z * 16 : (z + 1) * 16]

    @pl.loop(0, 4)
    def _(t):
        cols = pl.ds(pl.multiple_of(t * 256, 256), 256)
        origin = jnp.where(t == 0, 0, jnp.where(t == 1, 3, t - 1))
        owner = lax.rem(my_y + origin, 4)
        upstream = dot_bt(scaled_ref[...], all_out_ref[cols, :]).astype(BF)
        for s in range(4):
            rows = slice(s * 256, (s + 1) * 256)
            shape = (16, 256)
            line = lanes(shape)
            length = 1.0 / length_ref[s * 16 : (s + 1) * 16, 0:1]
            inside = (line // 16 == sublanes(shape)) & ((line % 16).astype(F32) + 0.5 < length)
            pool = inside.astype(F32).astype(BF)
            at_tokens = dot_t(pool, upstream[s * 16 : (s + 1) * 16])
            grad_ref[rows, :] = (slope_ref[rows, cols].astype(F32) * at_tokens).astype(BF)
        for half, chunk_ref in ((1 - core, given_ref), (core, kept_ref)):
            units = pl.ds(pl.multiple_of(t * 256 + half * 128, 128), 128)
            out = dot_t(pooled_ref[:, units], scaled_ref[...]).astype(BF)
            inner = dot(normed_t_ref[pl.ds(pl.multiple_of(half * 512, 512), 512), :], grad_ref[...]).astype(BF)
            for z in range(4):
                chunk_ref[z, owner, 32:64, :] = out[z * 32 : (z + 1) * 32]
                for i in range(4):
                    piece = inner[z * 128 + i * 32 : z * 128 + (i + 1) * 32]
                    chunk_ref[z, owner, 0:32, i * 256 : (i + 1) * 256] = piece


def place_kernel(where_ref, a0, a1, a2, a3, c0, c1, c2, c3, in_ref, out_ref, rel_ref):
    my_z, core = where_ref[0], where_ref[1]
    for pieces, half in (((a0, a1, a2, a3), core), ((c0, c1, c2, c3), 1 - core)):
        for piece, origin in zip(pieces, ORIGINS):
            z = lax.rem(my_z + origin, 4)
            values = piece[...].astype(F32)
            for i in range(4):
                rows = pl.ds(pl.multiple_of(half * 512 + z * 128 + i * 32, 32), 32)
                in_ref[rows, :] = values[0:32, i * 256 : (i + 1) * 256]
            out_ref[pl.ds(pl.multiple_of(half * 128 + z * 32, 32), 32), :] = values[32:64]
            rel_ref[pl.ds(pl.multiple_of(half * 32 + z * 8, 8), 8), :] = values[64:72]


def shards(
    hidden,
    desc_len,
    w_in,
    w_out,
    send_order,
    place_order,
    cache,
    halo_rows,
    edge_src,
    edge_dst,
    edge_rel,
    rel_table,
    w_msg,
    w_self,
    d_out,
):
    entities, length, width = hidden.shape
    tokens = entities * length
    units = w_in.shape[1]
    my_core = lax.axis_index("core")
    where = jnp.stack([lax.axis_index(name) for name in ("z", "core", "x", "y")]).astype(I32)
    src, dst, rel = edge_src[0], edge_dst[0], edge_rel[0]
    shard_rows = rel_table.shape[0]

    meta = row_of(jnp.concatenate([desc_len, send_order[0], rel // 32, rel % 32]), width)
    block, hidden_sum = local_call(
        norm_kernel,
        [((tokens + 16, width), BF), ((entities, width), F32)],
        [where, hidden.reshape(tokens, width), jnp.broadcast_to(meta, (16, width))],
    )
    blocks = [block] + [shift_by(block, "x", s) for s in SHIFTS]

    half_k, half_u = width // 2, units // 2
    in_half = lax.dynamic_slice_in_dim(w_in, my_core * half_k, half_k, 0)
    out_half = lax.dynamic_slice_in_dim(w_out, my_core * half_u, half_u, 0)
    rel_pad = jnp.pad(rel_table.reshape(2, shard_rows // 2, width), ((0, 0), (0, 32 - shard_rows // 2), (0, 0)))
    rel_half = lax.dynamic_index_in_dim(rel_pad, my_core, 0, keepdims=False)
    weights = jnp.concatenate(
        [
            jnp.concatenate([in_half[:units], in_half[units:]], axis=1),
            out_half[:, : 2 * units],
            out_half[:, 2 * units :],
            rel_half[:, : 2 * units],
            rel_half[:, 2 * units :],
        ],
        axis=0,
    )
    mine = [shift_by(weights, "y", s) for s in SHIFTS]
    other = [shift_by(part, "core", 1) for part in mine]

    halo = halo_rows[0]
    place = place_order[0]
    side = halo.shape[0] // 2
    cache_count = cache.shape[0]
    boundary = dot(one_hot(halo - entities, cache_count), cache).astype(BF)
    halo_hot = halo[:, None] == jnp.arange(entities, dtype=I32)[None, :]
    halo_place = jnp.where(halo < entities, jnp.sum(jnp.where(halo_hot, place[None, :], 0), axis=1), 16)

    def edge_of(rows, places):
        return jnp.concatenate([rows, jnp.pad(row_of(places, width), ((0, 15), (0, 0)))], axis=0)

    to_high, to_low = edge_of(boundary[side:], halo_place[side:]), edge_of(boundary[:side], halo_place[:side])
    to_high, to_low, *blocks = lax.optimization_barrier((to_high, to_low, *blocks))
    from_low = shift_by(to_high, GROUP, 1)
    from_high = shift_by(to_low, GROUP, 15)
    low_place = from_low[side, :side].astype(I32)
    high_place = from_high[side, :side].astype(I32)
    own_row = fresh_row(0, place)
    low_row = jnp.where(low_place < 16, fresh_row(-1, low_place), -1)
    high_row = jnp.where(high_place < 16, fresh_row(1, high_place), -1)
    table_row = jnp.concatenate([own_row, jnp.full((cache_count,), -1, I32), low_row, high_row])
    row_hot = one_hot(table_row, 64)
    base = jnp.concatenate([jnp.zeros((entities, width), BF), cache, from_low[:side], from_high[:side]], axis=0)
    node_count = entities + cache_count
    extended_count = node_count + 2 * side
    edge_count = src.shape[0]
    block_count = rel.shape[0]
    src_hot = one_hot(src, extended_count)
    src_row_hot = dot_bt(one_hot_t(table_row, 64), src_hot).astype(BF)

    outgoing, normed, slope, pooled, all_out, route, inverse, rel_hot, *asked = local_call(
        encode_kernel,
        [
            ((256, width), BF),
            ((4 * tokens, width), BF),
            ((4 * tokens, 4 * units), BF),
            ((4 * entities, 4 * units), BF),
            ((4 * units, width), BF),
            ((4 * entities, 256), BF),
            ((4 * entities, 128), F32),
            ((512, 64), BF),
        ]
        + [((entities, width), BF)] * 4,
        [where, *blocks, w_in, w_out, *mine, *other, rel_pad.reshape(64, width), hidden_sum],
        [
            pltpu.VMEM((width, 4 * units), BF),
            pltpu.VMEM((4 * entities, tokens), BF),
            pltpu.VMEM((256, width), BF),
        ],
        flops=2 * 4 * tokens * width * 4 * units,
    )
    arrived = lax.all_to_all(outgoing.reshape(16, 16, width), GROUP, 0, 0, tiled=True).reshape(256, width)
    rel_rows = [asked[0]] + [shift_by(rows, "x", o) for rows, o in zip(asked[1:], ORIGINS[1:])]
    normed_t = normed.T

    grad_table, grad_blocks, graph_out, aggregate, nodes, grad_pre = local_call(
        graph_kernel,
        [
            ((64, width), BF),
            ((block_count, width), BF),
            ((node_count, width), BF),
            ((node_count, width), BF),
            ((node_count, width), BF),
            ((node_count, width), BF),
        ],
        [
            where,
            arrived,
            base,
            row_hot,
            one_hot_t(own_row, 64),
            *rel_rows,
            src_hot,
            one_hot(dst, node_count),
            one_hot_t(dst, node_count),
            src_row_hot,
            w_msg,
            w_self,
            d_out,
        ],
        [
            pltpu.VMEM((extended_count, width), BF),
            pltpu.VMEM((edge_count, width), BF),
            pltpu.VMEM((edge_count, width), BF),
            pltpu.VMEM((node_count, width), BF),
            pltpu.VMEM((block_count, 1, width), F32),
            pltpu.VMEM((block_count, 1, width), F32),
        ],
        flops=6 * 10**9,
    )

    back = jnp.broadcast_to(grad_table.reshape(1, 4, 16, width), (4, 4, 16, width))
    returned = lax.all_to_all(back.reshape(16, 16, width), GROUP, 0, 0, tiled=True).reshape(256, width)
    rel_blocks = [grad_blocks] + [shift_by(grad_blocks, "x", s) for s in SHIFTS]

    graph_grads = jnp.stack([dot_t(aggregate, grad_pre).astype(BF), dot_t(nodes, grad_pre).astype(BF)])
    graph_grads = graph_grads.reshape(2, 4, 2, 4, 4, 8, width).transpose(2, 3, 1, 4, 0, 5, 6)
    graph_grads = graph_grads.reshape(2, 4, 16, 16, width)
    graph_kept = lax.dynamic_index_in_dim(graph_grads, my_core, 0, keepdims=False)
    graph_given = lax.dynamic_index_in_dim(graph_grads, 1 - my_core, 0, keepdims=False)
    chip = (graph_kept.astype(F32) + shift_by(graph_given, "core", 1).astype(F32)).astype(BF)
    returned, chip = lax.optimization_barrier((returned, chip))
    my_x = lax.axis_index("x")

    def for_x(shift):
        return lax.dynamic_index_in_dim(chip, (my_x + shift) % 4, 0, keepdims=False)

    line_sum = for_x(0).astype(F32)
    for s in SHIFTS:
        line_sum = line_sum + shift_by(for_x(s), "x", s).astype(F32)
    plane = lax.all_to_all(line_sum.astype(BF), ("z", "y"), 0, 0, tiled=True)
    weight_rows = jnp.sum(plane.astype(F32), axis=0)
    grad_msg, grad_self = weight_rows[:8], weight_rows[8:]

    kept, given = local_call(
        back_kernel,
        [((4, 4, 80, width), BF), ((4, 4, 80, width), BF)],
        [where, returned, route, inverse, all_out, slope, pooled, normed_t, rel_hot, *rel_blocks],
        [pltpu.VMEM((4 * entities, width), BF), pltpu.VMEM((4 * tokens, units), BF)],
        flops=2 * 4 * tokens * width * 4 * units,
    )
    chunks = (kept.astype(F32) + shift_by(given, "core", 1).astype(F32)).astype(BF)
    chunks = lax.all_to_all(chunks.reshape(16, 80, width), ("z", "y"), 0, 0, tiled=True)
    part = jnp.sum(chunks.astype(F32), axis=0).astype(BF)
    parts = [part] + [shift_by(part, "z", s) for s in SHIFTS]
    others = [shift_by(piece, "core", 1) for piece in parts]
    grad_w_in, grad_w_out, grad_rel = local_call(
        place_kernel,
        [((width, units), F32), ((units, width), F32), ((64, width), F32)],
        [where, *parts, *others],
    )
    return (graph_out, grad_w_in, grad_w_out, grad_rel[:shard_rows], grad_msg, grad_self)


def solution(mesh):
    fine = Mesh(mesh.devices.reshape(4, 2, 4, 4), ("z", "core", "x", "y"))
    every = ("z", "core", "x", "y")
    placed = (
        P(every, None, None),
        P(every),
        P(None, GROUP),
        P(GROUP, None),
        P(every, None),
        P(every, None),
        P(every, None),
        P(every, None),
        P(every, None),
        P(every, None),
        P(every, None),
        P(GROUP, None),
        P(),
        P(),
        P(every, None),
    )
    return jax.shard_map(
        shards,
        mesh=fine,
        in_specs=placed,
        out_specs=(
            P(every, None),
            P(None, GROUP),
            P(GROUP, None),
            P(GROUP, None),
            P(every, None),
            P(every, None),
        ),
        check_vma=False,
    )
```

```python
import jax
import jax.numpy as jnp
import numpy as np
from jax import lax
from jax.experimental import pallas as pl
from jax.experimental.pallas import tpu as pltpu
from jax.sharding import Mesh
from jax.sharding import PartitionSpec as P

BF = jnp.bfloat16
F32 = jnp.float32
I32 = jnp.int32
GROUP = ("x", "y")
SHIFTS = (1, 3, 2)
ORIGINS = (0, 3, 1, 2)
GELU_SCALE = float(np.sqrt(2.0 / np.pi))
GELU_CUBE = 0.044715


def shift_by(value, axis, shift):
    count = lax.axis_size(axis)
    return lax.ppermute(value, axis, [(i, (i + shift) % count) for i in range(count)])


def dot(a, b):
    return jnp.dot(a, b, preferred_element_type=F32)


def dot_t(a, b):
    return lax.dot_general(a, b, (((0,), (0,)), ((), ())), preferred_element_type=F32)


def dot_bt(a, b):
    return lax.dot_general(a, b, (((1,), (1,)), ((), ())), preferred_element_type=F32)


def one_hot(index, count):
    return (index[:, None] == jnp.arange(count, dtype=I32)[None, :]).astype(BF)


def one_hot_t(index, count):
    return (index[None, :] == jnp.arange(count, dtype=I32)[:, None]).astype(BF)


def lanes(shape):
    return lax.broadcasted_iota(I32, shape, 1)


def sublanes(shape):
    return lax.broadcasted_iota(I32, shape, 0)


def row_of(values, width):
    return jnp.pad(values.astype(BF), (0, width - values.shape[0]))[None, :]


def gather_ring(value, axis, cut):
    low, high = shift_by(value, axis, 1), shift_by(value, axis, 3)
    return [low, high, shift_by(low[:cut], axis, 1), shift_by(high[cut:], axis, 3)]


def fresh_row(side, place):
    return (place % 4) * 16 + (side + 1) * 4 + place // 4


class Copies:
    def __init__(self, sems):
        self.sems, self.used = sems, 0

    def start(self, source, target):
        copy = pltpu.make_async_copy(source, target, self.sems.at[self.used])
        self.used += 1
        copy.start()
        return copy


def local_call(body, outs, operands, scratch=(), copies=8, flops=0, limit=44):
    def kernel(*refs):
        body(Copies(refs[-1]), *refs[:-1])

    return pl.pallas_call(
        kernel,
        out_shape=[jax.ShapeDtypeStruct(shape, kind) for shape, kind in outs],
        in_specs=[pl.BlockSpec(memory_space=pltpu.SMEM)]
        + [pl.BlockSpec(memory_space=pl.ANY)] * (len(operands) - 1),
        out_specs=[pl.BlockSpec(memory_space=pl.ANY)] * len(outs),
        scratch_shapes=[*scratch, pltpu.SemaphoreType.DMA((copies,))],
        compiler_params=pltpu.CompilerParams(vmem_limit_bytes=limit * 1024 * 1024),
        cost_estimate=pl.CostEstimate(flops=flops, bytes_accessed=1024 * 1024, transcendentals=0),
    )(*operands)


def like(arrays):
    return [pltpu.VMEM(array.shape, array.dtype) for array in arrays]


def filled(outs):
    return [pltpu.VMEM(shape, kind) for shape, kind in outs]


def wait_all(copies):
    for copy in copies:
        copy.wait()


def length_column(meta):
    shape = meta.shape
    return jnp.sum(jnp.where(lanes(shape) == sublanes(shape), meta, 0.0), axis=1, keepdims=True)


def pool_rows(length, tokens):
    shape = (16, tokens)
    line = lanes(shape)
    inside = (line // 16 == sublanes(shape)) & ((line % 16).astype(F32) < length)
    return inside.astype(F32).astype(BF)


def norm_kernel(
    copies,
    where_ref,
    hidden_hbm, meta_hbm, in_hbm, out_hbm, rel_hbm,
    block_hbm, sum_hbm, weights_hbm,
    hidden_ref, meta_ref, block_ref, sum_ref,
):
    core = where_ref[1]
    first = [copies.start(hidden_hbm, hidden_ref), copies.start(meta_hbm, meta_ref)]
    later = []
    for i in range(2):
        cols, wide = pl.ds(i * 256, 256), pl.ds(i * 512, 512)
        source = in_hbm.at[pl.ds(pl.multiple_of(core * 512 + i * 256, 256), 256), :]
        later.append(copies.start(source, weights_hbm.at[pl.ds(0, 256), cols]))
        source = out_hbm.at[pl.ds(pl.multiple_of(core * 128, 128), 128), wide]
        later.append(copies.start(source, weights_hbm.at[pl.ds(256 + i * 128, 128), :]))
        source = rel_hbm.at[pl.ds(pl.multiple_of(core * 32, 32), 32), wide]
        later.append(copies.start(source, weights_hbm.at[pl.ds(512 + i * 32, 32), :]))
    wait_all(first)
    values = hidden_ref[...].astype(F32)
    center = values - jnp.mean(values, axis=-1, keepdims=True)
    spread = jnp.mean(center * center, axis=-1, keepdims=True)
    tokens = values.shape[0]
    block_ref[0:tokens, :] = (center * lax.rsqrt(spread + 1e-05)).astype(BF)
    block_ref[tokens : tokens + 16, :] = meta_ref[...]
    later.append(copies.start(block_ref, block_hbm))
    pool = pool_rows(length_column(meta_ref[:, 0:128].astype(F32)), tokens)
    sum_ref[...] = dot(pool, hidden_ref[...])
    later.append(copies.start(sum_ref, sum_hbm))
    wait_all(later)


def encode_kernel(
    copies,
    where_ref,
    b0, b1, b2, b3_top, b3_rest,
    own_in, own_out, own_rel,
    m1, m2, m3_in, m3_rest,
    o1, o2, o3_in, o3_rest,
    hidden_sum_hbm,
    outgoing_hbm, normed_hbm, slope_hbm, pooled_hbm, all_out_hbm, route_hbm, length_hbm, rel_hot_hbm,
    rel0_hbm, rel1_hbm, rel2_hbm, rel3_hbm,
    outgoing_ref, normed_ref, slope_ref, pooled_ref, all_out_ref, route_ref, length_ref, rel_hot_ref,
    rel0_ref, rel1_ref, rel2_ref, rel3_ref,
    in_ref, pool_ref, rel_ref, meta_ref, hidden_sum_ref,
):
    core, my_x, my_y = where_ref[1], where_ref[2], where_ref[3]
    metas, tokens, weights, tables = [], [], [[], [], [], []], []
    for s, (block, row) in enumerate(((b0, 256), (b1, 256), (b2, 256), (b3_rest, 128))):
        metas.append(copies.start(block.at[pl.ds(row, 16), pl.ds(0, 128)], meta_ref.at[s]))
    tables.append(copies.start(own_rel, rel_ref.at[pl.ds(0, 64), :]))
    pieces = []
    for t, (mine, other) in enumerate(
        (((m1, m1, 256), (o1, o1, 256)), ((m2, m2, 256), (o2, o2, 256)), ((m3_in, m3_rest, 0), (o3_in, o3_rest, 0))), 1
    ):
        for (inner, rest, at), half in ((mine, core), (other, 1 - core)):
            pieces.append((t, inner, rest, at, half))
            for i in range(2):
                rows = pl.ds(pl.multiple_of(t * 64 + half * 32, 32), 32)
                target = rel_ref.at[rows, pl.ds(i * 512, 512)]
                tables.append(copies.start(rest.at[pl.ds(at + 256 + i * 32, 32), :], target))
    for s, (block, row, count) in enumerate(((b0, 0, 256), (b1, 256, 256), (b2, 512, 256), (b3_top, 768, 128), (b3_rest, 896, 128))):
        tokens.append(copies.start(block.at[pl.ds(0, count), :], normed_ref.at[pl.ds(row, count), :]))
    weights[0].append(copies.start(own_in, in_ref.at[:, pl.ds(0, 256)]))
    for t, inner, rest, at, half in pieces:
        for i in range(2):
            rows = pl.ds(pl.multiple_of(half * 512 + i * 256, 256), 256)
            target = in_ref.at[rows, pl.ds(t * 256, 256)]
            weights[t].append(copies.start(inner.at[pl.ds(0, 256), pl.ds(i * 256, 256)], target))
    outer = [
        copies.start(own_out, all_out_ref.at[pl.ds(0, 256), :]),
        copies.start(hidden_sum_hbm, hidden_sum_ref),
    ]
    for t, inner, rest, at, half in pieces:
        for i in range(2):
            rows = pl.ds(pl.multiple_of(t * 256 + half * 128, 128), 128)
            target = all_out_ref.at[rows, pl.ds(i * 512, 512)]
            outer.append(copies.start(rest.at[pl.ds(at + i * 128, 128), :], target))
    wait_all(metas)
    wait_all(tables)

    wide = (16, 256)
    slot = lanes(wide) % 16
    bound = lanes((128, 256))
    bound = (bound // 16 + (bound % 16) // 4 + 15) % 16
    bound_hot = (sublanes((128, 256)) == bound + 16).astype(F32).astype(BF)
    ids = jnp.zeros((16, 64), F32)
    asked = (rel0_ref, rel1_ref, rel2_ref, rel3_ref)
    for s in range(4):
        meta = meta_ref[s]
        values = meta.astype(F32)
        apart = lanes(meta.shape) - sublanes(meta.shape)
        wanted = jnp.where(apart == 32, 32.0 * values, jnp.where(apart == 48, values, 0.0))
        wanted = jnp.sum(wanted, axis=1, keepdims=True)
        line = lanes(wide)
        owner_y = (my_y + jnp.where(line < 64, 0, jnp.where(line < 128, 3, line // 64 - 1))) % 4
        name = (my_x * 4 + owner_y) * 52 + line // 32 % 2 * 26 + line % 32
        pick = (name.astype(F32) == wanted) & (line % 32 < 26)
        asked[s][...] = dot(pick.astype(F32).astype(BF), rel_ref[...]).astype(BF)
        length = length_column(values)
        length_ref[s * 16 : (s + 1) * 16, :] = jnp.broadcast_to(1.0 / length, (16, 128))
        pool_ref[s * 16 : (s + 1) * 16, :] = pool_rows(length, 256)
        sent = dot(meta, bound_hot)
        encoder = lax.rem(my_x + ORIGINS[s], 4)
        chosen = (sent == sublanes(wide).astype(F32)) & (slot % 4 == encoder) & (slot < 12)
        route_ref[s * 16 : (s + 1) * 16, :] = chosen.astype(F32).astype(BF)
        at, to = sublanes((128, 64)), lanes((128, 64)) - s * 16
        inside = (to >= 0) & (to < 16)
        select = jnp.where(inside & (at == 32 + to), 32.0, jnp.where(inside & (at == 48 + to), 1.0, 0.0))
        ids = ids + dot(meta, select.astype(BF))
    line = sublanes((512, 64))
    local = (line // 64) % 2 * 32 + (line // 16) % 4 * 8 + line % 16
    name = (my_x * 4 + line // 128) * 52 + local
    good = (line % 16 < 8) & (local < 52)
    rel_hot_ref[...] = ((name.astype(F32) == ids[0:1, :]) & good).astype(F32).astype(BF)

    sent_out = [
        copies.start(rel0_ref, rel0_hbm),
        copies.start(rel1_ref, rel1_hbm),
        copies.start(rel2_ref, rel2_hbm),
        copies.start(rel3_ref, rel3_hbm),
        copies.start(route_ref, route_hbm),
        copies.start(length_ref, length_hbm),
        copies.start(rel_hot_ref, rel_hot_hbm),
    ]
    wait_all(tokens)
    sent_out.append(copies.start(normed_ref, normed_hbm))
    for t in range(4):
        cols = slice(t * 256, (t + 1) * 256)
        wait_all(weights[t])

        @pl.loop(0, 4)
        def _(s):
            rows = pl.ds(pl.multiple_of(s * 256, 256), 256)
            few = pl.ds(pl.multiple_of(s * 16, 16), 16)
            pre = dot(normed_ref[rows, :], in_ref[:, cols])
            square = pre * pre
            tanh = jnp.tanh(GELU_SCALE * pre * (1.0 + GELU_CUBE * square))
            upper = 0.5 + 0.5 * tanh
            slope = upper + (0.5 * GELU_SCALE) * pre * (1.0 - tanh * tanh) * (1.0 + 3.0 * GELU_CUBE * square)
            slope_ref[rows, cols] = slope.astype(BF)
            pooled_ref[few, cols] = dot(pool_ref[few, :], (pre * upper).astype(BF)).astype(BF)

    sent_out.append(copies.start(slope_ref, slope_hbm))
    sent_out.append(copies.start(pooled_ref, pooled_hbm))
    wait_all(outer)
    sent_out.append(copies.start(all_out_ref, all_out_hbm))
    partial = dot(pooled_ref[...], all_out_ref[...])
    partial = jnp.concatenate([partial[0:16] + hidden_sum_ref[...], partial[16:64]], axis=0)
    partial = (partial * length_ref[:, 0:1]).astype(BF)
    outgoing_ref[...] = dot_t(route_ref[...], partial).astype(BF)
    sent_out.append(copies.start(outgoing_ref, outgoing_hbm))
    wait_all(sent_out)


def graph_kernel(
    copies,
    where_ref,
    arrived_hbm, base_hbm, row_hot_hbm, own_hot_t_hbm, e0_hbm, e1_hbm, e2_hbm, e3_hbm,
    src_hot_hbm, dst_hot_hbm, dst_hot_t_hbm, src_row_hot_hbm,
    w_msg_hbm, w_self_hbm, d_out_hbm,
    table_out_hbm, blocks_hbm, graph_out_hbm, aggregate_hbm, nodes_hbm, pre_hbm,
    arrived_ref, base_ref, row_hot_ref, own_hot_t_ref, e0, e1, e2, e3,
    src_hot_ref, dst_hot_ref, dst_hot_t_ref, src_row_hot_ref,
    w_msg_ref, w_self_ref, d_out_ref,
    table_out_ref, blocks_ref, graph_out_ref, aggregate_ref, nodes_ref, pre_ref,
    ext_ref, sources_ref, edges_ref, agg_grad_ref, sums_ref, rel_ref,
):
    scale = (256 / 2048) ** 0.5
    first = [
        copies.start(arrived_hbm, arrived_ref),
        copies.start(base_hbm, base_ref),
        copies.start(row_hot_hbm, row_hot_ref),
        copies.start(e0_hbm, e0),
        copies.start(e1_hbm, e1),
        copies.start(e2_hbm, e2),
        copies.start(e3_hbm, e3),
        copies.start(src_hot_hbm, src_hot_ref),
    ]
    second = [copies.start(dst_hot_t_hbm, dst_hot_t_ref)]
    third = [
        copies.start(w_msg_hbm, w_msg_ref),
        copies.start(w_self_hbm, w_self_ref),
        copies.start(d_out_hbm, d_out_ref),
    ]
    fourth = [
        copies.start(dst_hot_hbm, dst_hot_ref),
        copies.start(src_row_hot_hbm, src_row_hot_ref),
        copies.start(own_hot_t_hbm, own_hot_t_ref),
    ]
    wait_all(first)
    rel = e0[...].astype(F32) + e1[...].astype(F32) + e2[...].astype(F32) + e3[...].astype(F32)
    for j in range(16):
        rel_ref[j] = rel[j : j + 1]
    total = arrived_ref[0:64, :].astype(F32)
    for i in range(1, 4):
        total = total + arrived_ref[i * 64 : (i + 1) * 64, :].astype(F32)
    table = total.astype(BF)
    ext_ref[...] = (base_ref[...].astype(F32) + dot(row_hot_ref[...], table)).astype(BF)
    nodes_ref[...] = ext_ref[0:256, :]
    sent_out = [copies.start(nodes_ref, nodes_hbm)]

    @pl.loop(0, 16)
    def _(j):
        rows = pl.ds(pl.multiple_of(j * 128, 128), 128)
        taken = dot(src_hot_ref[rows, :], ext_ref[...])
        sources_ref[rows, :] = taken.astype(BF)
        edges_ref[rows, :] = (taken * rel_ref[j]).astype(BF)

    wait_all(second)

    @pl.loop(0, 4)
    def _(n):
        cols = pl.ds(pl.multiple_of(n * 256, 256), 256)
        aggregate_ref[:, cols] = (scale * dot(dst_hot_t_ref[...], edges_ref[:, cols])).astype(BF)

    sent_out.append(copies.start(aggregate_ref, aggregate_hbm))
    wait_all(third)

    @pl.loop(0, 4)
    def _(n):
        cols = pl.ds(pl.multiple_of(n * 256, 256), 256)
        out_pre = dot(aggregate_ref[...], w_msg_ref[:, cols]) + dot(nodes_ref[...], w_self_ref[:, cols])
        squashed = jnp.tanh(out_pre)
        graph_out_ref[:, cols] = squashed.astype(BF)
        pre_ref[:, cols] = (d_out_ref[:, cols].astype(F32) * (1.0 - squashed * squashed)).astype(BF)

    sent_out.append(copies.start(graph_out_ref, graph_out_hbm))
    sent_out.append(copies.start(pre_ref, pre_hbm))

    @pl.loop(0, 4)
    def _(n):
        cols = pl.ds(pl.multiple_of(n * 256, 256), 256)
        agg_grad_ref[:, cols] = (scale * dot_bt(pre_ref[...], w_msg_ref[cols, :])).astype(BF)

    wait_all(fourth)

    @pl.loop(0, 16)
    def _(j):
        rows = pl.ds(pl.multiple_of(j * 128, 128), 128)
        at_dest = dot(dst_hot_ref[rows, :], agg_grad_ref[...])
        edges_ref[rows, :] = (at_dest * rel_ref[j]).astype(BF)
        sums_ref[j] = jnp.sum(at_dest * sources_ref[rows, :].astype(F32), axis=0, keepdims=True)

    blocks_ref[...] = jnp.concatenate([sums_ref[j] for j in range(16)], axis=0).astype(BF)
    sent_out.append(copies.start(blocks_ref, blocks_hbm))
    own_pre = dot(own_hot_t_ref[...], pre_ref[0:16, :]).astype(BF)

    @pl.loop(0, 4)
    def _(n):
        cols = pl.ds(pl.multiple_of(n * 256, 256), 256)
        grad = dot(src_row_hot_ref[...], edges_ref[:, cols]) + dot_bt(own_pre, w_self_ref[cols, :])
        table_out_ref[:, cols] = grad.astype(BF)

    sent_out.append(copies.start(table_out_ref, table_out_hbm))
    wait_all(sent_out)


def weight_kernel(
    copies,
    where_ref,
    aggregate_hbm, nodes_hbm, pre_hbm,
    kept_hbm, given_hbm,
    aggregate_ref, nodes_ref, pre_ref,
    kept_ref, given_ref,
):
    core = where_ref[1]
    wait_all(
        [copies.start(aggregate_hbm, aggregate_ref), copies.start(nodes_hbm, nodes_ref), copies.start(pre_hbm, pre_ref)]
    )
    sent_out = []
    for half, chunk_ref, chunk_hbm in ((1 - core, given_ref, given_hbm), (core, kept_ref, kept_hbm)):

        @pl.loop(0, 4)
        def _(z):
            rows = pl.ds(pl.multiple_of(z * 256 + half * 128, 128), 128)
            msg = dot_t(aggregate_ref[:, rows], pre_ref[...])
            own = dot_t(nodes_ref[:, rows], pre_ref[...])
            for x in range(4):
                for y in range(4):
                    at = (x * 4 + y) * 8
                    both = jnp.concatenate([msg[at : at + 8], own[at : at + 8]], axis=0)
                    chunk_ref[x, z * 4 + y] = both.astype(BF)

        sent_out.append(copies.start(chunk_ref, chunk_hbm))
    wait_all(sent_out)


def back_kernel(
    copies,
    where_ref,
    returned_hbm, route_hbm, length_hbm, all_out_hbm, slope_hbm, pooled_hbm, normed_t_hbm,
    rel_hot_hbm, r0_hbm, r1_hbm, r2_hbm, r3_hbm,
    kept_hbm, given_hbm,
    returned_ref, route_ref, length_ref, all_out_ref, slope_ref, pooled_ref, normed_t_ref,
    rel_hot_ref, r0, r1, r2, r3,
    kept_ref, given_ref,
    scaled_ref, grad_ref,
):
    core, my_y = where_ref[1], where_ref[3]
    first = [
        copies.start(returned_hbm, returned_ref),
        copies.start(route_hbm, route_ref),
        copies.start(length_hbm, length_ref),
        copies.start(rel_hot_hbm, rel_hot_ref),
        copies.start(r0_hbm, r0),
        copies.start(r1_hbm, r1),
        copies.start(r2_hbm, r2),
        copies.start(r3_hbm, r3),
    ]
    second = [
        copies.start(all_out_hbm, all_out_ref),
        copies.start(slope_hbm, slope_ref),
        copies.start(pooled_hbm, pooled_ref),
        copies.start(normed_t_hbm, normed_t_ref),
    ]
    wait_all(first)
    scaled_ref[...] = (dot(route_ref[...], returned_ref[...]) * length_ref[:, 0:1]).astype(BF)
    blocks = jnp.concatenate([r0[...], r1[...], r2[...], r3[...]], axis=0)
    for half, chunk_ref in ((core, kept_ref), (1 - core, given_ref)):
        for y in range(4):
            rows = pl.ds(pl.multiple_of(y * 128 + half * 64, 64), 64)
            rel = dot(rel_hot_ref[rows, :], blocks).astype(BF)
            for z in range(4):
                chunk_ref[z, y, 64:80, :] = rel[z * 16 : (z + 1) * 16]

    wait_all(second)

    @pl.loop(0, 4)
    def _(t):
        cols = pl.ds(pl.multiple_of(t * 256, 256), 256)
        origin = jnp.where(t == 0, 0, jnp.where(t == 1, 3, t - 1))
        owner = lax.rem(my_y + origin, 4)
        upstream = dot_bt(scaled_ref[...], all_out_ref[cols, :]).astype(BF)
        for s in range(4):
            rows = slice(s * 256, (s + 1) * 256)
            shape = (16, 256)
            line = lanes(shape)
            length = 1.0 / length_ref[s * 16 : (s + 1) * 16, 0:1]
            inside = (line // 16 == sublanes(shape)) & ((line % 16).astype(F32) + 0.5 < length)
            pool = inside.astype(F32).astype(BF)
            at_tokens = dot_t(pool, upstream[s * 16 : (s + 1) * 16])
            grad_ref[rows, :] = (slope_ref[rows, cols].astype(F32) * at_tokens).astype(BF)
        for half, chunk_ref in ((1 - core, given_ref), (core, kept_ref)):
            units = pl.ds(pl.multiple_of(t * 256 + half * 128, 128), 128)
            out = dot_t(pooled_ref[:, units], scaled_ref[...]).astype(BF)
            inner = dot(normed_t_ref[pl.ds(pl.multiple_of(half * 512, 512), 512), :], grad_ref[...]).astype(BF)
            for z in range(4):
                chunk_ref[z, owner, 32:64, :] = out[z * 32 : (z + 1) * 32]
                for i in range(4):
                    piece = inner[z * 128 + i * 32 : z * 128 + (i + 1) * 32]
                    chunk_ref[z, owner, 0:32, i * 256 : (i + 1) * 256] = piece


    sent_out = [copies.start(given_ref, given_hbm), copies.start(kept_ref, kept_hbm)]
    wait_all(sent_out)


def place_kernel(
    copies,
    where_ref,
    h0, h1, h2, h3, h4, h5, h6, h7,
    in_hbm, out_hbm, rel_hbm,
    a0, a1, a2, a3, c0, c1, c2, c3,
    in_ref, out_ref, rel_ref,
):
    sources = (h0, h1, h2, h3, h4, h5, h6, h7)
    targets = (a0, a1, a2, a3, c0, c1, c2, c3)
    wait_all([copies.start(source, target) for source, target in zip(sources, targets)])
    my_z, core = where_ref[0], where_ref[1]
    for pieces, half in (((a0, a1, a2, a3), core), ((c0, c1, c2, c3), 1 - core)):
        for piece, origin in zip(pieces, ORIGINS):
            z = lax.rem(my_z + origin, 4)
            values = piece[...].astype(F32)
            for i in range(4):
                rows = pl.ds(pl.multiple_of(half * 512 + z * 128 + i * 32, 32), 32)
                in_ref[rows, :] = values[0:32, i * 256 : (i + 1) * 256]
            out_ref[pl.ds(pl.multiple_of(half * 128 + z * 32, 32), 32), :] = values[32:64]
            rel_ref[pl.ds(pl.multiple_of(half * 32 + z * 8, 8), 8), :] = values[64:72]
    wait_all([copies.start(in_ref, in_hbm), copies.start(out_ref, out_hbm), copies.start(rel_ref, rel_hbm)])


def shards(
    hidden,
    desc_len,
    w_in,
    w_out,
    send_order,
    place_order,
    cache,
    halo_rows,
    edge_src,
    edge_dst,
    edge_rel,
    rel_table,
    w_msg,
    w_self,
    d_out,
):
    entities, length, width = hidden.shape
    tokens = entities * length
    units = w_in.shape[1]
    my_core = lax.axis_index("core")
    where = jnp.stack([lax.axis_index(name) for name in ("z", "core", "x", "y")]).astype(I32)
    src, dst, rel = edge_src[0], edge_dst[0], edge_rel[0]
    shard_rows = rel_table.shape[0]

    meta = row_of(jnp.concatenate([desc_len, send_order[0], rel // 32, rel % 32]), width)
    rel_pad = jnp.pad(rel_table.reshape(2, shard_rows // 2, width), ((0, 0), (0, 32 - shard_rows // 2), (0, 0)))
    rel_pad = rel_pad.reshape(64, width)
    operands = [hidden.reshape(tokens, width), jnp.broadcast_to(meta, (16, width)), w_in, w_out, rel_pad]
    outs = [((tokens + 16, width), BF), ((entities, width), F32)]
    block, hidden_sum, weights = local_call(
        norm_kernel,
        [*outs, ((576, 512), BF)],
        [where, *operands],
        like(operands[:2]) + filled(outs),
        copies=10,
    )
    blocks = [block, *gather_ring(block, "x", 128)]
    mine = gather_ring(weights, "y", 256)
    other = [shift_by(part, "core", 1) for part in mine]

    outs = [
        ((256, width), BF),
        ((4 * tokens, width), BF),
        ((4 * tokens, 4 * units), BF),
        ((4 * entities, 4 * units), BF),
        ((4 * units, width), BF),
        ((4 * entities, 256), BF),
        ((4 * entities, 128), F32),
        ((512, 64), BF),
    ] + [((entities, width), BF)] * 4
    outgoing, normed, slope, pooled, all_out, route, inverse, rel_hot, *asked = local_call(
        encode_kernel,
        outs,
        [where, *blocks, w_in, w_out, rel_pad, *mine, *other, hidden_sum],
        filled(outs)
        + [
            pltpu.VMEM((width, 4 * units), BF),
            pltpu.VMEM((4 * entities, tokens), BF),
            pltpu.VMEM((256, width), BF),
            pltpu.VMEM((4, 16, 128), BF),
            pltpu.VMEM((entities, width), F32),
        ],
        copies=64,
        flops=2 * 4 * tokens * width * 4 * units,
    )

    halo = halo_rows[0]
    place = place_order[0]
    side = halo.shape[0] // 2
    cache_count = cache.shape[0]
    boundary = dot(one_hot(halo - entities, cache_count), cache).astype(BF)
    halo_hot = halo[:, None] == jnp.arange(entities, dtype=I32)[None, :]
    halo_place = jnp.where(halo < entities, jnp.sum(jnp.where(halo_hot, place[None, :], 0), axis=1), 16)

    def edge_of(rows, places):
        return jnp.concatenate([rows, jnp.pad(row_of(places, width), ((0, 15), (0, 0)))], axis=0)

    to_high, to_low = edge_of(boundary[side:], halo_place[side:]), edge_of(boundary[:side], halo_place[:side])
    to_high, to_low, outgoing = lax.optimization_barrier((to_high, to_low, outgoing))
    from_low = shift_by(to_high, GROUP, 1)
    from_high = shift_by(to_low, GROUP, 15)
    low_place = from_low[side, :side].astype(I32)
    high_place = from_high[side, :side].astype(I32)
    own_row = fresh_row(0, place)
    low_row = jnp.where(low_place < 16, fresh_row(-1, low_place), -1)
    high_row = jnp.where(high_place < 16, fresh_row(1, high_place), -1)
    table_row = jnp.concatenate([own_row, jnp.full((cache_count,), -1, I32), low_row, high_row])
    row_hot = one_hot(table_row, 64)
    base = jnp.concatenate([jnp.zeros((entities, width), BF), cache, from_low[:side], from_high[:side]], axis=0)
    node_count = entities + cache_count
    extended_count = node_count + 2 * side
    edge_count = src.shape[0]
    block_count = rel.shape[0]
    src_hot = one_hot(src, extended_count)
    src_row_hot = dot_bt(one_hot_t(table_row, 64), src_hot).astype(BF)

    arrived = lax.all_to_all(outgoing.reshape(16, 16, width), GROUP, 0, 0, tiled=True).reshape(256, width)
    rel_rows = [asked[0]] + [shift_by(rows, "x", o) for rows, o in zip(asked[1:], ORIGINS[1:])]
    normed_t = normed.T

    outs = [((64, width), BF), ((block_count, width), BF)] + [((node_count, width), BF)] * 4
    operands = [
        arrived,
        base,
        row_hot,
        one_hot_t(own_row, 64),
        *rel_rows,
        src_hot,
        one_hot(dst, node_count),
        one_hot_t(dst, node_count),
        src_row_hot,
        w_msg,
        w_self,
        d_out,
    ]
    grad_table, grad_blocks, graph_out, aggregate, nodes, grad_pre = local_call(
        graph_kernel,
        outs,
        [where, *operands],
        like(operands)
        + filled(outs)
        + [
            pltpu.VMEM((extended_count, width), BF),
            pltpu.VMEM((edge_count, width), BF),
            pltpu.VMEM((edge_count, width), BF),
            pltpu.VMEM((node_count, width), BF),
            pltpu.VMEM((block_count, 1, width), F32),
            pltpu.VMEM((block_count, 1, width), F32),
        ],
        copies=24,
        flops=6 * 10**9,
    )

    back = jnp.broadcast_to(grad_table.reshape(1, 4, 16, width), (4, 4, 16, width))
    returned = lax.all_to_all(back.reshape(16, 16, width), GROUP, 0, 0, tiled=True).reshape(256, width)
    rel_blocks = [grad_blocks] + [shift_by(grad_blocks, "x", s) for s in SHIFTS]

    outs = [((4, 16, 16, width), BF)] * 2
    operands = [aggregate, nodes, grad_pre]
    graph_kept, graph_given = local_call(
        weight_kernel, outs, [where, *operands], like(operands) + filled(outs), flops=10**9
    )
    chip = (graph_kept.astype(F32) + shift_by(graph_given, "core", 1).astype(F32)).astype(BF)
    line = lax.all_to_all(chip, "x", 0, 0, tiled=True)

    outs = [((4, 4, 80, width), BF)] * 2
    operands = [returned, route, inverse, all_out, slope, pooled, normed_t, rel_hot, *rel_blocks]
    kept, given = local_call(
        back_kernel,
        outs,
        [where, *operands],
        like(operands)
        + filled(outs)
        + [pltpu.VMEM((4 * entities, width), BF), pltpu.VMEM((4 * tokens, units), BF)],
        copies=16,
        flops=2 * 4 * tokens * width * 4 * units,
    )
    given, line = lax.optimization_barrier((given, line))
    line_sum = jnp.sum(line.astype(F32), axis=0).astype(BF)
    chunks = (kept.astype(F32) + shift_by(given, "core", 1).astype(F32)).astype(BF)
    chunks = jnp.concatenate([chunks.reshape(16, 80, width), line_sum], axis=1)
    chunks = lax.all_to_all(chunks, ("z", "y"), 0, 0, tiled=True)
    summed = jnp.sum(chunks.astype(F32), axis=0)
    grad_msg, grad_self = summed[80:88], summed[88:96]
    part = summed[:80].astype(BF)
    parts = [part] + [shift_by(part, "z", s) for s in SHIFTS]
    others = [shift_by(piece, "core", 1) for piece in parts]
    outs = [((width, units), F32), ((units, width), F32), ((64, width), F32)]
    operands = [*parts, *others]
    grad_w_in, grad_w_out, grad_rel = local_call(
        place_kernel, outs, [where, *operands], like(operands) + filled(outs), copies=12
    )
    return (graph_out, grad_w_in, grad_w_out, grad_rel[:shard_rows], grad_msg, grad_self)


def solution(mesh):
    fine = Mesh(mesh.devices.reshape(4, 2, 4, 4), ("z", "core", "x", "y"))
    every = ("z", "core", "x", "y")
    placed = (
        P(every, None, None),
        P(every),
        P(None, GROUP),
        P(GROUP, None),
        P(every, None),
        P(every, None),
        P(every, None),
        P(every, None),
        P(every, None),
        P(every, None),
        P(every, None),
        P(GROUP, None),
        P(),
        P(),
        P(every, None),
    )
    return jax.shard_map(
        shards,
        mesh=fine,
        in_specs=placed,
        out_specs=(
            P(every, None),
            P(None, GROUP),
            P(GROUP, None),
            P(GROUP, None),
            P(every, None),
            P(every, None),
        ),
        check_vma=False,
    )
```

```python
import jax
import jax.numpy as jnp
import numpy as np
from jax import lax
from jax.experimental import pallas as pl
from jax.experimental.pallas import tpu as pltpu
from jax.sharding import Mesh
from jax.sharding import PartitionSpec as P

BF = jnp.bfloat16
F32 = jnp.float32
I32 = jnp.int32
GROUP = ("x", "y")
SHIFTS = (1, 3, 2)
ORIGINS = (0, 3, 1, 2)
GELU_SCALE = float(np.sqrt(2.0 / np.pi))
GELU_CUBE = 0.044715


def shift_by(value, axis, shift):
    count = lax.axis_size(axis)
    return lax.ppermute(value, axis, [(i, (i + shift) % count) for i in range(count)])


def dot(a, b):
    return jnp.dot(a, b, preferred_element_type=F32)


def dot_t(a, b):
    return lax.dot_general(a, b, (((0,), (0,)), ((), ())), preferred_element_type=F32)


def dot_bt(a, b):
    return lax.dot_general(a, b, (((1,), (1,)), ((), ())), preferred_element_type=F32)


def one_hot(index, count):
    return (index[:, None] == jnp.arange(count, dtype=I32)[None, :]).astype(BF)


def one_hot_t(index, count):
    return (index[None, :] == jnp.arange(count, dtype=I32)[:, None]).astype(BF)


def lanes(shape):
    return lax.broadcasted_iota(I32, shape, 1)


def sublanes(shape):
    return lax.broadcasted_iota(I32, shape, 0)


def row_of(values, width):
    return jnp.pad(values.astype(BF), (0, width - values.shape[0]))[None, :]


def gather_ring(value, axis, cut):
    low, high = shift_by(value, axis, 1), shift_by(value, axis, 3)
    return [low, high, shift_by(low[:cut], axis, 1), shift_by(high[cut:], axis, 3)]


def fresh_row(side, place):
    return (place % 4) * 16 + (side + 1) * 4 + place // 4


class Copies:
    def __init__(self, sems):
        self.sems, self.used = sems, 0

    def start(self, source, target):
        copy = pltpu.make_async_copy(source, target, self.sems.at[self.used])
        self.used += 1
        copy.start()
        return copy


def local_call(body, outs, operands, scratch=(), copies=8, flops=0, limit=60):
    def kernel(*refs):
        body(Copies(refs[-1]), *refs[:-1])

    return pl.pallas_call(
        kernel,
        out_shape=[jax.ShapeDtypeStruct(shape, kind) for shape, kind in outs],
        in_specs=[pl.BlockSpec(memory_space=pltpu.SMEM)]
        + [pl.BlockSpec(memory_space=pltpu.HBM)] * (len(operands) - 1),
        out_specs=[pl.BlockSpec(memory_space=pltpu.HBM)] * len(outs),
        scratch_shapes=[*scratch, pltpu.SemaphoreType.DMA((copies,))],
        compiler_params=pltpu.CompilerParams(vmem_limit_bytes=limit * 1024 * 1024),
        cost_estimate=pl.CostEstimate(flops=flops, bytes_accessed=1024 * 1024, transcendentals=0),
    )(*operands)


def like(arrays):
    return [pltpu.VMEM(array.shape, array.dtype) for array in arrays]


def filled(outs):
    return [pltpu.VMEM(shape, kind) for shape, kind in outs]


def wait_all(copies):
    for copy in copies:
        copy.wait()


def length_column(meta):
    shape = meta.shape
    return jnp.sum(jnp.where(lanes(shape) == sublanes(shape), meta, 0.0), axis=1, keepdims=True)


def pool_rows(length, tokens):
    shape = (16, tokens)
    line = lanes(shape)
    inside = (line // 16 == sublanes(shape)) & ((line % 16).astype(F32) < length)
    return inside.astype(F32).astype(BF)


def norm_kernel(
    copies,
    where_ref,
    hidden_hbm, meta_hbm, in_hbm, out_hbm, rel_hbm,
    block_hbm, sum_hbm, weights_hbm,
    hidden_ref, meta_ref, block_ref, sum_ref,
):
    core = where_ref[1]
    first = [copies.start(hidden_hbm, hidden_ref), copies.start(meta_hbm, meta_ref)]
    later = []
    for i in range(2):
        cols, wide = pl.ds(i * 256, 256), pl.ds(i * 512, 512)
        source = in_hbm.at[pl.ds(pl.multiple_of(core * 512 + i * 256, 256), 256), :]
        later.append(copies.start(source, weights_hbm.at[pl.ds(0, 256), cols]))
        source = out_hbm.at[pl.ds(pl.multiple_of(core * 128, 128), 128), wide]
        later.append(copies.start(source, weights_hbm.at[pl.ds(256 + i * 128, 128), :]))
        source = rel_hbm.at[pl.ds(pl.multiple_of(core * 32, 32), 32), wide]
        later.append(copies.start(source, weights_hbm.at[pl.ds(512 + i * 32, 32), :]))
    wait_all(first)
    values = hidden_ref[...].astype(F32)
    center = values - jnp.mean(values, axis=-1, keepdims=True)
    spread = jnp.mean(center * center, axis=-1, keepdims=True)
    tokens = values.shape[0]
    block_ref[0:tokens, :] = (center * lax.rsqrt(spread + 1e-05)).astype(BF)
    block_ref[tokens : tokens + 16, :] = meta_ref[...]
    later.append(copies.start(block_ref, block_hbm))
    pool = pool_rows(length_column(meta_ref[:, 0:128].astype(F32)), tokens)
    sum_ref[...] = dot(pool, hidden_ref[...])
    later.append(copies.start(sum_ref, sum_hbm))
    wait_all(later)


def encode_kernel(
    copies,
    where_ref,
    b0, b1, b2, b3_top, b3_rest,
    own_in, own_out, own_rel,
    m1, m2, m3_in, m3_rest,
    o1, o2, o3_in, o3_rest,
    hidden_sum_hbm,
    outgoing_hbm, normed_hbm, slope_hbm, pooled_hbm, all_out_hbm, route_hbm, length_hbm, rel_hot_hbm,
    rel0_hbm, rel1_hbm, rel2_hbm, rel3_hbm,
    outgoing_ref, normed_ref, slope_ref, pooled_ref, all_out_ref, route_ref, length_ref, rel_hot_ref,
    rel0_ref, rel1_ref, rel2_ref, rel3_ref,
    in_ref, pool_ref, rel_ref, meta_ref, hidden_sum_ref,
):
    core, my_x, my_y = where_ref[1], where_ref[2], where_ref[3]
    metas, tokens, weights, tables = [], [], [[], [], [], []], []
    for s, (block, row) in enumerate(((b0, 256), (b1, 256), (b2, 256), (b3_rest, 128))):
        metas.append(copies.start(block.at[pl.ds(row, 16), pl.ds(0, 128)], meta_ref.at[s]))
    tables.append(copies.start(own_rel, rel_ref.at[pl.ds(0, 64), :]))
    pieces = []
    for t, (mine, other) in enumerate(
        (((m1, m1, 256), (o1, o1, 256)), ((m2, m2, 256), (o2, o2, 256)), ((m3_in, m3_rest, 0), (o3_in, o3_rest, 0))), 1
    ):
        for (inner, rest, at), half in ((mine, core), (other, 1 - core)):
            pieces.append((t, inner, rest, at, half))
            for i in range(2):
                rows = pl.ds(pl.multiple_of(t * 64 + half * 32, 32), 32)
                target = rel_ref.at[rows, pl.ds(i * 512, 512)]
                tables.append(copies.start(rest.at[pl.ds(at + 256 + i * 32, 32), :], target))
    for s, (block, row, count) in enumerate(((b0, 0, 256), (b1, 256, 256), (b2, 512, 256), (b3_top, 768, 128), (b3_rest, 896, 128))):
        tokens.append(copies.start(block.at[pl.ds(0, count), :], normed_ref.at[pl.ds(row, count), :]))
    weights[0].append(copies.start(own_in, in_ref.at[:, pl.ds(0, 256)]))
    for t, inner, rest, at, half in pieces:
        for i in range(2):
            rows = pl.ds(pl.multiple_of(half * 512 + i * 256, 256), 256)
            target = in_ref.at[rows, pl.ds(t * 256, 256)]
            weights[t].append(copies.start(inner.at[pl.ds(0, 256), pl.ds(i * 256, 256)], target))
    outer = [
        copies.start(own_out, all_out_ref.at[pl.ds(0, 256), :]),
        copies.start(hidden_sum_hbm, hidden_sum_ref),
    ]
    for t, inner, rest, at, half in pieces:
        for i in range(2):
            rows = pl.ds(pl.multiple_of(t * 256 + half * 128, 128), 128)
            target = all_out_ref.at[rows, pl.ds(i * 512, 512)]
            outer.append(copies.start(rest.at[pl.ds(at + i * 128, 128), :], target))
    wait_all(metas)
    wait_all(tables)

    wide = (16, 256)
    slot = lanes(wide) % 16
    bound = lanes((128, 256))
    bound = (bound // 16 + (bound % 16) // 4 + 15) % 16
    bound_hot = (sublanes((128, 256)) == bound + 16).astype(F32).astype(BF)
    ids = jnp.zeros((16, 64), F32)
    asked = (rel0_ref, rel1_ref, rel2_ref, rel3_ref)
    for s in range(4):
        meta = meta_ref[s]
        values = meta.astype(F32)
        apart = lanes(meta.shape) - sublanes(meta.shape)
        wanted = jnp.where(apart == 32, 32.0 * values, jnp.where(apart == 48, values, 0.0))
        wanted = jnp.sum(wanted, axis=1, keepdims=True)
        line = lanes(wide)
        owner_y = (my_y + jnp.where(line < 64, 0, jnp.where(line < 128, 3, line // 64 - 1))) % 4
        name = (my_x * 4 + owner_y) * 52 + line // 32 % 2 * 26 + line % 32
        pick = (name.astype(F32) == wanted) & (line % 32 < 26)
        asked[s][...] = dot(pick.astype(F32).astype(BF), rel_ref[...]).astype(BF)
        length = length_column(values)
        length_ref[s * 16 : (s + 1) * 16, :] = jnp.broadcast_to(1.0 / length, (16, 128))
        pool_ref[s * 16 : (s + 1) * 16, :] = pool_rows(length, 256)
        sent = dot(meta, bound_hot)
        encoder = lax.rem(my_x + ORIGINS[s], 4)
        chosen = (sent == sublanes(wide).astype(F32)) & (slot % 4 == encoder) & (slot < 12)
        route_ref[s * 16 : (s + 1) * 16, :] = chosen.astype(F32).astype(BF)
        at, to = sublanes((128, 64)), lanes((128, 64)) - s * 16
        inside = (to >= 0) & (to < 16)
        select = jnp.where(inside & (at == 32 + to), 32.0, jnp.where(inside & (at == 48 + to), 1.0, 0.0))
        ids = ids + dot(meta, select.astype(BF))
    line = sublanes((512, 64))
    local = (line // 64) % 2 * 32 + (line // 16) % 4 * 8 + line % 16
    name = (my_x * 4 + line // 128) * 52 + local
    good = (line % 16 < 8) & (local < 52)
    rel_hot_ref[...] = ((name.astype(F32) == ids[0:1, :]) & good).astype(F32).astype(BF)

    sent_out = [
        copies.start(rel0_ref, rel0_hbm),
        copies.start(rel1_ref, rel1_hbm),
        copies.start(rel2_ref, rel2_hbm),
        copies.start(rel3_ref, rel3_hbm),
        copies.start(route_ref, route_hbm),
        copies.start(length_ref, length_hbm),
        copies.start(rel_hot_ref, rel_hot_hbm),
    ]
    wait_all(tokens)
    sent_out.append(copies.start(normed_ref, normed_hbm))
    for t in range(4):
        cols = slice(t * 256, (t + 1) * 256)
        wait_all(weights[t])

        @pl.loop(0, 2)
        def _(s):
            rows = pl.ds(pl.multiple_of(s * 512, 512), 512)
            pre = dot(normed_ref[rows, :], in_ref[:, cols])
            square = pre * pre
            tanh = jnp.tanh(GELU_SCALE * pre * (1.0 + GELU_CUBE * square))
            upper = 0.5 + 0.5 * tanh
            slope = upper + (0.5 * GELU_SCALE) * pre * (1.0 - tanh * tanh) * (1.0 + 3.0 * GELU_CUBE * square)
            slope_ref[rows, cols] = slope.astype(BF)
            activation = (pre * upper).astype(BF)
            for i in range(2):
                few = pl.ds(pl.multiple_of(s * 32 + i * 16, 16), 16)
                pooled = dot(pool_ref[few, :], activation[i * 256 : (i + 1) * 256])
                pooled_ref[few, cols] = pooled.astype(BF)

    sent_out.append(copies.start(slope_ref, slope_hbm))
    sent_out.append(copies.start(pooled_ref, pooled_hbm))
    wait_all(outer)
    sent_out.append(copies.start(all_out_ref, all_out_hbm))
    partial = dot(pooled_ref[...], all_out_ref[...])
    partial = jnp.concatenate([partial[0:16] + hidden_sum_ref[...], partial[16:64]], axis=0)
    partial = (partial * length_ref[:, 0:1]).astype(BF)
    outgoing_ref[...] = dot_t(route_ref[...], partial).astype(BF)
    sent_out.append(copies.start(outgoing_ref, outgoing_hbm))
    wait_all(sent_out)


def graph_kernel(
    copies,
    where_ref,
    arrived_hbm, base_hbm, row_hot_hbm, own_hot_t_hbm, e0_hbm, e1_hbm, e2_hbm, e3_hbm,
    src_hot_hbm, dst_hot_hbm, dst_hot_t_hbm, src_row_hot_hbm,
    w_msg_hbm, w_self_hbm, d_out_hbm,
    table_out_hbm, blocks_hbm, graph_out_hbm, aggregate_hbm, nodes_hbm, pre_hbm,
    arrived_ref, base_ref, row_hot_ref, own_hot_t_ref, e0, e1, e2, e3,
    src_hot_ref, dst_hot_ref, dst_hot_t_ref, src_row_hot_ref,
    w_msg_ref, w_self_ref, d_out_ref,
    table_out_ref, blocks_ref, graph_out_ref, aggregate_ref, nodes_ref, pre_ref,
    ext_ref, sources_ref, edges_ref, agg_grad_ref, sums_ref, rel_ref,
):
    scale = (256 / 2048) ** 0.5
    first = [
        copies.start(arrived_hbm, arrived_ref),
        copies.start(base_hbm, base_ref),
        copies.start(row_hot_hbm, row_hot_ref),
        copies.start(e0_hbm, e0),
        copies.start(e1_hbm, e1),
        copies.start(e2_hbm, e2),
        copies.start(e3_hbm, e3),
        copies.start(src_hot_hbm, src_hot_ref),
    ]
    second = [copies.start(dst_hot_t_hbm, dst_hot_t_ref)]
    third = [
        copies.start(w_msg_hbm, w_msg_ref),
        copies.start(w_self_hbm, w_self_ref),
        copies.start(d_out_hbm, d_out_ref),
    ]
    fourth = [
        copies.start(dst_hot_hbm, dst_hot_ref),
        copies.start(src_row_hot_hbm, src_row_hot_ref),
        copies.start(own_hot_t_hbm, own_hot_t_ref),
    ]
    wait_all(first)
    rel = e0[...].astype(F32) + e1[...].astype(F32) + e2[...].astype(F32) + e3[...].astype(F32)
    for j in range(16):
        rel_ref[j] = rel[j : j + 1]
    total = arrived_ref[0:64, :].astype(F32)
    for i in range(1, 4):
        total = total + arrived_ref[i * 64 : (i + 1) * 64, :].astype(F32)
    table = total.astype(BF)
    ext_ref[...] = (base_ref[...].astype(F32) + dot(row_hot_ref[...], table)).astype(BF)
    nodes_ref[...] = ext_ref[0:256, :]
    sent_out = [copies.start(nodes_ref, nodes_hbm)]

    for n in range(4):
        cols = slice(n * 256, (n + 1) * 256)

        @pl.loop(0, 4)
        def _(k):
            rows = pl.ds(pl.multiple_of(k * 512, 512), 512)
            taken = dot(src_hot_ref[rows, :], ext_ref[:, cols])
            sources_ref[rows, cols] = taken.astype(BF)
            for i in range(4):
                few = pl.ds(pl.multiple_of(k * 512 + i * 128, 128), 128)
                edges_ref[few, cols] = (taken[i * 128 : (i + 1) * 128] * rel_ref[k * 4 + i, :, cols]).astype(BF)

    wait_all(second)

    @pl.loop(0, 4)
    def _(n):
        cols = pl.ds(pl.multiple_of(n * 256, 256), 256)
        aggregate_ref[:, cols] = (scale * dot(dst_hot_t_ref[...], edges_ref[:, cols])).astype(BF)

    sent_out.append(copies.start(aggregate_ref, aggregate_hbm))
    wait_all(third)

    @pl.loop(0, 4)
    def _(n):
        cols = pl.ds(pl.multiple_of(n * 256, 256), 256)
        out_pre = dot(aggregate_ref[...], w_msg_ref[:, cols]) + dot(nodes_ref[...], w_self_ref[:, cols])
        squashed = jnp.tanh(out_pre)
        graph_out_ref[:, cols] = squashed.astype(BF)
        pre_ref[:, cols] = (d_out_ref[:, cols].astype(F32) * (1.0 - squashed * squashed)).astype(BF)

    sent_out.append(copies.start(graph_out_ref, graph_out_hbm))
    sent_out.append(copies.start(pre_ref, pre_hbm))

    @pl.loop(0, 4)
    def _(n):
        cols = pl.ds(pl.multiple_of(n * 256, 256), 256)
        agg_grad_ref[:, cols] = (scale * dot_bt(pre_ref[...], w_msg_ref[cols, :])).astype(BF)

    wait_all(fourth)

    for n in range(4):
        cols = slice(n * 256, (n + 1) * 256)

        @pl.loop(0, 4)
        def _(k):
            rows = pl.ds(pl.multiple_of(k * 512, 512), 512)
            at_dest = dot(dst_hot_ref[rows, :], agg_grad_ref[:, cols])
            for i in range(4):
                few = pl.ds(pl.multiple_of(k * 512 + i * 128, 128), 128)
                part = at_dest[i * 128 : (i + 1) * 128]
                edges_ref[few, cols] = (part * rel_ref[k * 4 + i, :, cols]).astype(BF)
                product = part * sources_ref[few, cols].astype(F32)
                sums_ref[k * 4 + i, :, cols] = jnp.sum(product, axis=0, keepdims=True)

    blocks_ref[...] = jnp.concatenate([sums_ref[j] for j in range(16)], axis=0).astype(BF)
    sent_out.append(copies.start(blocks_ref, blocks_hbm))
    own_pre = dot(own_hot_t_ref[...], pre_ref[0:16, :]).astype(BF)

    @pl.loop(0, 4)
    def _(n):
        cols = pl.ds(pl.multiple_of(n * 256, 256), 256)
        grad = dot(src_row_hot_ref[...], edges_ref[:, cols]) + dot_bt(own_pre, w_self_ref[cols, :])
        table_out_ref[:, cols] = grad.astype(BF)

    sent_out.append(copies.start(table_out_ref, table_out_hbm))
    wait_all(sent_out)


def weight_kernel(
    copies,
    where_ref,
    aggregate_hbm, nodes_hbm, pre_hbm,
    kept_hbm, given_hbm,
    aggregate_ref, nodes_ref, pre_ref,
    kept_ref, given_ref,
):
    core = where_ref[1]
    wait_all(
        [copies.start(aggregate_hbm, aggregate_ref), copies.start(nodes_hbm, nodes_ref), copies.start(pre_hbm, pre_ref)]
    )
    sent_out = []
    for half, chunk_ref, chunk_hbm in ((1 - core, given_ref, given_hbm), (core, kept_ref, kept_hbm)):

        @pl.loop(0, 4)
        def _(z):
            rows = pl.ds(pl.multiple_of(z * 256 + half * 128, 128), 128)
            msg = dot_t(aggregate_ref[:, rows], pre_ref[...])
            own = dot_t(nodes_ref[:, rows], pre_ref[...])
            for x in range(4):
                for y in range(4):
                    at = (x * 4 + y) * 8
                    both = jnp.concatenate([msg[at : at + 8], own[at : at + 8]], axis=0)
                    chunk_ref[x, z * 4 + y] = both.astype(BF)

        sent_out.append(copies.start(chunk_ref, chunk_hbm))
    wait_all(sent_out)


def encoder_grads(half, my_y, chunk_ref, blocks, rel_hot_ref, pooled_ref, scaled_ref, normed_t_ref, grad_ref, prepare):
    for y in range(4):
        rel = dot(rel_hot_ref[pl.ds(pl.multiple_of(y * 128 + half * 64, 64), 64), :], blocks).astype(BF)
        for z in range(4):
            chunk_ref[z, y, 64:80, :] = rel[z * 16 : (z + 1) * 16]

    prepare(None)

    @pl.loop(0, 4)
    def _(t):
        cols = pl.ds(pl.multiple_of(t * 256, 256), 256)
        origin = jnp.where(t == 0, 0, jnp.where(t == 1, 3, t - 1))
        owner = lax.rem(my_y + origin, 4)
        prepare(cols)
        units = pl.ds(pl.multiple_of(t * 256 + half * 128, 128), 128)
        out = dot_t(pooled_ref[:, units], scaled_ref[...]).astype(BF)
        inner = dot(normed_t_ref[pl.ds(pl.multiple_of(half * 512, 512), 512), :], grad_ref[:, cols]).astype(BF)
        for z in range(4):
            chunk_ref[z, owner, 32:64, :] = out[z * 32 : (z + 1) * 32]
            for i in range(4):
                piece = inner[z * 128 + i * 32 : z * 128 + (i + 1) * 32]
                chunk_ref[z, owner, 0:32, i * 256 : (i + 1) * 256] = piece


def back_kernel(
    copies,
    where_ref,
    returned_hbm, route_hbm, length_hbm, all_out_hbm, slope_hbm, pooled_hbm, normed_t_hbm,
    rel_hot_hbm, r0_hbm, r1_hbm, r2_hbm, r3_hbm,
    given_hbm, scaled_hbm, grad_hbm,
    returned_ref, route_ref, length_ref, all_out_ref, slope_ref, pooled_ref, normed_t_ref,
    rel_hot_ref, r0, r1, r2, r3,
    given_ref, scaled_ref, grad_ref,
):
    core, my_y = where_ref[1], where_ref[3]
    first = [
        copies.start(returned_hbm, returned_ref),
        copies.start(route_hbm, route_ref),
        copies.start(length_hbm, length_ref),
        copies.start(rel_hot_hbm, rel_hot_ref),
        copies.start(r0_hbm, r0),
        copies.start(r1_hbm, r1),
        copies.start(r2_hbm, r2),
        copies.start(r3_hbm, r3),
    ]
    second = [
        copies.start(all_out_hbm, all_out_ref),
        copies.start(slope_hbm, slope_ref),
        copies.start(pooled_hbm, pooled_ref),
        copies.start(normed_t_hbm, normed_t_ref),
    ]
    wait_all(first)
    scaled_ref[...] = (dot(route_ref[...], returned_ref[...]) * length_ref[:, 0:1]).astype(BF)
    blocks = jnp.concatenate([r0[...], r1[...], r2[...], r3[...]], axis=0)

    def prepare(cols):
        if cols is None:
            wait_all(second)
            return
        upstream = dot_bt(scaled_ref[...], all_out_ref[cols, :]).astype(BF)
        for s in range(4):
            rows = slice(s * 256, (s + 1) * 256)
            line = lanes((16, 256))
            length = 1.0 / length_ref[s * 16 : (s + 1) * 16, 0:1]
            inside = (line // 16 == sublanes((16, 256))) & ((line % 16).astype(F32) + 0.5 < length)
            pool = inside.astype(F32).astype(BF)
            at_tokens = dot_t(pool, upstream[s * 16 : (s + 1) * 16])
            grad_ref[rows, cols] = (slope_ref[rows, cols].astype(F32) * at_tokens).astype(BF)

    encoder_grads(
        1 - core, my_y, given_ref, blocks, rel_hot_ref, pooled_ref, scaled_ref, normed_t_ref, grad_ref, prepare
    )
    wait_all(
        [copies.start(given_ref, given_hbm), copies.start(scaled_ref, scaled_hbm), copies.start(grad_ref, grad_hbm)]
    )


def rest_kernel(
    copies,
    where_ref,
    scaled_hbm, grad_hbm, pooled_hbm, normed_t_hbm, rel_hot_hbm, r0_hbm, r1_hbm, r2_hbm, r3_hbm,
    kept_hbm,
    scaled_ref, grad_ref, pooled_ref, normed_t_ref, rel_hot_ref, r0, r1, r2, r3,
    kept_ref,
):
    core, my_y = where_ref[1], where_ref[3]
    first = [
        copies.start(rel_hot_hbm, rel_hot_ref),
        copies.start(r0_hbm, r0),
        copies.start(r1_hbm, r1),
        copies.start(r2_hbm, r2),
        copies.start(r3_hbm, r3),
    ]
    second = [
        copies.start(grad_hbm, grad_ref),
        copies.start(normed_t_hbm, normed_t_ref),
        copies.start(pooled_hbm, pooled_ref),
        copies.start(scaled_hbm, scaled_ref),
    ]
    wait_all(first)
    blocks = jnp.concatenate([r0[...], r1[...], r2[...], r3[...]], axis=0)

    def prepare(cols):
        if cols is None:
            wait_all(second)

    encoder_grads(
        core, my_y, kept_ref, blocks, rel_hot_ref, pooled_ref, scaled_ref, normed_t_ref, grad_ref, prepare
    )
    wait_all([copies.start(kept_ref, kept_hbm)])


def place_kernel(
    copies,
    where_ref,
    h0, h1, h2, h3, h4, h5, h6, h7,
    in_hbm, out_hbm, rel_hbm,
    a0, a1, a2, a3, c0, c1, c2, c3,
    in_ref, out_ref, rel_ref,
):
    sources = (h0, h1, h2, h3, h4, h5, h6, h7)
    targets = (a0, a1, a2, a3, c0, c1, c2, c3)
    wait_all([copies.start(source, target) for source, target in zip(sources, targets)])
    my_z, core = where_ref[0], where_ref[1]
    for pieces, half in (((a0, a1, a2, a3), core), ((c0, c1, c2, c3), 1 - core)):
        for piece, origin in zip(pieces, ORIGINS):
            z = lax.rem(my_z + origin, 4)
            values = piece[...].astype(F32)
            for i in range(4):
                rows = pl.ds(pl.multiple_of(half * 512 + z * 128 + i * 32, 32), 32)
                in_ref[rows, :] = values[0:32, i * 256 : (i + 1) * 256]
            out_ref[pl.ds(pl.multiple_of(half * 128 + z * 32, 32), 32), :] = values[32:64]
            rel_ref[pl.ds(pl.multiple_of(half * 32 + z * 8, 8), 8), :] = values[64:72]
    wait_all([copies.start(in_ref, in_hbm), copies.start(out_ref, out_hbm), copies.start(rel_ref, rel_hbm)])


def shards(
    hidden,
    desc_len,
    w_in,
    w_out,
    send_order,
    place_order,
    cache,
    halo_rows,
    edge_src,
    edge_dst,
    edge_rel,
    rel_table,
    w_msg,
    w_self,
    d_out,
):
    entities, length, width = hidden.shape
    tokens = entities * length
    units = w_in.shape[1]
    my_core = lax.axis_index("core")
    where = jnp.stack([lax.axis_index(name) for name in ("z", "core", "x", "y")]).astype(I32)
    src, dst, rel = edge_src[0], edge_dst[0], edge_rel[0]
    shard_rows = rel_table.shape[0]

    meta = row_of(jnp.concatenate([desc_len, send_order[0], rel // 32, rel % 32]), width)
    rel_pad = jnp.pad(rel_table.reshape(2, shard_rows // 2, width), ((0, 0), (0, 32 - shard_rows // 2), (0, 0)))
    rel_pad = rel_pad.reshape(64, width)
    operands = [hidden.reshape(tokens, width), jnp.broadcast_to(meta, (16, width)), w_in, w_out, rel_pad]
    outs = [((tokens + 16, width), BF), ((entities, width), F32)]
    block, hidden_sum, weights = local_call(
        norm_kernel,
        [*outs, ((576, 512), BF)],
        [where, *operands],
        like(operands[:2]) + filled(outs),
        copies=10,
    )
    blocks = [block, *gather_ring(block, "x", 128)]
    mine = gather_ring(weights, "y", 256)
    other = [shift_by(part, "core", 1) for part in mine]

    outs = [
        ((256, width), BF),
        ((4 * tokens, width), BF),
        ((4 * tokens, 4 * units), BF),
        ((4 * entities, 4 * units), BF),
        ((4 * units, width), BF),
        ((4 * entities, 256), BF),
        ((4 * entities, 128), F32),
        ((512, 64), BF),
    ] + [((entities, width), BF)] * 4
    outgoing, normed, slope, pooled, all_out, route, inverse, rel_hot, *asked = local_call(
        encode_kernel,
        outs,
        [where, *blocks, w_in, w_out, rel_pad, *mine, *other, hidden_sum],
        filled(outs)
        + [
            pltpu.VMEM((width, 4 * units), BF),
            pltpu.VMEM((4 * entities, tokens), BF),
            pltpu.VMEM((256, width), BF),
            pltpu.VMEM((4, 16, 128), BF),
            pltpu.VMEM((entities, width), F32),
        ],
        copies=64,
        flops=2 * 4 * tokens * width * 4 * units,
    )

    halo = halo_rows[0]
    place = place_order[0]
    side = halo.shape[0] // 2
    cache_count = cache.shape[0]
    boundary = dot(one_hot(halo - entities, cache_count), cache).astype(BF)
    halo_hot = halo[:, None] == jnp.arange(entities, dtype=I32)[None, :]
    halo_place = jnp.where(halo < entities, jnp.sum(jnp.where(halo_hot, place[None, :], 0), axis=1), 16)

    def edge_of(rows, places):
        return jnp.concatenate([rows, jnp.pad(row_of(places, width), ((0, 15), (0, 0)))], axis=0)

    to_high, to_low = edge_of(boundary[side:], halo_place[side:]), edge_of(boundary[:side], halo_place[:side])
    to_high, to_low, outgoing = lax.optimization_barrier((to_high, to_low, outgoing))
    from_low = shift_by(to_high, GROUP, 1)
    from_high = shift_by(to_low, GROUP, 15)
    low_place = from_low[side, :side].astype(I32)
    high_place = from_high[side, :side].astype(I32)
    own_row = fresh_row(0, place)
    low_row = jnp.where(low_place < 16, fresh_row(-1, low_place), -1)
    high_row = jnp.where(high_place < 16, fresh_row(1, high_place), -1)
    table_row = jnp.concatenate([own_row, jnp.full((cache_count,), -1, I32), low_row, high_row])
    row_hot = one_hot(table_row, 64)
    base = jnp.concatenate([jnp.zeros((entities, width), BF), cache, from_low[:side], from_high[:side]], axis=0)
    node_count = entities + cache_count
    extended_count = node_count + 2 * side
    edge_count = src.shape[0]
    block_count = rel.shape[0]
    src_hot = one_hot(src, extended_count)
    src_row_hot = dot_bt(one_hot_t(table_row, 64), src_hot).astype(BF)

    arrived = lax.all_to_all(outgoing.reshape(16, 16, width), GROUP, 0, 0, tiled=True).reshape(256, width)
    rel_rows = [asked[0]] + [shift_by(rows, "x", o) for rows, o in zip(asked[1:], ORIGINS[1:])]
    normed_t = normed.T

    outs = [((64, width), BF), ((block_count, width), BF)] + [((node_count, width), BF)] * 4
    operands = [
        arrived,
        base,
        row_hot,
        one_hot_t(own_row, 64),
        *rel_rows,
        src_hot,
        one_hot(dst, node_count),
        one_hot_t(dst, node_count),
        src_row_hot,
        w_msg,
        w_self,
        d_out,
    ]
    grad_table, grad_blocks, graph_out, aggregate, nodes, grad_pre = local_call(
        graph_kernel,
        outs,
        [where, *operands],
        like(operands)
        + filled(outs)
        + [
            pltpu.VMEM((extended_count, width), BF),
            pltpu.VMEM((edge_count, width), BF),
            pltpu.VMEM((edge_count, width), BF),
            pltpu.VMEM((node_count, width), BF),
            pltpu.VMEM((block_count, 1, width), F32),
            pltpu.VMEM((block_count, 1, width), F32),
        ],
        copies=24,
        flops=6 * 10**9,
    )

    back = jnp.broadcast_to(grad_table.reshape(1, 4, 16, width), (4, 4, 16, width))
    returned = lax.all_to_all(back.reshape(16, 16, width), GROUP, 0, 0, tiled=True).reshape(256, width)
    rel_blocks = [grad_blocks] + [shift_by(grad_blocks, "x", s) for s in SHIFTS]

    outs = [((4, 16, 16, width), BF)] * 2
    operands = [aggregate, nodes, grad_pre]
    graph_kept, graph_given = local_call(
        weight_kernel, outs, [where, *operands], like(operands) + filled(outs), flops=10**9
    )
    chip = (graph_kept.astype(F32) + shift_by(graph_given, "core", 1).astype(F32)).astype(BF)
    chip, *rel_blocks = lax.optimization_barrier((chip, *rel_blocks))
    line = lax.all_to_all(chip, "x", 0, 0, tiled=True)

    outs = [((4, 4, 80, width), BF), ((4 * entities, width), BF), ((4 * tokens, 4 * units), BF)]
    operands = [returned, route, inverse, all_out, slope, pooled, normed_t, rel_hot, *rel_blocks]
    given, scaled, grad_tokens = local_call(
        back_kernel,
        outs,
        [where, *operands],
        like(operands) + filled(outs),
        copies=16,
        flops=3 * 2 * tokens * width * 4 * units,
    )
    outs = [((4, 4, 80, width), BF)]
    operands = [scaled, grad_tokens, pooled, normed_t, rel_hot, *rel_blocks]
    (kept,) = local_call(
        rest_kernel,
        outs,
        [where, *operands],
        like(operands) + filled(outs),
        copies=12,
        flops=2 * 2 * tokens * width * 4 * units,
    )
    line_sum = jnp.sum(line.astype(F32), axis=0).astype(BF)
    chunks = (kept.astype(F32) + shift_by(given, "core", 1).astype(F32)).astype(BF)
    chunks = jnp.concatenate([chunks.reshape(16, 80, width), line_sum], axis=1)
    chunks = lax.all_to_all(chunks, ("z", "y"), 0, 0, tiled=True)
    summed = jnp.sum(chunks.astype(F32), axis=0)
    grad_msg, grad_self = summed[80:88], summed[88:96]
    part = summed[:80].astype(BF)
    parts = [part] + [shift_by(part, "z", s) for s in SHIFTS]
    others = [shift_by(piece, "core", 1) for piece in parts]
    outs = [((width, units), F32), ((units, width), F32), ((64, width), F32)]
    operands = [*parts, *others]
    grad_w_in, grad_w_out, grad_rel = local_call(
        place_kernel, outs, [where, *operands], like(operands) + filled(outs), copies=12
    )
    return (graph_out, grad_w_in, grad_w_out, grad_rel[:shard_rows], grad_msg, grad_self)


def solution(mesh):
    fine = Mesh(mesh.devices.reshape(4, 2, 4, 4), ("z", "core", "x", "y"))
    every = ("z", "core", "x", "y")
    placed = (
        P(every, None, None),
        P(every),
        P(None, GROUP),
        P(GROUP, None),
        P(every, None),
        P(every, None),
        P(every, None),
        P(every, None),
        P(every, None),
        P(every, None),
        P(every, None),
        P(GROUP, None),
        P(),
        P(),
        P(every, None),
    )
    return jax.shard_map(
        shards,
        mesh=fine,
        in_specs=placed,
        out_specs=(
            P(every, None),
            P(None, GROUP),
            P(GROUP, None),
            P(GROUP, None),
            P(every, None),
            P(every, None),
        ),
        check_vma=False,
    )
```

```python
import jax
import jax.numpy as jnp
import numpy as np
from jax import lax
from jax.experimental import pallas as pl
from jax.experimental.pallas import tpu as pltpu
from jax.sharding import Mesh
from jax.sharding import PartitionSpec as P

BF = jnp.bfloat16
F32 = jnp.float32
I32 = jnp.int32
GROUP = ("x", "y")
SHIFTS = (1, 3, 2)
ORIGINS = (0, 3, 1, 2)
GELU_SCALE = float(np.sqrt(2.0 / np.pi))
GELU_CUBE = 0.044715


def shift_by(value, axis, shift):
    count = lax.axis_size(axis)
    return lax.ppermute(value, axis, [(i, (i + shift) % count) for i in range(count)])


def dot(a, b):
    return jnp.dot(a, b, preferred_element_type=F32)


def dot_t(a, b):
    return lax.dot_general(a, b, (((0,), (0,)), ((), ())), preferred_element_type=F32)


def dot_bt(a, b):
    return lax.dot_general(a, b, (((1,), (1,)), ((), ())), preferred_element_type=F32)


def one_hot(index, count):
    return (index[:, None] == jnp.arange(count, dtype=I32)[None, :]).astype(BF)


def one_hot_t(index, count):
    return (index[None, :] == jnp.arange(count, dtype=I32)[:, None]).astype(BF)


def lanes(shape):
    return lax.broadcasted_iota(I32, shape, 1)


def sublanes(shape):
    return lax.broadcasted_iota(I32, shape, 0)


def row_of(values, width):
    return jnp.pad(values.astype(BF), (0, width - values.shape[0]))[None, :]


def gather_ring(value, axis, cut):
    low, high = shift_by(value, axis, 1), shift_by(value, axis, 3)
    return [low, high, shift_by(low[:cut], axis, 1), shift_by(high[cut:], axis, 3)]


def reduce_ring(chunks, axis):
    total = chunks[0].astype(F32)
    for chunk, origin in zip(chunks[1:], ORIGINS[1:]):
        total = total + shift_by(chunk, axis, origin).astype(F32)
    return total.astype(BF)


def fresh_row(side, place):
    return (place % 4) * 16 + (side + 1) * 4 + place // 4


class Copies:
    def __init__(self, sems):
        self.sems, self.used = sems, 0

    def start(self, source, target):
        copy = pltpu.make_async_copy(source, target, self.sems.at[self.used])
        self.used += 1
        copy.start()
        return copy


def local_call(body, outs, operands, scratch=(), copies=8, flops=0, limit=60):
    def kernel(*refs):
        body(Copies(refs[-1]), *refs[:-1])

    return pl.pallas_call(
        kernel,
        out_shape=[jax.ShapeDtypeStruct(shape, kind) for shape, kind in outs],
        in_specs=[pl.BlockSpec(memory_space=pltpu.SMEM)]
        + [pl.BlockSpec(memory_space=pltpu.HBM)] * (len(operands) - 1),
        out_specs=[pl.BlockSpec(memory_space=pltpu.HBM)] * len(outs),
        scratch_shapes=[*scratch, pltpu.SemaphoreType.DMA((copies,))],
        compiler_params=pltpu.CompilerParams(vmem_limit_bytes=limit * 1024 * 1024),
        cost_estimate=pl.CostEstimate(flops=flops, bytes_accessed=1024 * 1024, transcendentals=0),
    )(*operands)


def like(arrays):
    return [pltpu.VMEM(array.shape, array.dtype) for array in arrays]


def filled(outs):
    return [pltpu.VMEM(shape, kind) for shape, kind in outs]


def wait_all(copies):
    for copy in copies:
        copy.wait()


def length_column(meta):
    shape = meta.shape
    return jnp.sum(jnp.where(lanes(shape) == sublanes(shape), meta, 0.0), axis=1, keepdims=True)


def pool_rows(length, tokens):
    shape = (16, tokens)
    line = lanes(shape)
    inside = (line // 16 == sublanes(shape)) & ((line % 16).astype(F32) < length)
    return inside.astype(F32).astype(BF)


def norm_kernel(
    copies,
    where_ref,
    hidden_hbm, lens_hbm, order_hbm, rel_hbm, in_hbm, out_hbm, table_hbm,
    block_hbm, sum_hbm, weights_hbm,
    hidden_ref, lens_ref, order_ref, rel_ref,
    block_ref, sum_ref, weights_ref,
):
    core = where_ref[1]
    packed = []
    for i in range(2):
        cols, wide = pl.ds(i * 256, 256), pl.ds(i * 512, 512)
        source = in_hbm.at[pl.ds(pl.multiple_of(core * 512 + i * 256, 256), 256), :]
        packed.append(copies.start(source, weights_ref.at[pl.ds(0, 256), cols]))
        source = out_hbm.at[pl.ds(pl.multiple_of(core * 128, 128), 128), wide]
        packed.append(copies.start(source, weights_ref.at[pl.ds(256 + i * 128, 128), :]))
        source = table_hbm.at[pl.ds(pl.multiple_of(core * 32, 32), 32), wide]
        packed.append(copies.start(source, weights_ref.at[pl.ds(512 + i * 32, 32), :]))
    first = [
        copies.start(hidden_hbm, hidden_ref),
        copies.start(lens_hbm, lens_ref),
        copies.start(order_hbm, order_ref),
        copies.start(rel_hbm, rel_ref),
    ]
    wait_all(packed)
    later = [copies.start(weights_ref, weights_hbm)]
    wait_all(first)
    meta = jnp.zeros((16, 128), F32)
    high = rel_ref[...] // 32
    for i, row in enumerate((lens_ref[...], order_ref[...], high, rel_ref[...] - 32 * high)):
        values = jnp.broadcast_to(row.astype(F32), (16, 16)).astype(BF)
        select = (lanes((16, 128)) == sublanes((16, 128)) + 16 * i).astype(F32).astype(BF)
        meta = meta + dot(values, select)
    values = hidden_ref[...].astype(F32)
    center = values - jnp.mean(values, axis=-1, keepdims=True)
    spread = jnp.mean(center * center, axis=-1, keepdims=True)
    tokens = values.shape[0]
    block_ref[0:tokens, :] = (center * lax.rsqrt(spread + 1e-05)).astype(BF)
    block_ref[tokens : tokens + 16, :] = jnp.zeros((16, values.shape[1]), BF)
    block_ref[tokens : tokens + 16, 0:128] = meta.astype(BF)
    later.append(copies.start(block_ref, block_hbm))
    sum_ref[...] = dot(pool_rows(length_column(meta), tokens), hidden_ref[...])
    later.append(copies.start(sum_ref, sum_hbm))
    wait_all(later)


def encode_kernel(
    copies,
    where_ref,
    b0, b1, b2, b3_top, b3_rest,
    own_in, own_out, own_rel,
    m1, m2, m3_in, m3_rest,
    o1, o2, o3_in, o3_rest,
    hidden_sum_hbm,
    outgoing_hbm, normed_hbm, slope_hbm, pooled_hbm, all_out_hbm, route_hbm, length_hbm, rel_hot_hbm,
    rel0_hbm, rel1_hbm, rel2_hbm, rel3_hbm,
    outgoing_ref, normed_ref, slope_ref, pooled_ref, all_out_ref, route_ref, length_ref, rel_hot_ref,
    rel0_ref, rel1_ref, rel2_ref, rel3_ref,
    in_ref, pool_ref, rel_ref, meta_ref, hidden_sum_ref,
):
    core, my_x, my_y = where_ref[1], where_ref[2], where_ref[3]
    metas, tokens, weights, tables = [], [], [[], [], [], []], []
    for s, (block, row) in enumerate(((b0, 256), (b1, 256), (b2, 256), (b3_rest, 128))):
        metas.append(copies.start(block.at[pl.ds(row, 16), pl.ds(0, 128)], meta_ref.at[s]))
    tables.append(copies.start(own_rel, rel_ref.at[pl.ds(0, 64), :]))
    pieces = []
    for t, (mine, other) in enumerate(
        (((m1, m1, 256), (o1, o1, 256)), ((m2, m2, 256), (o2, o2, 256)), ((m3_in, m3_rest, 0), (o3_in, o3_rest, 0))), 1
    ):
        for (inner, rest, at), half in ((mine, core), (other, 1 - core)):
            pieces.append((t, inner, rest, at, half))
            for i in range(2):
                rows = pl.ds(pl.multiple_of(t * 64 + half * 32, 32), 32)
                target = rel_ref.at[rows, pl.ds(i * 512, 512)]
                tables.append(copies.start(rest.at[pl.ds(at + 256 + i * 32, 32), :], target))
    for s, (block, row, count) in enumerate(((b0, 0, 256), (b1, 256, 256), (b2, 512, 256), (b3_top, 768, 128), (b3_rest, 896, 128))):
        tokens.append(copies.start(block.at[pl.ds(0, count), :], normed_ref.at[pl.ds(row, count), :]))
    weights[0].append(copies.start(own_in, in_ref.at[:, pl.ds(0, 256)]))
    for t, inner, rest, at, half in pieces:
        for i in range(2):
            rows = pl.ds(pl.multiple_of(half * 512 + i * 256, 256), 256)
            target = in_ref.at[rows, pl.ds(t * 256, 256)]
            weights[t].append(copies.start(inner.at[pl.ds(0, 256), pl.ds(i * 256, 256)], target))
    outer = [
        copies.start(own_out, all_out_ref.at[pl.ds(0, 256), :]),
        copies.start(hidden_sum_hbm, hidden_sum_ref),
    ]
    for t, inner, rest, at, half in pieces:
        for i in range(2):
            rows = pl.ds(pl.multiple_of(t * 256 + half * 128, 128), 128)
            target = all_out_ref.at[rows, pl.ds(i * 512, 512)]
            outer.append(copies.start(rest.at[pl.ds(at + i * 128, 128), :], target))
    wait_all(metas)
    wait_all(tables)

    wide = (16, 256)
    slot = lanes(wide) % 16
    bound = lanes((128, 256))
    bound = (bound // 16 + (bound % 16) // 4 + 15) % 16
    bound_hot = (sublanes((128, 256)) == bound + 16).astype(F32).astype(BF)
    ids = jnp.zeros((16, 64), F32)
    asked = (rel0_ref, rel1_ref, rel2_ref, rel3_ref)
    for s in range(4):
        meta = meta_ref[s]
        values = meta.astype(F32)
        apart = lanes(meta.shape) - sublanes(meta.shape)
        wanted = jnp.where(apart == 32, 32.0 * values, jnp.where(apart == 48, values, 0.0))
        wanted = jnp.sum(wanted, axis=1, keepdims=True)
        line = lanes(wide)
        owner_y = (my_y + jnp.where(line < 64, 0, jnp.where(line < 128, 3, line // 64 - 1))) % 4
        name = (my_x * 4 + owner_y) * 52 + line % 64
        pick = (name.astype(F32) == wanted) & (line % 64 < 52)
        asked[s][...] = dot(pick.astype(F32).astype(BF), rel_ref[...]).astype(BF)
        length = length_column(values)
        length_ref[s * 16 : (s + 1) * 16, :] = jnp.broadcast_to(1.0 / length, (16, 128))
        pool_ref[s * 16 : (s + 1) * 16, :] = pool_rows(length, 256)
        sent = dot(meta, bound_hot)
        encoder = lax.rem(my_x + ORIGINS[s], 4)
        chosen = (sent == sublanes(wide).astype(F32)) & (slot % 4 == encoder) & (slot < 12)
        route_ref[s * 16 : (s + 1) * 16, :] = chosen.astype(F32).astype(BF)
        at, to = sublanes((128, 64)), lanes((128, 64)) - s * 16
        inside = (to >= 0) & (to < 16)
        select = jnp.where(inside & (at == 32 + to), 32.0, jnp.where(inside & (at == 48 + to), 1.0, 0.0))
        ids = ids + dot(meta, select.astype(BF))
    line = sublanes((512, 64))
    local = (line // 64) % 2 * 32 + (line // 16) % 4 * 8 + line % 16
    name = (my_x * 4 + line // 128) * 52 + local
    good = (line % 16 < 8) & (local < 52)
    rel_hot_ref[...] = ((name.astype(F32) == ids[0:1, :]) & good).astype(F32).astype(BF)

    sent_out = [
        copies.start(rel0_ref, rel0_hbm),
        copies.start(rel1_ref, rel1_hbm),
        copies.start(rel2_ref, rel2_hbm),
        copies.start(rel3_ref, rel3_hbm),
        copies.start(route_ref, route_hbm),
        copies.start(length_ref, length_hbm),
        copies.start(rel_hot_ref, rel_hot_hbm),
    ]
    wait_all(tokens)
    sent_out.append(copies.start(normed_ref, normed_hbm))
    for t in range(4):
        cols = slice(t * 256, (t + 1) * 256)
        wait_all(weights[t])

        @pl.loop(0, 2)
        def _(s):
            rows = pl.ds(pl.multiple_of(s * 512, 512), 512)
            pre = dot(normed_ref[rows, :], in_ref[:, cols])
            square = pre * pre
            tanh = jnp.tanh(GELU_SCALE * pre * (1.0 + GELU_CUBE * square))
            upper = 0.5 + 0.5 * tanh
            slope = upper + (0.5 * GELU_SCALE) * pre * (1.0 - tanh * tanh) * (1.0 + 3.0 * GELU_CUBE * square)
            slope_ref[rows, cols] = slope.astype(BF)
            activation = (pre * upper).astype(BF)
            for i in range(2):
                few = pl.ds(pl.multiple_of(s * 32 + i * 16, 16), 16)
                pooled = dot(pool_ref[few, :], activation[i * 256 : (i + 1) * 256])
                pooled_ref[few, cols] = pooled.astype(BF)

    sent_out.append(copies.start(slope_ref, slope_hbm))
    sent_out.append(copies.start(pooled_ref, pooled_hbm))
    wait_all(outer)
    sent_out.append(copies.start(all_out_ref, all_out_hbm))
    partial = dot(pooled_ref[...], all_out_ref[...])
    partial = jnp.concatenate([partial[0:16] + hidden_sum_ref[...], partial[16:64]], axis=0)
    partial = (partial * length_ref[:, 0:1]).astype(BF)
    outgoing_ref[...] = dot_t(route_ref[...], partial).astype(BF)
    sent_out.append(copies.start(outgoing_ref, outgoing_hbm))
    wait_all(sent_out)


def graph_kernel(
    copies,
    where_ref,
    arrived_hbm, own_hot_t_hbm, e0_hbm, e1_hbm, e2_hbm, e3_hbm,
    src_hot_hbm, dst_hot_hbm, dst_hot_t_hbm,
    w_msg_hbm, w_self_hbm, d_out_hbm,
    cache_hbm, low_hbm, high_hbm,
    table_out_hbm, blocks_hbm, graph_out_hbm, aggregate_hbm, nodes_hbm, pre_hbm,
    arrived_ref, own_hot_t_ref, e0, e1, e2, e3,
    src_hot_ref, dst_hot_ref, dst_hot_t_ref,
    w_msg_ref, w_self_ref, d_out_ref,
    table_out_ref, blocks_ref, graph_out_ref, aggregate_ref, nodes_ref, pre_ref,
    base_ref, places_ref, row_hot_t_ref, src_row_hot_ref,
    ext_ref, sources_ref, edges_ref, agg_grad_ref, sums_ref, rel_ref,
):
    scale = (256 / 2048) ** 0.5
    first = [
        copies.start(low_hbm.at[pl.ds(64, 16), pl.ds(0, 128)], places_ref.at[0]),
        copies.start(high_hbm.at[pl.ds(64, 16), pl.ds(0, 128)], places_ref.at[1]),
        copies.start(own_hot_t_hbm, own_hot_t_ref),
        copies.start(arrived_hbm, arrived_ref),
        copies.start(cache_hbm, base_ref.at[pl.ds(16, 240), :]),
        copies.start(low_hbm.at[pl.ds(0, 64), :], base_ref.at[pl.ds(256, 64), :]),
        copies.start(high_hbm.at[pl.ds(0, 64), :], base_ref.at[pl.ds(320, 64), :]),
        copies.start(e0_hbm, e0),
        copies.start(e1_hbm, e1),
        copies.start(e2_hbm, e2),
        copies.start(e3_hbm, e3),
        copies.start(src_hot_hbm, src_hot_ref),
    ]
    second = [copies.start(dst_hot_t_hbm, dst_hot_t_ref)]
    third = [
        copies.start(w_msg_hbm, w_msg_ref),
        copies.start(w_self_hbm, w_self_ref),
        copies.start(d_out_hbm, d_out_ref),
    ]
    fourth = [copies.start(dst_hot_hbm, dst_hot_ref)]
    base_ref[0:16, :] = jnp.zeros((16, 1024), BF)
    wait_all(first)
    rel = e0[...].astype(F32) + e1[...].astype(F32) + e2[...].astype(F32) + e3[...].astype(F32)
    for j in range(16):
        rel_ref[j] = rel[j : j + 1]

    to = lanes((128, 128)) - sublanes((128, 128))
    inside = sublanes((128, 128)) < 64
    low_move = ((to == 0) & inside).astype(F32).astype(BF)
    high_move = ((to == 64) & inside).astype(F32).astype(BF)
    places = (dot(places_ref[0], low_move) + dot(places_ref[1], high_move))[0:1].astype(I32)
    upper = (lax.broadcasted_iota(I32, (1, 128), 1) >= 64).astype(I32)
    table_row = jnp.where(places < 16, (places % 4) * 16 + upper * 8 + places // 4, -1)
    row_hot_t_ref[:, 0:256] = own_hot_t_ref[...]
    row_hot_t_ref[:, 256:384] = (sublanes((64, 128)) == table_row).astype(F32).astype(BF)
    src_row_hot_ref[...] = dot_bt(row_hot_t_ref[...], src_hot_ref[...]).astype(BF)
    total = arrived_ref[0:64, :].astype(F32)
    for i in range(1, 4):
        total = total + arrived_ref[i * 64 : (i + 1) * 64, :].astype(F32)
    table = total.astype(BF)
    ext_ref[...] = (base_ref[...].astype(F32) + dot_t(row_hot_t_ref[...], table)).astype(BF)
    nodes_ref[...] = ext_ref[0:256, :]
    sent_out = [copies.start(nodes_ref, nodes_hbm)]

    for n in range(4):
        cols = slice(n * 256, (n + 1) * 256)

        @pl.loop(0, 4)
        def _(k):
            rows = pl.ds(pl.multiple_of(k * 512, 512), 512)
            taken = dot(src_hot_ref[rows, :], ext_ref[:, cols])
            sources_ref[rows, cols] = taken.astype(BF)
            for i in range(4):
                few = pl.ds(pl.multiple_of(k * 512 + i * 128, 128), 128)
                edges_ref[few, cols] = (taken[i * 128 : (i + 1) * 128] * rel_ref[k * 4 + i, :, cols]).astype(BF)

    wait_all(second)

    @pl.loop(0, 4)
    def _(n):
        cols = pl.ds(pl.multiple_of(n * 256, 256), 256)
        aggregate_ref[:, cols] = (scale * dot(dst_hot_t_ref[...], edges_ref[:, cols])).astype(BF)

    sent_out.append(copies.start(aggregate_ref, aggregate_hbm))
    wait_all(third)

    @pl.loop(0, 4)
    def _(n):
        cols = pl.ds(pl.multiple_of(n * 256, 256), 256)
        out_pre = dot(aggregate_ref[...], w_msg_ref[:, cols]) + dot(nodes_ref[...], w_self_ref[:, cols])
        squashed = jnp.tanh(out_pre)
        graph_out_ref[:, cols] = squashed.astype(BF)
        pre_ref[:, cols] = (d_out_ref[:, cols].astype(F32) * (1.0 - squashed * squashed)).astype(BF)

    sent_out.append(copies.start(graph_out_ref, graph_out_hbm))
    sent_out.append(copies.start(pre_ref, pre_hbm))

    @pl.loop(0, 4)
    def _(n):
        cols = pl.ds(pl.multiple_of(n * 256, 256), 256)
        agg_grad_ref[:, cols] = (scale * dot_bt(pre_ref[...], w_msg_ref[cols, :])).astype(BF)

    wait_all(fourth)

    for n in range(4):
        cols = slice(n * 256, (n + 1) * 256)

        @pl.loop(0, 4)
        def _(k):
            rows = pl.ds(pl.multiple_of(k * 512, 512), 512)
            at_dest = dot(dst_hot_ref[rows, :], agg_grad_ref[:, cols])
            for i in range(4):
                few = pl.ds(pl.multiple_of(k * 512 + i * 128, 128), 128)
                part = at_dest[i * 128 : (i + 1) * 128]
                edges_ref[few, cols] = (part * rel_ref[k * 4 + i, :, cols]).astype(BF)
                product = part * sources_ref[few, cols].astype(F32)
                sums_ref[k * 4 + i, :, cols] = jnp.sum(product, axis=0, keepdims=True)

    blocks_ref[...] = jnp.concatenate([sums_ref[j] for j in range(16)], axis=0).astype(BF)
    sent_out.append(copies.start(blocks_ref, blocks_hbm))
    own_pre = dot(own_hot_t_ref[...], pre_ref[...]).astype(BF)

    @pl.loop(0, 4)
    def _(n):
        cols = pl.ds(pl.multiple_of(n * 256, 256), 256)
        grad = dot(src_row_hot_ref[...], edges_ref[:, cols]) + dot_bt(own_pre, w_self_ref[cols, :])
        table_out_ref[:, cols] = grad.astype(BF)

    sent_out.append(copies.start(table_out_ref, table_out_hbm))
    wait_all(sent_out)


def weight_kernel(
    copies,
    where_ref,
    aggregate_hbm, nodes_hbm, pre_hbm,
    kept_hbm, given_hbm,
    aggregate_ref, nodes_ref, pre_ref,
    kept_ref, given_ref,
):
    core = where_ref[1]
    wait_all(
        [copies.start(aggregate_hbm, aggregate_ref), copies.start(nodes_hbm, nodes_ref), copies.start(pre_hbm, pre_ref)]
    )
    sent_out = []
    for half, chunk_ref, chunk_hbm in ((1 - core, given_ref, given_hbm), (core, kept_ref, kept_hbm)):

        @pl.loop(0, 4)
        def _(z):
            rows = pl.ds(pl.multiple_of(z * 256 + half * 128, 128), 128)
            msg = dot_t(aggregate_ref[:, rows], pre_ref[...])
            own = dot_t(nodes_ref[:, rows], pre_ref[...])
            for x in range(4):
                for y in range(4):
                    at = (x * 4 + y) * 8
                    both = jnp.concatenate([msg[at : at + 8], own[at : at + 8]], axis=0)
                    chunk_ref[x, z * 4 + y] = both.astype(BF)

        sent_out.append(copies.start(chunk_ref, chunk_hbm))
    wait_all(sent_out)


def back_kernel(
    copies,
    where_ref,
    returned_hbm, route_hbm, length_hbm, all_out_hbm, slope_hbm, pooled_hbm, normed_t_hbm,
    rel_hot_hbm, r0_hbm, r1_hbm, r2_hbm, r3_hbm,
    out_kept_hbm, out_given_hbm, in_kept_hbm, in_given_hbm,
    returned_ref, route_ref, length_ref, all_out_ref, slope_ref, pooled_ref, normed_t_ref,
    rel_hot_ref, r0, r1, r2, r3,
    out_kept_ref, out_given_ref, in_kept_ref, in_given_ref,
    scaled_ref, grad_ref,
):
    my_z, core, my_y = where_ref[0], where_ref[1], where_ref[3]
    first = [
        copies.start(returned_hbm, returned_ref),
        copies.start(route_hbm, route_ref),
        copies.start(length_hbm, length_ref),
        copies.start(rel_hot_hbm, rel_hot_ref),
        copies.start(r0_hbm, r0),
        copies.start(r1_hbm, r1),
        copies.start(r2_hbm, r2),
        copies.start(r3_hbm, r3),
    ]
    second = [
        copies.start(all_out_hbm, all_out_ref),
        copies.start(pooled_hbm, pooled_ref),
        copies.start(slope_hbm, slope_ref),
        copies.start(normed_t_hbm, normed_t_ref),
    ]
    wait_all(first)
    scaled_ref[...] = (dot(route_ref[...], returned_ref[...]) * length_ref[:, 0:1]).astype(BF)
    blocks = jnp.concatenate([r0[...], r1[...], r2[...], r3[...]], axis=0)
    places = []
    for z in range(4):
        ahead = lax.rem(z - my_z + 4, 4)
        places.append(jnp.where(ahead == 0, 0, jnp.where(ahead == 3, 1, ahead + 1)))
    wait_all(second)

    @pl.loop(0, 4)
    def _(t):
        cols = pl.ds(pl.multiple_of(t * 256, 256), 256)
        origin = jnp.where(t == 0, 0, jnp.where(t == 1, 3, t - 1))
        owner = lax.rem(my_y + origin, 4)
        upstream = dot_bt(scaled_ref[...], all_out_ref[cols, :]).astype(BF)
        for s in range(4):
            rows = slice(s * 256, (s + 1) * 256)
            line = lanes((16, 256))
            length = 1.0 / length_ref[s * 16 : (s + 1) * 16, 0:1]
            inside = (line // 16 == sublanes((16, 256))) & ((line % 16).astype(F32) + 0.5 < length)
            pool = inside.astype(F32).astype(BF)
            at_tokens = dot_t(pool, upstream[s * 16 : (s + 1) * 16])
            grad_ref[rows, :] = (slope_ref[rows, cols].astype(F32) * at_tokens).astype(BF)
        for half, out_ref, in_ref in ((1 - core, out_given_ref, in_given_ref), (core, out_kept_ref, in_kept_ref)):
            units = pl.ds(pl.multiple_of(t * 256 + half * 128, 128), 128)
            out = dot_t(pooled_ref[:, units], scaled_ref[...]).astype(BF)
            rel_rows = pl.ds(pl.multiple_of(owner * 128 + half * 64, 64), 64)
            rel = dot(rel_hot_ref[rel_rows, :], blocks).astype(BF)
            inner = dot(normed_t_ref[pl.ds(pl.multiple_of(half * 512, 512), 512), :], grad_ref[...]).astype(BF)
            for z in range(4):
                out_ref[t, places[z], 0:32, :] = out[z * 32 : (z + 1) * 32]
                out_ref[t, places[z], 32:48, :] = rel[z * 16 : (z + 1) * 16]
                for i in range(4):
                    piece = inner[z * 128 + i * 32 : z * 128 + (i + 1) * 32]
                    in_ref[places[z], t, :, i * 256 : (i + 1) * 256] = piece

    wait_all(
        [
            copies.start(out_given_ref, out_given_hbm),
            copies.start(in_given_ref, in_given_hbm),
            copies.start(out_kept_ref, out_kept_hbm),
            copies.start(in_kept_ref, in_kept_hbm),
        ]
    )


def place_kernel(
    copies,
    where_ref,
    h0, h1, h2, h3, h4, h5, h6, h7,
    in_hbm, out_hbm, rel_hbm,
    a0, a1, a2, a3, c0, c1, c2, c3,
    in_ref, out_ref, owned_ref, rel_ref,
):
    sources = (h0, h1, h2, h3, h4, h5, h6, h7)
    targets = (a0, a1, a2, a3, c0, c1, c2, c3)
    wait_all([copies.start(source, target) for source, target in zip(sources, targets)])
    my_z, core = where_ref[0], where_ref[1]
    for pieces, half in (((a0, a1, a2, a3), core), ((c0, c1, c2, c3), 1 - core)):
        for piece, origin in zip(pieces, ORIGINS):
            z = lax.rem(my_z + origin, 4)
            values = piece[...].astype(F32)
            for i in range(4):
                rows = pl.ds(pl.multiple_of(half * 512 + z * 128 + i * 32, 32), 32)
                in_ref[rows, :] = values[0:32, i * 256 : (i + 1) * 256]
            out_ref[pl.ds(pl.multiple_of(half * 128 + z * 32, 32), 32), :] = values[32:64]
            rel_ref[pl.ds(pl.multiple_of(half * 32 + z * 8, 8), 8), :] = values[64:72]
    owned_ref[...] = rel_ref[0:52, :]
    wait_all([copies.start(in_ref, in_hbm), copies.start(out_ref, out_hbm), copies.start(owned_ref, rel_hbm)])


def shards(
    hidden,
    desc_len,
    w_in,
    w_out,
    send_order,
    place_order,
    cache,
    halo_rows,
    edge_src,
    edge_dst,
    edge_rel,
    rel_table,
    w_msg,
    w_self,
    d_out,
):
    entities, length, width = hidden.shape
    tokens = entities * length
    units = w_in.shape[1]
    my_core = lax.axis_index("core")
    where = jnp.stack([lax.axis_index(name) for name in ("z", "core", "x", "y")]).astype(I32)
    src, dst, rel = edge_src[0], edge_dst[0], edge_rel[0]
    shard_rows = rel_table.shape[0]

    rel_pad = jnp.pad(rel_table, ((0, 64 - shard_rows), (0, 0)))
    operands = [hidden.reshape(tokens, width), desc_len[None, :], send_order, edge_rel]
    outs = [((tokens + 16, width), BF), ((entities, width), F32), ((576, 512), BF)]
    block, hidden_sum, weights = local_call(
        norm_kernel,
        outs,
        [where, *operands, w_in, w_out, rel_pad],
        like(operands) + filled(outs),
        copies=14,
    )
    blocks = [block, *gather_ring(block, "x", 128)]
    mine = gather_ring(weights, "y", 256)
    other = [shift_by(part, "core", 1) for part in mine]

    outs = [
        ((256, width), BF),
        ((4 * tokens, width), BF),
        ((4 * tokens, 4 * units), BF),
        ((4 * entities, 4 * units), BF),
        ((4 * units, width), BF),
        ((4 * entities, 256), BF),
        ((4 * entities, 128), F32),
        ((512, 64), BF),
    ] + [((entities, width), BF)] * 4
    outgoing, normed, slope, pooled, all_out, route, inverse, rel_hot, *asked = local_call(
        encode_kernel,
        outs,
        [where, *blocks, w_in, w_out, rel_pad, *mine, *other, hidden_sum],
        filled(outs)
        + [
            pltpu.VMEM((width, 4 * units), BF),
            pltpu.VMEM((4 * entities, tokens), BF),
            pltpu.VMEM((256, width), BF),
            pltpu.VMEM((4, 16, 128), BF),
            pltpu.VMEM((entities, width), F32),
        ],
        copies=64,
        flops=2 * 4 * tokens * width * 4 * units,
    )

    halo = halo_rows[0]
    place = place_order[0]
    side = halo.shape[0] // 2
    cache_count = cache.shape[0]
    boundary = dot(one_hot(halo - entities, cache_count), cache).astype(BF)
    halo_hot = halo[:, None] == jnp.arange(entities, dtype=I32)[None, :]
    halo_place = jnp.where(halo < entities, jnp.sum(jnp.where(halo_hot, place[None, :], 0), axis=1), 16)

    def edge_of(rows, places):
        return jnp.concatenate([rows, jnp.pad(row_of(places, width), ((0, 15), (0, 0)))], axis=0)

    to_high, to_low = edge_of(boundary[side:], halo_place[side:]), edge_of(boundary[:side], halo_place[:side])
    to_high, to_low, outgoing = lax.optimization_barrier((to_high, to_low, outgoing))
    from_low = shift_by(to_high, GROUP, 1)
    from_high = shift_by(to_low, GROUP, 15)
    own_row = jnp.concatenate([fresh_row(0, place), jnp.full((cache_count,), -1, I32)])
    node_count = entities + cache_count
    extended_count = node_count + 2 * side
    edge_count = src.shape[0]
    block_count = rel.shape[0]
    src_hot = one_hot(src, extended_count)
    arrived = lax.all_to_all(outgoing.reshape(16, 16, width), GROUP, 0, 0, tiled=True).reshape(256, width)
    rel_rows = [asked[0]] + [shift_by(rows, "x", o) for rows, o in zip(asked[1:], ORIGINS[1:])]
    normed_t = normed.T

    outs = [((64, width), BF), ((block_count, width), BF)] + [((node_count, width), BF)] * 4
    operands = [
        arrived,
        one_hot_t(own_row, 64),
        *rel_rows,
        src_hot,
        one_hot(dst, node_count),
        one_hot_t(dst, node_count),
        w_msg,
        w_self,
        d_out,
    ]
    grad_table, grad_blocks, graph_out, aggregate, nodes, grad_pre = local_call(
        graph_kernel,
        outs,
        [where, *operands, cache, from_low, from_high],
        like(operands)
        + filled(outs)
        + [
            pltpu.VMEM((extended_count, width), BF),
            pltpu.VMEM((2, 16, 128), BF),
            pltpu.VMEM((64, extended_count), BF),
            pltpu.VMEM((64, edge_count), BF),
            pltpu.VMEM((extended_count, width), BF),
            pltpu.VMEM((edge_count, width), BF),
            pltpu.VMEM((edge_count, width), BF),
            pltpu.VMEM((node_count, width), BF),
            pltpu.VMEM((block_count, 1, width), F32),
            pltpu.VMEM((block_count, 1, width), F32),
        ],
        copies=26,
        flops=6 * 10**9,
    )

    back = jnp.broadcast_to(grad_table.reshape(1, 4, 16, width), (4, 4, 16, width))
    returned = lax.all_to_all(back.reshape(16, 16, width), GROUP, 0, 0, tiled=True).reshape(256, width)
    rel_blocks = [grad_blocks] + [shift_by(grad_blocks, "x", s) for s in SHIFTS]

    outs = [((4, 16, 16, width), BF)] * 2
    grad_pre, *rel_blocks = lax.optimization_barrier((grad_pre, *rel_blocks))
    operands = [aggregate, nodes, grad_pre]
    graph_kept, graph_given = local_call(
        weight_kernel, outs, [where, *operands], like(operands) + filled(outs), flops=10**9
    )
    chip = (graph_kept.astype(F32) + shift_by(graph_given, "core", 1).astype(F32)).astype(BF)
    line = lax.all_to_all(chip, "x", 0, 0, tiled=True)
    plane = lax.all_to_all(jnp.sum(line.astype(F32), axis=0).astype(BF), ("z", "y"), 0, 0, tiled=True)
    weight_rows = jnp.sum(plane.astype(F32), axis=0)
    grad_msg, grad_self = weight_rows[:8], weight_rows[8:]

    outs = [((4, 4, 48, width), BF)] * 2 + [((4, 4, 32, width), BF)] * 2
    operands = [returned, route, inverse, all_out, slope, pooled, normed_t, rel_hot, *rel_blocks]
    out_kept, out_given, in_kept, in_given = local_call(
        back_kernel,
        outs,
        [where, *operands],
        like(operands)
        + filled(outs)
        + [pltpu.VMEM((4 * entities, width), BF), pltpu.VMEM((4 * tokens, units), BF)],
        copies=16,
        flops=2 * 4 * tokens * width * 4 * units,
    )
    out_chip = (out_kept.astype(F32) + shift_by(out_given, "core", 1).astype(F32)).astype(BF)
    in_chip = (in_kept.astype(F32) + shift_by(in_given, "core", 1).astype(F32)).astype(BF)
    out_part = reduce_ring([out_chip[i].reshape(192, width) for i in range(4)], "y").reshape(4, 48, width)
    in_part = reduce_ring([in_chip[i].reshape(128, width) for i in range(4)], "z").reshape(4, 32, width)
    out_part = reduce_ring([out_part[i] for i in range(4)], "z")
    in_part = reduce_ring([in_part[i] for i in range(4)], "y")
    part = jnp.concatenate([in_part, out_part], axis=0)
    parts = [part] + [shift_by(part, "z", s) for s in SHIFTS]
    others = [shift_by(piece, "core", 1) for piece in parts]
    outs = [((width, units), F32), ((units, width), F32), ((shard_rows, width), F32)]
    operands = [*parts, *others]
    grad_w_in, grad_w_out, grad_rel = local_call(
        place_kernel,
        outs,
        [where, *operands],
        like(operands) + filled(outs) + [pltpu.VMEM((64, width), F32)],
        copies=12,
    )
    return (graph_out, grad_w_in, grad_w_out, grad_rel, grad_msg, grad_self)


def solution(mesh):
    fine = Mesh(mesh.devices.reshape(4, 2, 4, 4), ("z", "core", "x", "y"))
    every = ("z", "core", "x", "y")
    placed = (
        P(every, None, None),
        P(every),
        P(None, GROUP),
        P(GROUP, None),
        P(every, None),
        P(every, None),
        P(every, None),
        P(every, None),
        P(every, None),
        P(every, None),
        P(every, None),
        P(GROUP, None),
        P(),
        P(),
        P(every, None),
    )
    return jax.shard_map(
        shards,
        mesh=fine,
        in_specs=placed,
        out_specs=(
            P(every, None),
            P(None, GROUP),
            P(GROUP, None),
            P(GROUP, None),
            P(every, None),
            P(every, None),
        ),
        check_vma=False,
    )
```

```python
import jax
import jax.numpy as jnp
import numpy as np
from jax import lax
from jax.experimental import pallas as pl
from jax.experimental.pallas import tpu as pltpu
from jax.sharding import Mesh
from jax.sharding import PartitionSpec as P

BF = jnp.bfloat16
F32 = jnp.float32
I32 = jnp.int32
GROUP = ("x", "y")
SHIFTS = (1, 3, 2)
ORIGINS = (0, 3, 1, 2)
GELU_SCALE = float(np.sqrt(2.0 / np.pi))
GELU_CUBE = 0.044715


def shift_by(value, axis, shift):
    count = lax.axis_size(axis)
    return lax.ppermute(value, axis, [(i, (i + shift) % count) for i in range(count)])


def dot(a, b):
    return jnp.dot(a, b, preferred_element_type=F32)


def dot_t(a, b):
    return lax.dot_general(a, b, (((0,), (0,)), ((), ())), preferred_element_type=F32)


def dot_bt(a, b):
    return lax.dot_general(a, b, (((1,), (1,)), ((), ())), preferred_element_type=F32)


def one_hot(index, count):
    return (index[:, None] == jnp.arange(count, dtype=I32)[None, :]).astype(BF)


def one_hot_t(index, count):
    return (index[None, :] == jnp.arange(count, dtype=I32)[:, None]).astype(BF)


def lanes(shape):
    return lax.broadcasted_iota(I32, shape, 1)


def sublanes(shape):
    return lax.broadcasted_iota(I32, shape, 0)


def row_of(values, width):
    return jnp.pad(values.astype(BF), (0, width - values.shape[0]))[None, :]


def gather_ring(value, axis, cut):
    low, high = shift_by(value, axis, 1), shift_by(value, axis, 3)
    return [low, high, shift_by(low[:cut], axis, 1), shift_by(high[cut:], axis, 3)]


def reduce_ring(chunks, axis):
    total = chunks[0].astype(F32)
    for chunk, origin in zip(chunks[1:], ORIGINS[1:]):
        total = total + shift_by(chunk, axis, origin).astype(F32)
    return total.astype(BF)


def fresh_row(side, place):
    return (place % 4) * 16 + (side + 1) * 4 + place // 4


class Copies:
    def __init__(self, sems):
        self.sems, self.used = sems, 0

    def start(self, source, target):
        copy = pltpu.make_async_copy(source, target, self.sems.at[self.used])
        self.used += 1
        copy.start()
        return copy


def local_call(body, outs, operands, scratch=(), copies=8, flops=0, limit=60):
    def kernel(*refs):
        body(Copies(refs[-1]), *refs[:-1])

    return pl.pallas_call(
        kernel,
        out_shape=[jax.ShapeDtypeStruct(shape, kind) for shape, kind in outs],
        in_specs=[pl.BlockSpec(memory_space=pltpu.SMEM)]
        + [pl.BlockSpec(memory_space=pltpu.HBM)] * (len(operands) - 1),
        out_specs=[pl.BlockSpec(memory_space=pltpu.HBM)] * len(outs),
        scratch_shapes=[*scratch, pltpu.SemaphoreType.DMA((copies,))],
        compiler_params=pltpu.CompilerParams(vmem_limit_bytes=limit * 1024 * 1024),
        cost_estimate=pl.CostEstimate(flops=flops, bytes_accessed=1024 * 1024, transcendentals=0),
    )(*operands)


def like(arrays):
    return [pltpu.VMEM(array.shape, array.dtype) for array in arrays]


def filled(outs):
    return [pltpu.VMEM(shape, kind) for shape, kind in outs]


def wait_all(copies):
    for copy in copies:
        copy.wait()


def length_column(meta):
    shape = meta.shape
    return jnp.sum(jnp.where(lanes(shape) == sublanes(shape), meta, 0.0), axis=1, keepdims=True)


def pool_rows(length, tokens):
    shape = (16, tokens)
    line = lanes(shape)
    inside = (line // 16 == sublanes(shape)) & ((line % 16).astype(F32) < length)
    return inside.astype(F32).astype(BF)


def norm_kernel(
    copies,
    where_ref,
    hidden_hbm, lens_hbm, order_hbm, rel_hbm, in_hbm, out_hbm, table_hbm,
    block_hbm, sum_hbm, weights_hbm,
    hidden_ref, lens_ref, order_ref, rel_ref,
    block_ref, sum_ref, weights_ref,
):
    core = where_ref[1]
    packed = []
    for i in range(2):
        cols, wide = pl.ds(i * 256, 256), pl.ds(i * 512, 512)
        source = in_hbm.at[pl.ds(pl.multiple_of(core * 512 + i * 256, 256), 256), :]
        packed.append(copies.start(source, weights_ref.at[pl.ds(0, 256), cols]))
        source = out_hbm.at[pl.ds(pl.multiple_of(core * 128, 128), 128), wide]
        packed.append(copies.start(source, weights_ref.at[pl.ds(256 + i * 128, 128), :]))
        source = table_hbm.at[pl.ds(pl.multiple_of(core * 32, 32), 32), wide]
        packed.append(copies.start(source, weights_ref.at[pl.ds(512 + i * 32, 32), :]))
    first = [
        copies.start(hidden_hbm, hidden_ref),
        copies.start(lens_hbm, lens_ref),
        copies.start(order_hbm, order_ref),
        copies.start(rel_hbm, rel_ref),
    ]
    wait_all(packed)
    later = [copies.start(weights_ref, weights_hbm)]
    wait_all(first)
    meta = jnp.zeros((16, 128), F32)
    high = rel_ref[...] // 32
    for i, row in enumerate((lens_ref[...], order_ref[...], high, rel_ref[...] - 32 * high)):
        values = jnp.broadcast_to(row.astype(F32), (16, 16)).astype(BF)
        select = (lanes((16, 128)) == sublanes((16, 128)) + 16 * i).astype(F32).astype(BF)
        meta = meta + dot(values, select)
    values = hidden_ref[...].astype(F32)
    center = values - jnp.mean(values, axis=-1, keepdims=True)
    spread = jnp.mean(center * center, axis=-1, keepdims=True)
    tokens = values.shape[0]
    block_ref[0:tokens, :] = (center * lax.rsqrt(spread + 1e-05)).astype(BF)
    block_ref[tokens : tokens + 16, :] = jnp.zeros((16, values.shape[1]), BF)
    block_ref[tokens : tokens + 16, 0:128] = meta.astype(BF)
    later.append(copies.start(block_ref, block_hbm))
    sum_ref[...] = dot(pool_rows(length_column(meta), tokens), hidden_ref[...])
    later.append(copies.start(sum_ref, sum_hbm))
    wait_all(later)


def encode_kernel(
    copies,
    where_ref,
    b0, b1, b2, b3_top, b3_rest,
    own_in, own_out, own_rel,
    m1, m2, m3_in, m3_rest,
    o1, o2, o3_in, o3_rest,
    hidden_sum_hbm,
    outgoing_hbm, normed_hbm, slope_hbm, pooled_hbm, all_out_hbm, route_hbm, length_hbm, rel_hot_hbm,
    rel0_hbm, rel1_hbm, rel2_hbm, rel3_hbm,
    outgoing_ref, normed_ref, slope_ref, pooled_ref, all_out_ref, route_ref, length_ref, rel_hot_ref,
    rel0_ref, rel1_ref, rel2_ref, rel3_ref,
    in_ref, pool_ref, rel_ref, meta_ref, hidden_sum_ref,
):
    core, my_x, my_y = where_ref[1], where_ref[2], where_ref[3]
    metas, tokens, weights, tables = [], [], [[], [], [], []], []
    for s, (block, row) in enumerate(((b0, 256), (b1, 256), (b2, 256), (b3_rest, 128))):
        metas.append(copies.start(block.at[pl.ds(row, 16), pl.ds(0, 128)], meta_ref.at[s]))
    tables.append(copies.start(own_rel, rel_ref.at[pl.ds(0, 64), :]))
    pieces = []
    for t, (mine, other) in enumerate(
        (((m1, m1, 256), (o1, o1, 256)), ((m2, m2, 256), (o2, o2, 256)), ((m3_in, m3_rest, 0), (o3_in, o3_rest, 0))), 1
    ):
        for (inner, rest, at), half in ((mine, core), (other, 1 - core)):
            pieces.append((t, inner, rest, at, half))
            for i in range(2):
                rows = pl.ds(pl.multiple_of(t * 64 + half * 32, 32), 32)
                target = rel_ref.at[rows, pl.ds(i * 512, 512)]
                tables.append(copies.start(rest.at[pl.ds(at + 256 + i * 32, 32), :], target))
    for s, (block, row, count) in enumerate(((b0, 0, 256), (b1, 256, 256), (b2, 512, 256), (b3_top, 768, 128), (b3_rest, 896, 128))):
        tokens.append(copies.start(block.at[pl.ds(0, count), :], normed_ref.at[pl.ds(row, count), :]))
    weights[0].append(copies.start(own_in, in_ref.at[:, pl.ds(0, 256)]))
    for t, inner, rest, at, half in pieces:
        for i in range(2):
            rows = pl.ds(pl.multiple_of(half * 512 + i * 256, 256), 256)
            target = in_ref.at[rows, pl.ds(t * 256, 256)]
            weights[t].append(copies.start(inner.at[pl.ds(0, 256), pl.ds(i * 256, 256)], target))
    outer = [
        copies.start(own_out, all_out_ref.at[pl.ds(0, 256), :]),
        copies.start(hidden_sum_hbm, hidden_sum_ref),
    ]
    for t, inner, rest, at, half in pieces:
        for i in range(2):
            rows = pl.ds(pl.multiple_of(t * 256 + half * 128, 128), 128)
            target = all_out_ref.at[rows, pl.ds(i * 512, 512)]
            outer.append(copies.start(rest.at[pl.ds(at + i * 128, 128), :], target))
    wait_all(metas)
    wait_all(tables)

    wide = (16, 256)
    slot = lanes(wide) % 16
    bound = lanes((128, 256))
    bound = (bound // 16 + (bound % 16) // 4 + 15) % 16
    bound_hot = (sublanes((128, 256)) == bound + 16).astype(F32).astype(BF)
    ids = jnp.zeros((16, 64), F32)
    asked = (rel0_ref, rel1_ref, rel2_ref, rel3_ref)
    for s in range(4):
        meta = meta_ref[s]
        values = meta.astype(F32)
        apart = lanes(meta.shape) - sublanes(meta.shape)
        wanted = jnp.where(apart == 32, 32.0 * values, jnp.where(apart == 48, values, 0.0))
        wanted = jnp.sum(wanted, axis=1, keepdims=True)
        line = lanes(wide)
        owner_y = (my_y + jnp.where(line < 64, 0, jnp.where(line < 128, 3, line // 64 - 1))) % 4
        name = (my_x * 4 + owner_y) * 52 + line % 64
        pick = (name.astype(F32) == wanted) & (line % 64 < 52)
        asked[s][...] = dot(pick.astype(F32).astype(BF), rel_ref[...]).astype(BF)
        length = length_column(values)
        length_ref[s * 16 : (s + 1) * 16, :] = jnp.broadcast_to(1.0 / length, (16, 128))
        pool_ref[s * 16 : (s + 1) * 16, :] = pool_rows(length, 256)
        sent = dot(meta, bound_hot)
        encoder = lax.rem(my_x + ORIGINS[s], 4)
        chosen = (sent == sublanes(wide).astype(F32)) & (slot % 4 == encoder) & (slot < 12)
        route_ref[s * 16 : (s + 1) * 16, :] = chosen.astype(F32).astype(BF)
        at, to = sublanes((128, 64)), lanes((128, 64)) - s * 16
        inside = (to >= 0) & (to < 16)
        select = jnp.where(inside & (at == 32 + to), 32.0, jnp.where(inside & (at == 48 + to), 1.0, 0.0))
        ids = ids + dot(meta, select.astype(BF))
    line = sublanes((512, 64))
    local = (line // 64) % 2 * 32 + (line // 16) % 4 * 8 + line % 16
    name = (my_x * 4 + line // 128) * 52 + local
    good = (line % 16 < 8) & (local < 52)
    rel_hot_ref[...] = ((name.astype(F32) == ids[0:1, :]) & good).astype(F32).astype(BF)

    sent_out = [
        copies.start(rel0_ref, rel0_hbm),
        copies.start(rel1_ref, rel1_hbm),
        copies.start(rel2_ref, rel2_hbm),
        copies.start(rel3_ref, rel3_hbm),
        copies.start(route_ref, route_hbm),
        copies.start(length_ref, length_hbm),
        copies.start(rel_hot_ref, rel_hot_hbm),
    ]
    wait_all(tokens)
    sent_out.append(copies.start(normed_ref, normed_hbm))
    for t in range(4):
        cols = slice(t * 256, (t + 1) * 256)
        wait_all(weights[t])

        @pl.loop(0, 2)
        def _(s):
            rows = pl.ds(pl.multiple_of(s * 512, 512), 512)
            pre = dot(normed_ref[rows, :], in_ref[:, cols])
            square = pre * pre
            tanh = jnp.tanh(GELU_SCALE * pre * (1.0 + GELU_CUBE * square))
            upper = 0.5 + 0.5 * tanh
            slope = upper + (0.5 * GELU_SCALE) * pre * (1.0 - tanh * tanh) * (1.0 + 3.0 * GELU_CUBE * square)
            slope_ref[rows, cols] = slope.astype(BF)
            activation = (pre * upper).astype(BF)
            for i in range(2):
                few = pl.ds(pl.multiple_of(s * 32 + i * 16, 16), 16)
                pooled = dot(pool_ref[few, :], activation[i * 256 : (i + 1) * 256])
                pooled_ref[few, cols] = pooled.astype(BF)

    sent_out.append(copies.start(slope_ref, slope_hbm))
    sent_out.append(copies.start(pooled_ref, pooled_hbm))
    wait_all(outer)
    sent_out.append(copies.start(all_out_ref, all_out_hbm))
    partial = dot(pooled_ref[...], all_out_ref[...])
    partial = jnp.concatenate([partial[0:16] + hidden_sum_ref[...], partial[16:64]], axis=0)
    partial = (partial * length_ref[:, 0:1]).astype(BF)
    outgoing_ref[...] = dot_t(route_ref[...], partial).astype(BF)
    sent_out.append(copies.start(outgoing_ref, outgoing_hbm))
    wait_all(sent_out)


def graph_kernel(
    copies,
    where_ref,
    arrived_hbm, own_hot_t_hbm, e0_hbm, e1_hbm, e2_hbm, e3_hbm,
    src_hot_hbm, dst_hot_hbm, dst_hot_t_hbm,
    w_msg_hbm, w_self_hbm, d_out_hbm,
    cache_hbm, low_hbm, high_hbm,
    table_out_hbm, blocks_hbm, graph_out_hbm, aggregate_hbm, nodes_hbm, pre_hbm,
    arrived_ref, own_hot_t_ref, e0, e1, e2, e3,
    src_hot_ref, dst_hot_ref, dst_hot_t_ref,
    w_msg_ref, w_self_ref, d_out_ref,
    table_out_ref, blocks_ref, graph_out_ref, aggregate_ref, nodes_ref, pre_ref,
    base_ref, places_ref, row_hot_t_ref, src_row_hot_ref,
    ext_ref, sources_ref, edges_ref, agg_grad_ref, sums_ref, rel_ref,
):
    scale = (256 / 2048) ** 0.5
    first = [
        copies.start(low_hbm.at[pl.ds(64, 16), pl.ds(0, 128)], places_ref.at[0]),
        copies.start(high_hbm.at[pl.ds(64, 16), pl.ds(0, 128)], places_ref.at[1]),
        copies.start(own_hot_t_hbm, own_hot_t_ref),
        copies.start(arrived_hbm, arrived_ref),
        copies.start(cache_hbm, base_ref.at[pl.ds(16, 240), :]),
        copies.start(low_hbm.at[pl.ds(0, 64), :], base_ref.at[pl.ds(256, 64), :]),
        copies.start(high_hbm.at[pl.ds(0, 64), :], base_ref.at[pl.ds(320, 64), :]),
        copies.start(e0_hbm, e0),
        copies.start(e1_hbm, e1),
        copies.start(e2_hbm, e2),
        copies.start(e3_hbm, e3),
        copies.start(src_hot_hbm, src_hot_ref),
    ]
    second = [copies.start(dst_hot_t_hbm, dst_hot_t_ref)]
    third = [
        copies.start(w_msg_hbm, w_msg_ref),
        copies.start(w_self_hbm, w_self_ref),
        copies.start(d_out_hbm, d_out_ref),
    ]
    fourth = [copies.start(dst_hot_hbm, dst_hot_ref)]
    base_ref[0:16, :] = jnp.zeros((16, 1024), BF)
    wait_all(first)
    rel = e0[...].astype(F32) + e1[...].astype(F32) + e2[...].astype(F32) + e3[...].astype(F32)
    for j in range(16):
        rel_ref[j] = rel[j : j + 1]

    to = lanes((128, 128)) - sublanes((128, 128))
    inside = sublanes((128, 128)) < 64
    low_move = ((to == 0) & inside).astype(F32).astype(BF)
    high_move = ((to == 64) & inside).astype(F32).astype(BF)
    places = (dot(places_ref[0], low_move) + dot(places_ref[1], high_move))[0:1].astype(I32)
    upper = (lax.broadcasted_iota(I32, (1, 128), 1) >= 64).astype(I32)
    table_row = jnp.where(places < 16, (places % 4) * 16 + upper * 8 + places // 4, -1)
    row_hot_t_ref[:, 0:256] = own_hot_t_ref[...]
    row_hot_t_ref[:, 256:384] = (sublanes((64, 128)) == table_row).astype(F32).astype(BF)
    src_row_hot_ref[...] = dot_bt(row_hot_t_ref[...], src_hot_ref[...]).astype(BF)
    total = arrived_ref[0:64, :].astype(F32)
    for i in range(1, 4):
        total = total + arrived_ref[i * 64 : (i + 1) * 64, :].astype(F32)
    table = total.astype(BF)
    ext_ref[...] = (base_ref[...].astype(F32) + dot_t(row_hot_t_ref[...], table)).astype(BF)
    nodes_ref[...] = ext_ref[0:256, :]
    sent_out = [copies.start(nodes_ref, nodes_hbm)]

    for n in range(4):
        cols = slice(n * 256, (n + 1) * 256)

        @pl.loop(0, 4)
        def _(k):
            rows = pl.ds(pl.multiple_of(k * 512, 512), 512)
            taken = dot(src_hot_ref[rows, :], ext_ref[:, cols])
            taken = taken.astype(BF)
            sources_ref[rows, cols] = taken
            for i in range(4):
                few = pl.ds(pl.multiple_of(k * 512 + i * 128, 128), 128)
                edges_ref[few, cols] = taken[i * 128 : (i + 1) * 128] * rel_ref[k * 4 + i, :, cols].astype(BF)

    wait_all(second)

    @pl.loop(0, 4)
    def _(n):
        cols = pl.ds(pl.multiple_of(n * 256, 256), 256)
        aggregate_ref[:, cols] = (scale * dot(dst_hot_t_ref[...], edges_ref[:, cols])).astype(BF)

    sent_out.append(copies.start(aggregate_ref, aggregate_hbm))
    wait_all(third)

    @pl.loop(0, 4)
    def _(n):
        cols = pl.ds(pl.multiple_of(n * 256, 256), 256)
        out_pre = dot(aggregate_ref[...], w_msg_ref[:, cols]) + dot(nodes_ref[...], w_self_ref[:, cols])
        squashed = jnp.tanh(out_pre)
        graph_out_ref[:, cols] = squashed.astype(BF)
        pre_ref[:, cols] = (d_out_ref[:, cols].astype(F32) * (1.0 - squashed * squashed)).astype(BF)

    sent_out.append(copies.start(graph_out_ref, graph_out_hbm))
    sent_out.append(copies.start(pre_ref, pre_hbm))

    @pl.loop(0, 4)
    def _(n):
        cols = pl.ds(pl.multiple_of(n * 256, 256), 256)
        agg_grad_ref[:, cols] = (scale * dot_bt(pre_ref[...], w_msg_ref[cols, :])).astype(BF)

    wait_all(fourth)

    for n in range(4):
        cols = slice(n * 256, (n + 1) * 256)

        @pl.loop(0, 4)
        def _(k):
            rows = pl.ds(pl.multiple_of(k * 512, 512), 512)
            at_dest = dot(dst_hot_ref[rows, :], agg_grad_ref[:, cols])
            for i in range(4):
                few = pl.ds(pl.multiple_of(k * 512 + i * 128, 128), 128)
                part = at_dest[i * 128 : (i + 1) * 128]
                edges_ref[few, cols] = part.astype(BF) * rel_ref[k * 4 + i, :, cols].astype(BF)
                product = part * sources_ref[few, cols].astype(F32)
                sums_ref[k * 4 + i, :, cols] = jnp.sum(product, axis=0, keepdims=True)

    blocks_ref[...] = jnp.concatenate([sums_ref[j] for j in range(16)], axis=0).astype(BF)
    sent_out.append(copies.start(blocks_ref, blocks_hbm))
    own_pre = dot(own_hot_t_ref[...], pre_ref[...]).astype(BF)

    @pl.loop(0, 4)
    def _(n):
        cols = pl.ds(pl.multiple_of(n * 256, 256), 256)
        grad = dot(src_row_hot_ref[...], edges_ref[:, cols]) + dot_bt(own_pre, w_self_ref[cols, :])
        table_out_ref[:, cols] = grad.astype(BF)

    for x in range(4):
        sent_out.append(copies.start(table_out_ref, table_out_hbm.at[pl.ds(x * 64, 64), :]))
    wait_all(sent_out)


def weight_kernel(
    copies,
    where_ref,
    aggregate_hbm, nodes_hbm, pre_hbm,
    kept_hbm, given_hbm,
    aggregate_ref, nodes_ref, pre_ref,
    kept_ref, given_ref,
):
    core = where_ref[1]
    places = ring_places(where_ref[2])
    wait_all(
        [copies.start(aggregate_hbm, aggregate_ref), copies.start(nodes_hbm, nodes_ref), copies.start(pre_hbm, pre_ref)]
    )
    sent_out = []
    for half, chunk_ref, chunk_hbm in ((1 - core, given_ref, given_hbm), (core, kept_ref, kept_hbm)):

        @pl.loop(0, 4)
        def _(z):
            rows = pl.ds(pl.multiple_of(z * 256 + half * 128, 128), 128)
            msg = dot_t(aggregate_ref[:, rows], pre_ref[...])
            own = dot_t(nodes_ref[:, rows], pre_ref[...])
            for x in range(4):
                for y in range(4):
                    at = (x * 4 + y) * 8
                    both = jnp.concatenate([msg[at : at + 8], own[at : at + 8]], axis=0)
                    chunk_ref[places[x], z * 4 + y] = both.astype(BF)

        sent_out.append(copies.start(chunk_ref, chunk_hbm))
    wait_all(sent_out)


def out_kernel(
    copies,
    where_ref,
    returned_hbm, route_hbm, length_hbm, rel_hot_hbm, pooled_hbm, r0_hbm, r1_hbm, r2_hbm, r3_hbm,
    given_hbm, kept_hbm, scaled_hbm,
    returned_ref, route_ref, length_ref, rel_hot_ref, pooled_ref, r0, r1, r2, r3,
    given_ref, kept_ref, scaled_ref,
):
    my_z, core, my_y = where_ref[0], where_ref[1], where_ref[3]
    wait_all(
        [
            copies.start(returned_hbm, returned_ref),
            copies.start(route_hbm, route_ref),
            copies.start(length_hbm, length_ref),
            copies.start(rel_hot_hbm, rel_hot_ref),
            copies.start(pooled_hbm, pooled_ref),
            copies.start(r0_hbm, r0),
            copies.start(r1_hbm, r1),
            copies.start(r2_hbm, r2),
            copies.start(r3_hbm, r3),
        ]
    )
    scaled_ref[...] = (dot(route_ref[...], returned_ref[...]) * length_ref[:, 0:1]).astype(BF)
    sent_out = [copies.start(scaled_ref, scaled_hbm)]
    blocks = jnp.concatenate([r0[...], r1[...], r2[...], r3[...]], axis=0)
    places = ring_places(my_z)
    for half, out_ref, out_hbm in ((1 - core, given_ref, given_hbm), (core, kept_ref, kept_hbm)):
        for t in range(4):
            owner = lax.rem(my_y + ORIGINS[t], 4)
            units = pl.ds(pl.multiple_of(t * 256 + half * 128, 128), 128)
            out = dot_t(pooled_ref[:, units], scaled_ref[...]).astype(BF)
            rel_rows = pl.ds(pl.multiple_of(owner * 128 + half * 64, 64), 64)
            rel = dot(rel_hot_ref[rel_rows, :], blocks).astype(BF)
            for z in range(4):
                out_ref[owner, places[z], 0:32, :] = out[z * 32 : (z + 1) * 32]
                out_ref[owner, places[z], 32:48, :] = rel[z * 16 : (z + 1) * 16]
        sent_out.append(copies.start(out_ref, out_hbm))
    wait_all(sent_out)


def ring_places(mine):
    places = []
    for at in range(4):
        ahead = lax.rem(at - mine + 4, 4)
        places.append(jnp.where(ahead == 0, 0, jnp.where(ahead == 3, 1, ahead + 1)))
    return places


def in_kernel(
    copies,
    where_ref,
    scaled_hbm, length_hbm, all_out_hbm, slope_hbm, normed_t_hbm,
    given_hbm, kept_hbm,
    scaled_ref, length_ref, all_out_ref, slope_ref, normed_t_ref,
    given_ref, kept_ref,
    grad_ref,
):
    my_z, core = where_ref[0], where_ref[1]
    wait_first = [
        copies.start(scaled_hbm, scaled_ref),
        copies.start(length_hbm, length_ref),
        copies.start(all_out_hbm, all_out_ref),
        copies.start(slope_hbm, slope_ref),
    ]
    wait_next = [copies.start(normed_t_hbm, normed_t_ref)]
    places = ring_places(my_z)
    wait_all(wait_first)
    pools = []
    for s in range(4):
        line = lanes((16, 256))
        length = 1.0 / length_ref[s * 16 : (s + 1) * 16, 0:1]
        inside = (line // 16 == sublanes((16, 256))) & ((line % 16).astype(F32) + 0.5 < length)
        pools.append(inside.astype(F32).astype(BF))

    @pl.loop(0, 4)
    def _(t):
        cols = pl.ds(pl.multiple_of(t * 256, 256), 256)
        upstream = dot_bt(scaled_ref[...], all_out_ref[cols, :]).astype(BF)
        for s in range(4):
            rows = slice(s * 256, (s + 1) * 256)
            at_tokens = dot_t(pools[s], upstream[s * 16 : (s + 1) * 16])
            grad_ref[rows, cols] = (slope_ref[rows, cols].astype(F32) * at_tokens).astype(BF)

    wait_all(wait_next)
    sent_out = []
    for half, in_ref, in_hbm in ((1 - core, given_ref, given_hbm), (core, kept_ref, kept_hbm)):

        @pl.loop(0, 4)
        def _(t):
            cols = pl.ds(pl.multiple_of(t * 256, 256), 256)
            inner = dot(normed_t_ref[pl.ds(pl.multiple_of(half * 512, 512), 512), :], grad_ref[:, cols]).astype(BF)
            for z in range(4):
                for i in range(4):
                    piece = inner[z * 128 + i * 32 : z * 128 + (i + 1) * 32]
                    in_ref[places[z], t, :, i * 256 : (i + 1) * 256] = piece

        sent_out.append(copies.start(in_ref, in_hbm))
    wait_all(sent_out)


def place_kernel(
    copies,
    where_ref,
    h0, h1, h2, h3, h4, h5, h6, h7,
    in_hbm, out_hbm, rel_hbm,
    a0, a1, a2, a3, c0, c1, c2, c3,
    in_ref, out_ref, owned_ref, rel_ref,
):
    sources = (h0, h1, h2, h3, h4, h5, h6, h7)
    targets = (a0, a1, a2, a3, c0, c1, c2, c3)
    wait_all([copies.start(source, target) for source, target in zip(sources, targets)])
    my_z, core = where_ref[0], where_ref[1]
    for pieces, half in (((a0, a1, a2, a3), core), ((c0, c1, c2, c3), 1 - core)):
        for piece, origin in zip(pieces, ORIGINS):
            z = lax.rem(my_z + origin, 4)
            values = piece[...].astype(F32)
            for i in range(4):
                rows = pl.ds(pl.multiple_of(half * 512 + z * 128 + i * 32, 32), 32)
                in_ref[rows, :] = values[0:32, i * 256 : (i + 1) * 256]
            out_ref[pl.ds(pl.multiple_of(half * 128 + z * 32, 32), 32), :] = values[32:64]
            rel_ref[pl.ds(pl.multiple_of(half * 32 + z * 8, 8), 8), :] = values[64:72]
    owned_ref[...] = rel_ref[0:52, :]
    wait_all([copies.start(in_ref, in_hbm), copies.start(out_ref, out_hbm), copies.start(owned_ref, rel_hbm)])


def shards(
    hidden,
    desc_len,
    w_in,
    w_out,
    send_order,
    place_order,
    cache,
    halo_rows,
    edge_src,
    edge_dst,
    edge_rel,
    rel_table,
    w_msg,
    w_self,
    d_out,
):
    entities, length, width = hidden.shape
    tokens = entities * length
    units = w_in.shape[1]
    my_core = lax.axis_index("core")
    where = jnp.stack([lax.axis_index(name) for name in ("z", "core", "x", "y")]).astype(I32)
    src, dst, rel = edge_src[0], edge_dst[0], edge_rel[0]
    shard_rows = rel_table.shape[0]

    rel_pad = jnp.pad(rel_table, ((0, 64 - shard_rows), (0, 0)))
    operands = [hidden.reshape(tokens, width), desc_len[None, :], send_order, edge_rel]
    outs = [((tokens + 16, width), BF), ((entities, width), F32), ((576, 512), BF)]
    block, hidden_sum, weights = local_call(
        norm_kernel,
        outs,
        [where, *operands, w_in, w_out, rel_pad],
        like(operands) + filled(outs),
        copies=14,
    )
    blocks = [block, *gather_ring(block, "x", 128)]
    mine = gather_ring(weights, "y", 256)
    other = [shift_by(part, "core", 1) for part in mine]

    outs = [
        ((256, width), BF),
        ((4 * tokens, width), BF),
        ((4 * tokens, 4 * units), BF),
        ((4 * entities, 4 * units), BF),
        ((4 * units, width), BF),
        ((4 * entities, 256), BF),
        ((4 * entities, 128), F32),
        ((512, 64), BF),
    ] + [((entities, width), BF)] * 4
    outgoing, normed, slope, pooled, all_out, route, inverse, rel_hot, *asked = local_call(
        encode_kernel,
        outs,
        [where, *blocks, w_in, w_out, rel_pad, *mine, *other, hidden_sum],
        filled(outs)
        + [
            pltpu.VMEM((width, 4 * units), BF),
            pltpu.VMEM((4 * entities, tokens), BF),
            pltpu.VMEM((256, width), BF),
            pltpu.VMEM((4, 16, 128), BF),
            pltpu.VMEM((entities, width), F32),
        ],
        copies=64,
        flops=2 * 4 * tokens * width * 4 * units,
    )

    halo = halo_rows[0]
    place = place_order[0]
    side = halo.shape[0] // 2
    cache_count = cache.shape[0]
    boundary = dot(one_hot(halo - entities, cache_count), cache).astype(BF)
    halo_hot = halo[:, None] == jnp.arange(entities, dtype=I32)[None, :]
    halo_place = jnp.where(halo < entities, jnp.sum(jnp.where(halo_hot, place[None, :], 0), axis=1), 16)

    def edge_of(rows, places):
        return jnp.concatenate([rows, jnp.pad(row_of(places, width), ((0, 15), (0, 0)))], axis=0)

    to_high, to_low = edge_of(boundary[side:], halo_place[side:]), edge_of(boundary[:side], halo_place[:side])
    to_high, to_low, outgoing = lax.optimization_barrier((to_high, to_low, outgoing))
    from_low = shift_by(to_high, GROUP, 1)
    from_high = shift_by(to_low, GROUP, 15)
    own_row = jnp.concatenate([fresh_row(0, place), jnp.full((cache_count,), -1, I32)])
    node_count = entities + cache_count
    extended_count = node_count + 2 * side
    edge_count = src.shape[0]
    block_count = rel.shape[0]
    src_hot = one_hot(src, extended_count)
    arrived = lax.all_to_all(outgoing.reshape(16, 16, width), GROUP, 0, 0, tiled=True).reshape(256, width)
    rel_rows = [asked[0]] + [shift_by(rows, "x", o) for rows, o in zip(asked[1:], ORIGINS[1:])]
    arrived, normed_t = lax.optimization_barrier((arrived, normed.T))

    outs = [((256, width), BF), ((block_count, width), BF)] + [((node_count, width), BF)] * 4
    operands = [
        arrived,
        one_hot_t(own_row, 64),
        *rel_rows,
        src_hot,
        one_hot(dst, node_count),
        one_hot_t(dst, node_count),
        w_msg,
        w_self,
        d_out,
    ]
    grad_table, grad_blocks, graph_out, aggregate, nodes, grad_pre = local_call(
        graph_kernel,
        outs,
        [where, *operands, cache, from_low, from_high],
        like(operands)
        + filled([((64, width), BF), *outs[1:]])
        + [
            pltpu.VMEM((extended_count, width), BF),
            pltpu.VMEM((2, 16, 128), BF),
            pltpu.VMEM((64, extended_count), BF),
            pltpu.VMEM((64, edge_count), BF),
            pltpu.VMEM((extended_count, width), BF),
            pltpu.VMEM((edge_count, width), BF),
            pltpu.VMEM((edge_count, width), BF),
            pltpu.VMEM((node_count, width), BF),
            pltpu.VMEM((block_count, 1, width), F32),
            pltpu.VMEM((block_count, 1, width), F32),
        ],
        copies=30,
        flops=6 * 10**9,
    )

    returned = lax.all_to_all(grad_table.reshape(16, 16, width), GROUP, 0, 0, tiled=True).reshape(256, width)
    rel_blocks = [grad_blocks] + [shift_by(grad_blocks, "x", s) for s in SHIFTS]

    outs = [((4, 16, 16, width), BF)] * 2
    grad_pre, *rel_blocks = lax.optimization_barrier((grad_pre, *rel_blocks))
    operands = [aggregate, nodes, grad_pre]
    graph_kept, graph_given = local_call(
        weight_kernel, outs, [where, *operands], like(operands) + filled(outs), flops=10**9
    )
    chip = (graph_kept.astype(F32) + shift_by(graph_given, "core", 1).astype(F32)).astype(BF)
    outs = [((4, 4, 48, width), BF)] * 2 + [((4 * entities, width), BF)]
    operands = [returned, route, inverse, rel_hot, pooled, *rel_blocks]
    out_given, out_kept, scaled = local_call(
        out_kernel, outs, [where, *operands], like(operands) + filled(outs), copies=12, flops=10**9
    )
    out_chip = (out_kept.astype(F32) + shift_by(out_given, "core", 1).astype(F32)).astype(BF)
    scaled, out_chip, chip = lax.optimization_barrier((scaled, out_chip, chip))
    out_lines = lax.all_to_all(out_chip, "y", 0, 0, tiled=True)
    outs = [((4, 4, 32, width), BF)] * 2
    operands = [scaled, inverse, all_out, slope, normed_t]
    in_given, in_kept = local_call(
        in_kernel,
        outs,
        [where, *operands],
        like(operands) + filled(outs) + [pltpu.VMEM((4 * tokens, 4 * units), BF)],
        flops=10 * 4 * tokens * width * 4 * units,
    )

    line = reduce_ring([chip[i] for i in range(4)], "x")
    plane = lax.all_to_all(line, ("z", "y"), 0, 0, tiled=True)
    weight_rows = jnp.sum(plane.astype(F32), axis=0)
    grad_msg, grad_self = weight_rows[:8], weight_rows[8:]
    in_chip = (in_kept.astype(F32) + shift_by(in_given, "core", 1).astype(F32)).astype(BF)
    out_part = jnp.sum(out_lines.astype(F32), axis=0).astype(BF)
    in_part = reduce_ring([in_chip[i].reshape(128, width) for i in range(4)], "z").reshape(4, 32, width)
    out_part = reduce_ring([out_part[i] for i in range(4)], "z")
    in_part = reduce_ring([in_part[i] for i in range(4)], "y")
    part = jnp.concatenate([in_part, out_part], axis=0)
    parts = [part] + [shift_by(part, "z", s) for s in SHIFTS]
    others = [shift_by(piece, "core", 1) for piece in parts]
    outs = [((width, units), F32), ((units, width), F32), ((shard_rows, width), F32)]
    operands = [*parts, *others]
    grad_w_in, grad_w_out, grad_rel = local_call(
        place_kernel,
        outs,
        [where, *operands],
        like(operands) + filled(outs) + [pltpu.VMEM((64, width), F32)],
        copies=12,
    )
    return (graph_out, grad_w_in, grad_w_out, grad_rel, grad_msg, grad_self)


def solution(mesh):
    fine = Mesh(mesh.devices.reshape(4, 2, 4, 4), ("z", "core", "x", "y"))
    every = ("z", "core", "x", "y")
    placed = (
        P(every, None, None),
        P(every),
        P(None, GROUP),
        P(GROUP, None),
        P(every, None),
        P(every, None),
        P(every, None),
        P(every, None),
        P(every, None),
        P(every, None),
        P(every, None),
        P(GROUP, None),
        P(),
        P(),
        P(every, None),
    )
    return jax.shard_map(
        shards,
        mesh=fine,
        in_specs=placed,
        out_specs=(
            P(every, None),
            P(None, GROUP),
            P(GROUP, None),
            P(GROUP, None),
            P(every, None),
            P(every, None),
        ),
        check_vma=False,
    )
```

```python
import jax
import jax.numpy as jnp
import numpy as np
from jax import lax
from jax.experimental import pallas as pl
from jax.experimental.pallas import tpu as pltpu
from jax.sharding import Mesh
from jax.sharding import PartitionSpec as P

BF = jnp.bfloat16
F32 = jnp.float32
I32 = jnp.int32
GROUP = ("x", "y")
SHIFTS = (1, 3, 2)
ORIGINS = (0, 3, 1, 2)
GELU_SCALE = float(np.sqrt(2.0 / np.pi))
GELU_CUBE = 0.044715


def shift_by(value, axis, shift):
    count = lax.axis_size(axis)
    return lax.ppermute(value, axis, [(i, (i + shift) % count) for i in range(count)])


def dot(a, b):
    return jnp.dot(a, b, preferred_element_type=F32)


def dot_t(a, b):
    return lax.dot_general(a, b, (((0,), (0,)), ((), ())), preferred_element_type=F32)


def dot_bt(a, b):
    return lax.dot_general(a, b, (((1,), (1,)), ((), ())), preferred_element_type=F32)


def one_hot(index, count):
    return (index[:, None] == jnp.arange(count, dtype=I32)[None, :]).astype(BF)


def one_hot_t(index, count):
    return (index[None, :] == jnp.arange(count, dtype=I32)[:, None]).astype(BF)


def lanes(shape):
    return lax.broadcasted_iota(I32, shape, 1)


def sublanes(shape):
    return lax.broadcasted_iota(I32, shape, 0)


def row_of(values, width):
    return jnp.pad(values.astype(BF), (0, width - values.shape[0]))[None, :]


def gather_ring(value, axis, cut):
    low, high = shift_by(value, axis, 1), shift_by(value, axis, 3)
    return [low, high, shift_by(low[:cut], axis, 1), shift_by(high[cut:], axis, 3)]


def reduce_ring(chunks, axis):
    total = chunks[0].astype(F32)
    for chunk, origin in zip(chunks[1:], ORIGINS[1:]):
        total = total + shift_by(chunk, axis, origin).astype(F32)
    return total.astype(BF)


def fresh_row(side, place):
    return (place % 4) * 16 + (side + 1) * 4 + place // 4


class Copies:
    def __init__(self, sems):
        self.sems, self.used = sems, 0

    def start(self, source, target):
        copy = pltpu.make_async_copy(source, target, self.sems.at[self.used])
        self.used += 1
        copy.start()
        return copy


def local_call(body, outs, operands, scratch=(), copies=8, flops=0, limit=60):
    def kernel(*refs):
        body(Copies(refs[-1]), *refs[:-1])

    return pl.pallas_call(
        kernel,
        out_shape=[jax.ShapeDtypeStruct(shape, kind) for shape, kind in outs],
        in_specs=[pl.BlockSpec(memory_space=pltpu.SMEM)]
        + [pl.BlockSpec(memory_space=pltpu.HBM)] * (len(operands) - 1),
        out_specs=[pl.BlockSpec(memory_space=pltpu.HBM)] * len(outs),
        scratch_shapes=[*scratch, pltpu.SemaphoreType.DMA((copies,))],
        compiler_params=pltpu.CompilerParams(vmem_limit_bytes=limit * 1024 * 1024),
        cost_estimate=pl.CostEstimate(flops=flops, bytes_accessed=1024 * 1024, transcendentals=0),
    )(*operands)


def like(arrays):
    return [pltpu.VMEM(array.shape, array.dtype) for array in arrays]


def filled(outs):
    return [pltpu.VMEM(shape, kind) for shape, kind in outs]


def wait_all(copies):
    for copy in copies:
        copy.wait()


def length_column(meta):
    shape = meta.shape
    return jnp.sum(jnp.where(lanes(shape) == sublanes(shape), meta, 0.0), axis=1, keepdims=True)


def pool_rows(length, tokens):
    shape = (16, tokens)
    line = lanes(shape)
    inside = (line // 16 == sublanes(shape)) & ((line % 16).astype(F32) < length)
    return inside.astype(F32).astype(BF)


def norm_kernel(
    copies,
    where_ref,
    hidden_hbm, lens_hbm, order_hbm, in_hbm, out_hbm, table_hbm,
    block_hbm, sum_hbm, weights_hbm,
    hidden_ref, lens_ref, order_ref,
    block_ref, sum_ref, weights_ref,
):
    core = where_ref[1]
    packed = []
    for i in range(2):
        cols, wide = pl.ds(i * 256, 256), pl.ds(i * 512, 512)
        source = in_hbm.at[pl.ds(pl.multiple_of(core * 512 + i * 256, 256), 256), :]
        packed.append(copies.start(source, weights_ref.at[pl.ds(0, 256), cols]))
        source = out_hbm.at[pl.ds(pl.multiple_of(core * 128, 128), 128), wide]
        packed.append(copies.start(source, weights_ref.at[pl.ds(256 + i * 128, 128), :]))
        source = table_hbm.at[pl.ds(pl.multiple_of(core * 32, 32), 32), wide]
        packed.append(copies.start(source, weights_ref.at[pl.ds(512 + i * 32, 32), :]))
    first = [
        copies.start(hidden_hbm, hidden_ref),
        copies.start(lens_hbm, lens_ref),
        copies.start(order_hbm, order_ref),
    ]
    wait_all(packed)
    later = [copies.start(weights_ref, weights_hbm)]
    wait_all(first)
    meta = jnp.zeros((16, 128), F32)
    for i, row in enumerate((lens_ref[...], order_ref[...])):
        values = jnp.broadcast_to(row.astype(F32), (16, 16)).astype(BF)
        select = (lanes((16, 128)) == sublanes((16, 128)) + 16 * i).astype(F32).astype(BF)
        meta = meta + dot(values, select)
    values = hidden_ref[...].astype(F32)
    center = values - jnp.mean(values, axis=-1, keepdims=True)
    spread = jnp.mean(center * center, axis=-1, keepdims=True)
    tokens = values.shape[0]
    block_ref[0:tokens, :] = (center * lax.rsqrt(spread + 1e-05)).astype(BF)
    block_ref[tokens : tokens + 16, :] = jnp.zeros((16, values.shape[1]), BF)
    block_ref[tokens : tokens + 16, 0:128] = meta.astype(BF)
    later.append(copies.start(block_ref, block_hbm))
    sum_ref[...] = dot(pool_rows(length_column(meta), tokens), hidden_ref[...])
    later.append(copies.start(sum_ref, sum_hbm))
    wait_all(later)


def encode_kernel(
    copies,
    where_ref,
    b0, b1, b2, b3_top, b3_rest,
    own_in, own_out, own_rel,
    m1, m2, m3_in, m3_rest,
    o1, o2, o3_in, o3_rest,
    hidden_sum_hbm, numbers_hbm,
    outgoing_hbm, normed_hbm, slope_hbm, pooled_hbm, all_out_hbm, route_hbm, length_hbm, rel_hot_hbm,
    outgoing_ref, normed_ref, slope_ref, pooled_ref, all_out_ref, route_ref, length_ref, rel_hot_ref,
    in_ref, pool_ref, rel_ref, meta_ref, hidden_sum_ref, numbers_ref,
):
    core, my_x, my_y = where_ref[1], where_ref[2], where_ref[3]
    metas, tokens, weights, tables = [], [], [[], [], [], []], []
    for s, (block, row) in enumerate(((b0, 256), (b1, 256), (b2, 256), (b3_rest, 128))):
        metas.append(copies.start(block.at[pl.ds(row, 16), pl.ds(0, 128)], meta_ref.at[s]))
    tables.append(copies.start(own_rel, rel_ref.at[pl.ds(0, 64), :]))
    tables.append(copies.start(numbers_hbm, numbers_ref))
    pieces = []
    for t, (mine, other) in enumerate(
        (((m1, m1, 256), (o1, o1, 256)), ((m2, m2, 256), (o2, o2, 256)), ((m3_in, m3_rest, 0), (o3_in, o3_rest, 0))), 1
    ):
        for (inner, rest, at), half in ((mine, core), (other, 1 - core)):
            pieces.append((t, inner, rest, at, half))
            for i in range(2):
                rows = pl.ds(pl.multiple_of(t * 64 + half * 32, 32), 32)
                target = rel_ref.at[rows, pl.ds(i * 512, 512)]
                tables.append(copies.start(rest.at[pl.ds(at + 256 + i * 32, 32), :], target))
    for s, (block, row, count) in enumerate(((b0, 0, 256), (b1, 256, 256), (b2, 512, 256), (b3_top, 768, 128), (b3_rest, 896, 128))):
        tokens.append(copies.start(block.at[pl.ds(0, count), :], normed_ref.at[pl.ds(row, count), :]))
    weights[0].append(copies.start(own_in, in_ref.at[:, pl.ds(0, 256)]))
    for t, inner, rest, at, half in pieces:
        for i in range(2):
            rows = pl.ds(pl.multiple_of(half * 512 + i * 256, 256), 256)
            target = in_ref.at[rows, pl.ds(t * 256, 256)]
            weights[t].append(copies.start(inner.at[pl.ds(0, 256), pl.ds(i * 256, 256)], target))
    outer = [
        copies.start(own_out, all_out_ref.at[pl.ds(0, 256), :]),
        copies.start(hidden_sum_hbm, hidden_sum_ref),
    ]
    for t, inner, rest, at, half in pieces:
        for i in range(2):
            rows = pl.ds(pl.multiple_of(t * 256 + half * 128, 128), 128)
            target = all_out_ref.at[rows, pl.ds(i * 512, 512)]
            outer.append(copies.start(rest.at[pl.ds(at + i * 128, 128), :], target))
    wait_all(metas)
    wait_all(tables)

    wide = (16, 256)
    slot = lanes(wide) % 16
    bound = lanes((128, 256))
    bound = (bound // 16 + (bound % 16) // 4 + 15) % 16
    bound_hot = (sublanes((128, 256)) == bound + 16).astype(F32).astype(BF)
    for s in range(4):
        meta = meta_ref[s]
        values = meta.astype(F32)
        length = length_column(values)
        length_ref[s * 16 : (s + 1) * 16, :] = jnp.broadcast_to(1.0 / length, (16, 128))
        pool_ref[s * 16 : (s + 1) * 16, :] = pool_rows(length, 256)
        sent = dot(meta, bound_hot)
        encoder = lax.rem(my_x + ORIGINS[s], 4)
        chosen = (sent == sublanes(wide).astype(F32)) & (slot % 4 == encoder) & (slot < 12)
        route_ref[s * 16 : (s + 1) * 16, :] = chosen.astype(F32).astype(BF)

    high = numbers_ref[...] // 32
    digits = (high.astype(F32).astype(BF), (numbers_ref[...] - 32 * high).astype(F32).astype(BF))
    tall, flat = (256, 128), (16, 256)
    chosen = lanes(tall) == sublanes(tall) % 16 - 12
    source_hot = (sublanes((256, 16)) // 16 == lanes((256, 16))).astype(F32).astype(BF)
    column = [jnp.sum(jnp.where(chosen, dot(source_hot, part), 0.0), axis=1, keepdims=True) for part in digits]
    line = lanes((256, 256))
    owner_y = (my_y + jnp.where(line < 64, 0, jnp.where(line < 128, 3, line // 64 - 1))) % 4
    name = ((my_x * 4 + owner_y) * 52 + line % 64).astype(F32)
    served = (name == 32.0 * column[0] + column[1]) & (line % 64 < 52) & (sublanes((256, 256)) % 16 >= 12)
    slot_hot = (sublanes((128, 256)) == lanes((128, 256)) % 16 - 12).astype(F32).astype(BF)
    own = sublanes(flat) == lanes(flat) // 16
    row = [jnp.sum(jnp.where(own, dot(part, slot_hot), 0.0), axis=0, keepdims=True) for part in digits]
    line = sublanes((512, 256))
    local = (line // 64) % 2 * 32 + (line // 16) % 4 * 8 + line % 16
    name = ((my_x * 4 + line // 128) * 52 + local).astype(F32)
    good = (line % 16 < 8) & (local < 52) & (lanes((512, 256)) % 16 >= 12)
    rel_hot_ref[...] = ((name == 32.0 * row[0] + row[1]) & good).astype(F32).astype(BF)
    relations = dot(served.astype(F32).astype(BF), rel_ref[...])

    sent_out = [
        copies.start(route_ref, route_hbm),
        copies.start(length_ref, length_hbm),
        copies.start(rel_hot_ref, rel_hot_hbm),
    ]
    wait_all(tokens)
    sent_out.append(copies.start(normed_ref, normed_hbm))
    for t in range(4):
        cols = slice(t * 256, (t + 1) * 256)
        wait_all(weights[t])

        @pl.loop(0, 2)
        def _(s):
            rows = pl.ds(pl.multiple_of(s * 512, 512), 512)
            pre = dot(normed_ref[rows, :], in_ref[:, cols])
            square = pre * pre
            tanh = jnp.tanh(GELU_SCALE * pre * (1.0 + GELU_CUBE * square))
            upper = 0.5 + 0.5 * tanh
            slope = upper + (0.5 * GELU_SCALE) * pre * (1.0 - tanh * tanh) * (1.0 + 3.0 * GELU_CUBE * square)
            slope_ref[rows, cols] = slope.astype(BF)
            activation = (pre * upper).astype(BF)
            for i in range(2):
                few = pl.ds(pl.multiple_of(s * 32 + i * 16, 16), 16)
                pooled = dot(pool_ref[few, :], activation[i * 256 : (i + 1) * 256])
                pooled_ref[few, cols] = pooled.astype(BF)

    sent_out.append(copies.start(slope_ref, slope_hbm))
    sent_out.append(copies.start(pooled_ref, pooled_hbm))
    wait_all(outer)
    sent_out.append(copies.start(all_out_ref, all_out_hbm))
    partial = dot(pooled_ref[...], all_out_ref[...])
    partial = jnp.concatenate([partial[0:16] + hidden_sum_ref[...], partial[16:64]], axis=0)
    partial = (partial * length_ref[:, 0:1]).astype(BF)
    outgoing_ref[...] = (dot_t(route_ref[...], partial) + relations).astype(BF)
    sent_out.append(copies.start(outgoing_ref, outgoing_hbm))
    wait_all(sent_out)


def graph_kernel(
    copies,
    where_ref,
    arrived_hbm, own_hot_t_hbm,
    src_hot_hbm, dst_hot_hbm, dst_hot_t_hbm,
    w_msg_hbm, w_self_hbm, d_out_hbm,
    cache_hbm, low_hbm, high_hbm,
    table_out_hbm, graph_out_hbm, aggregate_hbm, nodes_hbm, pre_hbm,
    arrived_ref, own_hot_t_ref,
    src_hot_ref, dst_hot_ref, dst_hot_t_ref,
    w_msg_ref, w_self_ref, d_out_ref,
    table_out_ref, graph_out_ref, aggregate_ref, nodes_ref, pre_ref,
    base_ref, places_ref, row_hot_t_ref, src_row_hot_ref,
    ext_ref, sources_ref, edges_ref, agg_grad_ref, sums_ref, rel_ref, blocks_ref,
):
    scale = (256 / 2048) ** 0.5
    first = [
        copies.start(low_hbm.at[pl.ds(64, 16), pl.ds(0, 128)], places_ref.at[0]),
        copies.start(high_hbm.at[pl.ds(64, 16), pl.ds(0, 128)], places_ref.at[1]),
        copies.start(own_hot_t_hbm, own_hot_t_ref),
        copies.start(arrived_hbm, arrived_ref),
        copies.start(cache_hbm, base_ref.at[pl.ds(16, 240), :]),
        copies.start(low_hbm.at[pl.ds(0, 64), :], base_ref.at[pl.ds(256, 64), :]),
        copies.start(high_hbm.at[pl.ds(0, 64), :], base_ref.at[pl.ds(320, 64), :]),
        copies.start(src_hot_hbm, src_hot_ref),
    ]
    second = [copies.start(dst_hot_t_hbm, dst_hot_t_ref)]
    third = [
        copies.start(w_msg_hbm, w_msg_ref),
        copies.start(w_self_hbm, w_self_ref),
        copies.start(d_out_hbm, d_out_ref),
    ]
    fourth = [copies.start(dst_hot_hbm, dst_hot_ref)]
    base_ref[0:16, :] = jnp.zeros((16, 1024), BF)
    wait_all(first)
    to = lanes((128, 128)) - sublanes((128, 128))
    inside = sublanes((128, 128)) < 64
    low_move = ((to == 0) & inside).astype(F32).astype(BF)
    high_move = ((to == 64) & inside).astype(F32).astype(BF)
    places = (dot(places_ref[0], low_move) + dot(places_ref[1], high_move))[0:1].astype(I32)
    upper = (lax.broadcasted_iota(I32, (1, 128), 1) >= 64).astype(I32)
    table_row = jnp.where(places < 16, (places % 4) * 16 + upper * 8 + places // 4, -1)
    row_hot_t_ref[:, 0:256] = own_hot_t_ref[...]
    row_hot_t_ref[:, 256:384] = (sublanes((64, 128)) == table_row).astype(F32).astype(BF)
    src_row_hot_ref[...] = dot_bt(row_hot_t_ref[...], src_hot_ref[...]).astype(BF)
    total = arrived_ref[0:64, :].astype(F32)
    for i in range(1, 4):
        total = total + arrived_ref[i * 64 : (i + 1) * 64, :].astype(F32)
    for j in range(16):
        at = j // 4 * 16 + 12 + j % 4
        rel_ref[j] = total[at : at + 1]
    table = total.astype(BF)
    ext_ref[...] = (base_ref[...].astype(F32) + dot_t(row_hot_t_ref[...], table)).astype(BF)
    nodes_ref[...] = ext_ref[0:256, :]
    sent_out = [copies.start(nodes_ref, nodes_hbm)]

    for n in range(4):
        cols = slice(n * 256, (n + 1) * 256)

        @pl.loop(0, 4)
        def _(k):
            rows = pl.ds(pl.multiple_of(k * 512, 512), 512)
            taken = dot(src_hot_ref[rows, :], ext_ref[:, cols])
            taken = taken.astype(BF)
            sources_ref[rows, cols] = taken
            for i in range(4):
                few = pl.ds(pl.multiple_of(k * 512 + i * 128, 128), 128)
                edges_ref[few, cols] = taken[i * 128 : (i + 1) * 128] * rel_ref[k * 4 + i, :, cols].astype(BF)

    wait_all(second)

    @pl.loop(0, 4)
    def _(n):
        cols = pl.ds(pl.multiple_of(n * 256, 256), 256)
        aggregate_ref[:, cols] = (scale * dot(dst_hot_t_ref[...], edges_ref[:, cols])).astype(BF)

    sent_out.append(copies.start(aggregate_ref, aggregate_hbm))
    wait_all(third)

    @pl.loop(0, 4)
    def _(n):
        cols = pl.ds(pl.multiple_of(n * 256, 256), 256)
        out_pre = dot(aggregate_ref[...], w_msg_ref[:, cols]) + dot(nodes_ref[...], w_self_ref[:, cols])
        squashed = jnp.tanh(out_pre)
        graph_out_ref[:, cols] = squashed.astype(BF)
        pre_ref[:, cols] = (d_out_ref[:, cols].astype(F32) * (1.0 - squashed * squashed)).astype(BF)

    sent_out.append(copies.start(graph_out_ref, graph_out_hbm))
    sent_out.append(copies.start(pre_ref, pre_hbm))

    @pl.loop(0, 4)
    def _(n):
        cols = pl.ds(pl.multiple_of(n * 256, 256), 256)
        agg_grad_ref[:, cols] = (scale * dot_bt(pre_ref[...], w_msg_ref[cols, :])).astype(BF)

    wait_all(fourth)

    for n in range(4):
        cols = slice(n * 256, (n + 1) * 256)

        @pl.loop(0, 4)
        def _(k):
            rows = pl.ds(pl.multiple_of(k * 512, 512), 512)
            at_dest = dot(dst_hot_ref[rows, :], agg_grad_ref[:, cols])
            for i in range(4):
                few = pl.ds(pl.multiple_of(k * 512 + i * 128, 128), 128)
                part = at_dest[i * 128 : (i + 1) * 128]
                edges_ref[few, cols] = part.astype(BF) * rel_ref[k * 4 + i, :, cols].astype(BF)
                product = part * sources_ref[few, cols].astype(F32)
                sums_ref[k * 4 + i, :, cols] = jnp.sum(product, axis=0, keepdims=True)

    blocks_ref[...] = jnp.concatenate([sums_ref[j] for j in range(16)], axis=0).astype(BF)
    block = lanes((64, 16))
    block_hot = (sublanes((64, 16)) == block // 4 * 16 + 12 + block % 4).astype(F32).astype(BF)
    own_pre = dot(own_hot_t_ref[...], pre_ref[...]).astype(BF)

    @pl.loop(0, 4)
    def _(n):
        cols = pl.ds(pl.multiple_of(n * 256, 256), 256)
        grad = dot(src_row_hot_ref[...], edges_ref[:, cols]) + dot_bt(own_pre, w_self_ref[cols, :])
        grad = grad + dot(block_hot, blocks_ref[:, cols])
        table_out_ref[:, cols] = grad.astype(BF)

    for x in range(4):
        sent_out.append(copies.start(table_out_ref, table_out_hbm.at[pl.ds(x * 64, 64), :]))
    wait_all(sent_out)


def weight_kernel(
    copies,
    where_ref,
    aggregate_hbm, nodes_hbm, pre_hbm,
    kept_hbm, given_hbm,
    aggregate_ref, nodes_ref, pre_ref,
    kept_ref, given_ref,
):
    core = where_ref[1]
    wait_all(
        [copies.start(aggregate_hbm, aggregate_ref), copies.start(nodes_hbm, nodes_ref), copies.start(pre_hbm, pre_ref)]
    )
    sent_out = []
    for half, chunk_ref, chunk_hbm in ((1 - core, given_ref, given_hbm), (core, kept_ref, kept_hbm)):

        @pl.loop(0, 4)
        def _(z):
            rows = pl.ds(pl.multiple_of(z * 256 + half * 128, 128), 128)
            msg = dot_t(aggregate_ref[:, rows], pre_ref[...])
            own = dot_t(nodes_ref[:, rows], pre_ref[...])
            for x in range(4):
                for y in range(4):
                    at = (x * 4 + y) * 8
                    both = jnp.concatenate([msg[at : at + 8], own[at : at + 8]], axis=0)
                    chunk_ref[z * 16 + x * 4 + y] = both.astype(BF)

        sent_out.append(copies.start(chunk_ref, chunk_hbm))
    wait_all(sent_out)


def ring_places(mine):
    places = []
    for at in range(4):
        ahead = lax.rem(at - mine + 4, 4)
        places.append(jnp.where(ahead == 0, 0, jnp.where(ahead == 3, 1, ahead + 1)))
    return places


def back_kernel(
    copies,
    where_ref,
    returned_hbm, route_hbm, length_hbm, rel_hot_hbm, pooled_hbm, all_out_hbm, slope_hbm, normed_t_hbm,
    given_hbm, kept_hbm,
    returned_ref, route_ref, length_ref, rel_hot_ref, pooled_ref, all_out_ref, slope_ref, normed_t_ref,
    given_ref, kept_ref,
    scaled_ref, grad_ref,
):
    my_z, core, my_y = where_ref[0], where_ref[1], where_ref[3]
    first = [
        copies.start(returned_hbm, returned_ref),
        copies.start(route_hbm, route_ref),
        copies.start(length_hbm, length_ref),
        copies.start(rel_hot_hbm, rel_hot_ref),
        copies.start(pooled_hbm, pooled_ref),
    ]
    second = [copies.start(all_out_hbm, all_out_ref), copies.start(slope_hbm, slope_ref)]
    third = [copies.start(normed_t_hbm, normed_t_ref)]
    places = ring_places(my_z)
    pools = []
    wait_all(first)
    scaled_ref[...] = (dot(route_ref[...], returned_ref[...]) * length_ref[:, 0:1]).astype(BF)
    for s in range(4):
        line = lanes((16, 256))
        length = 1.0 / length_ref[s * 16 : (s + 1) * 16, 0:1]
        inside = (line // 16 == sublanes((16, 256))) & ((line % 16).astype(F32) + 0.5 < length)
        pools.append(inside.astype(F32).astype(BF))
    wait_all(second)

    @pl.loop(0, 4)
    def _(t):
        cols = pl.ds(pl.multiple_of(t * 256, 256), 256)
        upstream = dot_bt(scaled_ref[...], all_out_ref[cols, :]).astype(BF)
        for s in range(4):
            rows = slice(s * 256, (s + 1) * 256)
            at_tokens = dot_t(pools[s], upstream[s * 16 : (s + 1) * 16])
            grad_ref[rows, cols] = (slope_ref[rows, cols].astype(F32) * at_tokens).astype(BF)

    wait_all(third)
    sent_out = []
    for half, chunk_ref, chunk_hbm in ((1 - core, given_ref, given_hbm), (core, kept_ref, kept_hbm)):

        @pl.loop(0, 4)
        def _(t):
            cols = pl.ds(pl.multiple_of(t * 256, 256), 256)
            origin = jnp.where(t == 0, 0, jnp.where(t == 1, 3, t - 1))
            owner = lax.rem(my_y + origin, 4)
            units = pl.ds(pl.multiple_of(t * 256 + half * 128, 128), 128)
            out = dot_t(pooled_ref[:, units], scaled_ref[...]).astype(BF)
            rel_rows = pl.ds(pl.multiple_of(owner * 128 + half * 64, 64), 64)
            rel = dot(rel_hot_ref[rel_rows, :], returned_ref[...]).astype(BF)
            inner = dot(normed_t_ref[pl.ds(pl.multiple_of(half * 512, 512), 512), :], grad_ref[:, cols]).astype(BF)
            for z in range(4):
                chunk_ref[t, places[z], 32:64, :] = out[z * 32 : (z + 1) * 32]
                chunk_ref[t, places[z], 64:80, :] = rel[z * 16 : (z + 1) * 16]
                for i in range(4):
                    piece = inner[z * 128 + i * 32 : z * 128 + (i + 1) * 32]
                    chunk_ref[t, places[z], 0:32, i * 256 : (i + 1) * 256] = piece

        sent_out.append(copies.start(chunk_ref, chunk_hbm))
    wait_all(sent_out)


def place_kernel(
    copies,
    where_ref,
    h0, h1, h2, h3, h4, h5, h6, h7,
    in_hbm, out_hbm, rel_hbm,
    a0, a1, a2, a3, c0, c1, c2, c3,
    in_ref, out_ref, owned_ref, rel_ref,
):
    sources = (h0, h1, h2, h3, h4, h5, h6, h7)
    targets = (a0, a1, a2, a3, c0, c1, c2, c3)
    wait_all([copies.start(source, target) for source, target in zip(sources, targets)])
    my_z, core = where_ref[0], where_ref[1]
    for pieces, half in (((a0, a1, a2, a3), core), ((c0, c1, c2, c3), 1 - core)):
        for piece, origin in zip(pieces, ORIGINS):
            z = lax.rem(my_z + origin, 4)
            values = piece[...].astype(F32)
            for i in range(4):
                rows = pl.ds(pl.multiple_of(half * 512 + z * 128 + i * 32, 32), 32)
                in_ref[rows, :] = values[0:32, i * 256 : (i + 1) * 256]
            out_ref[pl.ds(pl.multiple_of(half * 128 + z * 32, 32), 32), :] = values[32:64]
            rel_ref[pl.ds(pl.multiple_of(half * 32 + z * 8, 8), 8), :] = values[64:72]
    owned_ref[...] = rel_ref[0:52, :]
    wait_all([copies.start(in_ref, in_hbm), copies.start(out_ref, out_hbm), copies.start(owned_ref, rel_hbm)])


def shards(
    hidden,
    desc_len,
    w_in,
    w_out,
    send_order,
    place_order,
    cache,
    halo_rows,
    edge_src,
    edge_dst,
    edge_rel,
    rel_table,
    w_msg,
    w_self,
    d_out,
):
    entities, length, width = hidden.shape
    tokens = entities * length
    units = w_in.shape[1]
    my_core = lax.axis_index("core")
    where = jnp.stack([lax.axis_index(name) for name in ("z", "core", "x", "y")]).astype(I32)
    src, dst, rel = edge_src[0], edge_dst[0], edge_rel[0]
    shard_rows = rel_table.shape[0]

    numbers = jnp.broadcast_to(rel.reshape(1, 4, 4), (4, 4, 4)).reshape(16, 4)
    numbers = lax.all_to_all(jnp.pad(numbers, ((0, 0), (0, 124))), GROUP, 0, 0, tiled=True)

    rel_pad = jnp.pad(rel_table, ((0, 64 - shard_rows), (0, 0)))
    operands = [hidden.reshape(tokens, width), desc_len[None, :], send_order]
    outs = [((tokens + 16, width), BF), ((entities, width), F32), ((576, 512), BF)]
    block, hidden_sum, weights = local_call(
        norm_kernel,
        outs,
        [where, *operands, w_in, w_out, rel_pad],
        like(operands) + filled(outs),
        copies=14,
    )
    blocks = [block, *gather_ring(block, "x", 128)]
    mine = gather_ring(weights, "y", 256)
    other = [shift_by(part, "core", 1) for part in mine]

    outs = [
        ((256, width), BF),
        ((4 * tokens, width), BF),
        ((4 * tokens, 4 * units), BF),
        ((4 * entities, 4 * units), BF),
        ((4 * units, width), BF),
        ((4 * entities, 256), BF),
        ((4 * entities, 128), F32),
        ((512, 256), BF),
    ]
    outgoing, normed, slope, pooled, all_out, route, inverse, rel_hot = local_call(
        encode_kernel,
        outs,
        [where, *blocks, w_in, w_out, rel_pad, *mine, *other, hidden_sum, numbers],
        filled(outs)
        + [
            pltpu.VMEM((width, 4 * units), BF),
            pltpu.VMEM((4 * entities, tokens), BF),
            pltpu.VMEM((256, width), BF),
            pltpu.VMEM((4, 16, 128), BF),
            pltpu.VMEM((entities, width), F32),
            pltpu.VMEM((16, 128), I32),
        ],
        copies=64,
        flops=2 * 4 * tokens * width * 4 * units,
    )

    halo = halo_rows[0]
    place = place_order[0]
    side = halo.shape[0] // 2
    cache_count = cache.shape[0]
    boundary = dot(one_hot(halo - entities, cache_count), cache).astype(BF)
    halo_hot = halo[:, None] == jnp.arange(entities, dtype=I32)[None, :]
    halo_place = jnp.where(halo < entities, jnp.sum(jnp.where(halo_hot, place[None, :], 0), axis=1), 16)

    def edge_of(rows, places):
        return jnp.concatenate([rows, jnp.pad(row_of(places, width), ((0, 15), (0, 0)))], axis=0)

    to_high, to_low = edge_of(boundary[side:], halo_place[side:]), edge_of(boundary[:side], halo_place[:side])
    to_high, to_low, outgoing = lax.optimization_barrier((to_high, to_low, outgoing))
    from_low = shift_by(to_high, GROUP, 1)
    from_high = shift_by(to_low, GROUP, 15)
    own_row = jnp.concatenate([fresh_row(0, place), jnp.full((cache_count,), -1, I32)])
    node_count = entities + cache_count
    extended_count = node_count + 2 * side
    edge_count = src.shape[0]
    block_count = rel.shape[0]
    src_hot = one_hot(src, extended_count)
    arrived = lax.all_to_all(outgoing.reshape(16, 16, width), GROUP, 0, 0, tiled=True).reshape(256, width)
    arrived, normed_t = lax.optimization_barrier((arrived, normed.T))

    outs = [((256, width), BF)] + [((node_count, width), BF)] * 4
    operands = [
        arrived,
        one_hot_t(own_row, 64),
        src_hot,
        one_hot(dst, node_count),
        one_hot_t(dst, node_count),
        w_msg,
        w_self,
        d_out,
    ]
    grad_table, graph_out, aggregate, nodes, grad_pre = local_call(
        graph_kernel,
        outs,
        [where, *operands, cache, from_low, from_high],
        like(operands)
        + filled([((64, width), BF), *outs[1:]])
        + [
            pltpu.VMEM((extended_count, width), BF),
            pltpu.VMEM((2, 16, 128), BF),
            pltpu.VMEM((64, extended_count), BF),
            pltpu.VMEM((64, edge_count), BF),
            pltpu.VMEM((extended_count, width), BF),
            pltpu.VMEM((edge_count, width), BF),
            pltpu.VMEM((edge_count, width), BF),
            pltpu.VMEM((node_count, width), BF),
            pltpu.VMEM((block_count, 1, width), F32),
            pltpu.VMEM((block_count, 1, width), F32),
            pltpu.VMEM((block_count, width), BF),
        ],
        copies=30,
        flops=6 * 10**9,
    )

    returned = lax.all_to_all(grad_table.reshape(16, 16, width), GROUP, 0, 0, tiled=True).reshape(256, width)

    outs = [((64, 16, width), BF)] * 2
    operands = [aggregate, nodes, grad_pre]
    graph_kept, graph_given = local_call(
        weight_kernel, outs, [where, *operands], like(operands) + filled(outs), flops=10**9
    )
    returned, graph_kept, graph_given = lax.optimization_barrier((returned, graph_kept, graph_given))
    chip = (graph_kept.astype(F32) + shift_by(graph_given, "core", 1).astype(F32)).astype(BF)
    plane = lax.all_to_all(chip, ("z", "x", "y"), 0, 0, tiled=True)
    weight_rows = jnp.sum(plane.astype(F32), axis=0)
    grad_msg, grad_self = weight_rows[:8], weight_rows[8:]

    outs = [((4, 4, 80, width), BF)] * 2
    operands = [returned, route, inverse, rel_hot, pooled, all_out, slope, normed_t]
    given, kept = local_call(
        back_kernel,
        outs,
        [where, *operands],
        like(operands)
        + filled(outs)
        + [pltpu.VMEM((4 * entities, width), BF), pltpu.VMEM((4 * tokens, 4 * units), BF)],
        copies=12,
        flops=2 * 4 * tokens * width * 4 * units,
    )
    mixed = (kept.astype(F32) + shift_by(given, "core", 1).astype(F32)).astype(BF)
    part = reduce_ring([mixed[i].reshape(320, width) for i in range(4)], "y").reshape(4, 80, width)
    part = reduce_ring([part[i] for i in range(4)], "z")
    parts = [part] + [shift_by(part, "z", s) for s in SHIFTS]
    others = [shift_by(piece, "core", 1) for piece in parts]
    outs = [((width, units), F32), ((units, width), F32), ((shard_rows, width), F32)]
    operands = [*parts, *others]
    grad_w_in, grad_w_out, grad_rel = local_call(
        place_kernel,
        outs,
        [where, *operands],
        like(operands) + filled(outs) + [pltpu.VMEM((64, width), F32)],
        copies=12,
    )
    return (graph_out, grad_w_in, grad_w_out, grad_rel, grad_msg, grad_self)


def solution(mesh):
    fine = Mesh(mesh.devices.reshape(4, 2, 4, 4), ("z", "core", "x", "y"))
    every = ("z", "core", "x", "y")
    placed = (
        P(every, None, None),
        P(every),
        P(None, GROUP),
        P(GROUP, None),
        P(every, None),
        P(every, None),
        P(every, None),
        P(every, None),
        P(every, None),
        P(every, None),
        P(every, None),
        P(GROUP, None),
        P(),
        P(),
        P(every, None),
    )
    return jax.shard_map(
        shards,
        mesh=fine,
        in_specs=placed,
        out_specs=(
            P(every, None),
            P(None, GROUP),
            P(GROUP, None),
            P(GROUP, None),
            P(every, None),
            P(every, None),
        ),
        check_vma=False,
    )
```

```python
import jax
import jax.numpy as jnp
import numpy as np
from jax import lax
from jax.experimental import pallas as pl
from jax.experimental.pallas import tpu as pltpu
from jax.sharding import Mesh
from jax.sharding import PartitionSpec as P

BF = jnp.bfloat16
F32 = jnp.float32
I32 = jnp.int32
GROUP = ("x", "y")
SHIFTS = (1, 3, 2)
ORIGINS = (0, 3, 1, 2)
GELU_SCALE = float(np.sqrt(2.0 / np.pi))
GELU_CUBE = 0.044715


def shift_by(value, axis, shift):
    count = lax.axis_size(axis)
    return lax.ppermute(value, axis, [(i, (i + shift) % count) for i in range(count)])


def dot(a, b):
    return jnp.dot(a, b, preferred_element_type=F32)


def dot_t(a, b):
    return lax.dot_general(a, b, (((0,), (0,)), ((), ())), preferred_element_type=F32)


def dot_bt(a, b):
    return lax.dot_general(a, b, (((1,), (1,)), ((), ())), preferred_element_type=F32)


def one_hot(index, count):
    return (index[:, None] == jnp.arange(count, dtype=I32)[None, :]).astype(BF)


def one_hot_t(index, count):
    return (index[None, :] == jnp.arange(count, dtype=I32)[:, None]).astype(BF)


def lanes(shape):
    return lax.broadcasted_iota(I32, shape, 1)


def sublanes(shape):
    return lax.broadcasted_iota(I32, shape, 0)


def row_of(values, width):
    return jnp.pad(values.astype(BF), (0, width - values.shape[0]))[None, :]


def gather_ring(value, axis, cut):
    low, high = shift_by(value, axis, 1), shift_by(value, axis, 3)
    return [low, high, shift_by(low[:cut], axis, 1), shift_by(high[cut:], axis, 3)]


def reduce_ring(chunks, axis):
    total = chunks[0].astype(F32)
    for chunk, origin in zip(chunks[1:], ORIGINS[1:]):
        total = total + shift_by(chunk, axis, origin).astype(F32)
    return total.astype(BF)


def fresh_row(side, place):
    return (place % 4) * 16 + (side + 1) * 4 + place // 4


class Copies:
    def __init__(self, sems):
        self.sems, self.used = sems, 0

    def start(self, source, target):
        copy = pltpu.make_async_copy(source, target, self.sems.at[self.used])
        self.used += 1
        copy.start()
        return copy


def local_call(body, outs, operands, scratch=(), copies=8, flops=0, limit=60):
    def kernel(*refs):
        body(Copies(refs[-1]), *refs[:-1])

    return pl.pallas_call(
        kernel,
        out_shape=[jax.ShapeDtypeStruct(shape, kind) for shape, kind in outs],
        in_specs=[pl.BlockSpec(memory_space=pltpu.SMEM)]
        + [pl.BlockSpec(memory_space=pltpu.HBM)] * (len(operands) - 1),
        out_specs=[pl.BlockSpec(memory_space=pltpu.HBM)] * len(outs),
        scratch_shapes=[*scratch, pltpu.SemaphoreType.DMA((copies,))],
        compiler_params=pltpu.CompilerParams(vmem_limit_bytes=limit * 1024 * 1024),
        cost_estimate=pl.CostEstimate(flops=flops, bytes_accessed=1024 * 1024, transcendentals=0),
    )(*operands)


def like(arrays):
    return [pltpu.VMEM(array.shape, array.dtype) for array in arrays]


def filled(outs):
    return [pltpu.VMEM(shape, kind) for shape, kind in outs]


def wait_all(copies):
    for copy in copies:
        copy.wait()


def length_column(meta):
    shape = meta.shape
    return jnp.sum(jnp.where(lanes(shape) == sublanes(shape), meta, 0.0), axis=1, keepdims=True)


def pool_rows(length, tokens):
    shape = (16, tokens)
    line = lanes(shape)
    inside = (line // 16 == sublanes(shape)) & ((line % 16).astype(F32) < length)
    return inside.astype(F32).astype(BF)


def norm_kernel(
    copies,
    where_ref,
    hidden_hbm, lens_hbm, order_hbm, in_hbm, out_hbm, table_hbm,
    block_hbm, sum_hbm, weights_hbm,
    hidden_ref, lens_ref, order_ref,
    block_ref, sum_ref, weights_ref,
):
    core = where_ref[1]
    packed = []
    for i in range(2):
        cols, wide = pl.ds(i * 256, 256), pl.ds(i * 512, 512)
        source = in_hbm.at[pl.ds(pl.multiple_of(core * 512 + i * 256, 256), 256), :]
        packed.append(copies.start(source, weights_ref.at[pl.ds(0, 256), cols]))
        source = out_hbm.at[pl.ds(pl.multiple_of(core * 128, 128), 128), wide]
        packed.append(copies.start(source, weights_ref.at[pl.ds(256 + i * 128, 128), :]))
        source = table_hbm.at[pl.ds(pl.multiple_of(core * 32, 32), 32), wide]
        packed.append(copies.start(source, weights_ref.at[pl.ds(512 + i * 32, 32), :]))
    first = [
        copies.start(hidden_hbm, hidden_ref),
        copies.start(lens_hbm, lens_ref),
        copies.start(order_hbm, order_ref),
    ]
    wait_all(packed)
    later = [copies.start(weights_ref, weights_hbm)]
    wait_all(first)
    meta = jnp.zeros((16, 128), F32)
    for i, row in enumerate((lens_ref[...], order_ref[...])):
        values = jnp.broadcast_to(row.astype(F32), (16, 16)).astype(BF)
        select = (lanes((16, 128)) == sublanes((16, 128)) + 16 * i).astype(F32).astype(BF)
        meta = meta + dot(values, select)
    values = hidden_ref[...].astype(F32)
    center = values - jnp.mean(values, axis=-1, keepdims=True)
    spread = jnp.mean(center * center, axis=-1, keepdims=True)
    tokens = values.shape[0]
    block_ref[0:tokens, :] = (center * lax.rsqrt(spread + 1e-05)).astype(BF)
    block_ref[tokens : tokens + 16, :] = jnp.zeros((16, values.shape[1]), BF)
    block_ref[tokens : tokens + 16, 0:128] = meta.astype(BF)
    later.append(copies.start(block_ref, block_hbm))
    sum_ref[...] = dot(pool_rows(length_column(meta), tokens), hidden_ref[...])
    later.append(copies.start(sum_ref, sum_hbm))
    wait_all(later)


def encode_kernel(
    copies,
    where_ref,
    b0, b1, b2, b3_top, b3_rest,
    own_in, own_out, own_rel,
    m1, m2, m3_in, m3_rest,
    o1, o2, o3_in, o3_rest,
    hidden_sum_hbm, numbers_hbm,
    outgoing_hbm, normed_hbm, slope_hbm, pooled_hbm, all_out_hbm, route_hbm, length_hbm, rel_hot_hbm,
    outgoing_ref, normed_ref, slope_ref, pooled_ref, all_out_ref, route_ref, length_ref, rel_hot_ref,
    in_ref, pool_ref, rel_ref, meta_ref, hidden_sum_ref, numbers_ref,
):
    core, my_x, my_y = where_ref[1], where_ref[2], where_ref[3]
    metas, tokens, weights, tables = [], [], [[], [], [], []], []
    for s, (block, row) in enumerate(((b0, 256), (b1, 256), (b2, 256), (b3_rest, 128))):
        metas.append(copies.start(block.at[pl.ds(row, 16), pl.ds(0, 128)], meta_ref.at[s]))
    tables.append(copies.start(own_rel, rel_ref.at[pl.ds(0, 64), :]))
    tables.append(copies.start(numbers_hbm, numbers_ref))
    pieces = []
    for t, (mine, other) in enumerate(
        (((m1, m1, 256), (o1, o1, 256)), ((m2, m2, 256), (o2, o2, 256)), ((m3_in, m3_rest, 0), (o3_in, o3_rest, 0))), 1
    ):
        for (inner, rest, at), half in ((mine, core), (other, 1 - core)):
            pieces.append((t, inner, rest, at, half))
            for i in range(2):
                rows = pl.ds(pl.multiple_of(t * 64 + half * 32, 32), 32)
                target = rel_ref.at[rows, pl.ds(i * 512, 512)]
                tables.append(copies.start(rest.at[pl.ds(at + 256 + i * 32, 32), :], target))
    for s, (block, row, count) in enumerate(((b0, 0, 256), (b1, 256, 256), (b2, 512, 256), (b3_top, 768, 128), (b3_rest, 896, 128))):
        tokens.append(copies.start(block.at[pl.ds(0, count), :], normed_ref.at[pl.ds(row, count), :]))
    weights[0].append(copies.start(own_in, in_ref.at[:, pl.ds(0, 256)]))
    for t, inner, rest, at, half in pieces:
        for i in range(2):
            rows = pl.ds(pl.multiple_of(half * 512 + i * 256, 256), 256)
            target = in_ref.at[rows, pl.ds(t * 256, 256)]
            weights[t].append(copies.start(inner.at[pl.ds(0, 256), pl.ds(i * 256, 256)], target))
    outer = [
        copies.start(own_out, all_out_ref.at[pl.ds(0, 256), :]),
        copies.start(hidden_sum_hbm, hidden_sum_ref),
    ]
    for t, inner, rest, at, half in pieces:
        for i in range(2):
            rows = pl.ds(pl.multiple_of(t * 256 + half * 128, 128), 128)
            target = all_out_ref.at[rows, pl.ds(i * 512, 512)]
            outer.append(copies.start(rest.at[pl.ds(at + i * 128, 128), :], target))
    wait_all(metas)
    wait_all(tables)

    wide = (16, 256)
    slot = lanes(wide) % 16
    bound = lanes((128, 256))
    bound = (bound // 16 + (bound % 16) // 4 + 15) % 16
    bound_hot = (sublanes((128, 256)) == bound + 16).astype(F32).astype(BF)
    for s in range(4):
        meta = meta_ref[s]
        values = meta.astype(F32)
        length = length_column(values)
        length_ref[s * 16 : (s + 1) * 16, :] = jnp.broadcast_to(1.0 / length, (16, 128))
        pool_ref[s * 16 : (s + 1) * 16, :] = pool_rows(length, 256)
        sent = dot(meta, bound_hot)
        encoder = lax.rem(my_x + ORIGINS[s], 4)
        chosen = (sent == sublanes(wide).astype(F32)) & (slot % 4 == encoder) & (slot < 12)
        route_ref[s * 16 : (s + 1) * 16, :] = chosen.astype(F32).astype(BF)

    high = numbers_ref[...] // 32
    digits = (high.astype(F32).astype(BF), (numbers_ref[...] - 32 * high).astype(F32).astype(BF))
    tall, flat = (256, 128), (16, 256)
    chosen = lanes(tall) == sublanes(tall) % 16 - 12
    source_hot = (sublanes((256, 16)) // 16 == lanes((256, 16))).astype(F32).astype(BF)
    column = [jnp.sum(jnp.where(chosen, dot(source_hot, part), 0.0), axis=1, keepdims=True) for part in digits]
    line = lanes((256, 256))
    owner_y = (my_y + jnp.where(line < 64, 0, jnp.where(line < 128, 3, line // 64 - 1))) % 4
    name = ((my_x * 4 + owner_y) * 52 + line % 64).astype(F32)
    served = (name == 32.0 * column[0] + column[1]) & (line % 64 < 52) & (sublanes((256, 256)) % 16 >= 12)
    slot_hot = (sublanes((128, 256)) == lanes((128, 256)) % 16 - 12).astype(F32).astype(BF)
    own = sublanes(flat) == lanes(flat) // 16
    row = [jnp.sum(jnp.where(own, dot(part, slot_hot), 0.0), axis=0, keepdims=True) for part in digits]
    line = sublanes((512, 256))
    local = (line // 64) % 2 * 32 + (line // 16) % 4 * 8 + line % 16
    name = ((my_x * 4 + line // 128) * 52 + local).astype(F32)
    good = (line % 16 < 8) & (local < 52) & (lanes((512, 256)) % 16 >= 12)
    rel_hot_ref[...] = ((name == 32.0 * row[0] + row[1]) & good).astype(F32).astype(BF)
    relations = dot(served.astype(F32).astype(BF), rel_ref[...])

    sent_out = [
        copies.start(route_ref, route_hbm),
        copies.start(length_ref, length_hbm),
        copies.start(rel_hot_ref, rel_hot_hbm),
    ]
    wait_all(tokens)
    sent_out.append(copies.start(normed_ref, normed_hbm))
    for t in range(4):
        cols = slice(t * 256, (t + 1) * 256)
        wait_all(weights[t])

        @pl.loop(0, 2)
        def _(s):
            rows = pl.ds(pl.multiple_of(s * 512, 512), 512)
            pre = dot(normed_ref[rows, :], in_ref[:, cols])
            square = pre * pre
            tanh = jnp.tanh(GELU_SCALE * pre * (1.0 + GELU_CUBE * square))
            upper = 0.5 + 0.5 * tanh
            slope = upper + (0.5 * GELU_SCALE) * pre * (1.0 - tanh * tanh) * (1.0 + 3.0 * GELU_CUBE * square)
            slope_ref[rows, cols] = slope.astype(BF)
            activation = (pre * upper).astype(BF)
            for i in range(2):
                few = pl.ds(pl.multiple_of(s * 32 + i * 16, 16), 16)
                pooled = dot(pool_ref[few, :], activation[i * 256 : (i + 1) * 256])
                pooled_ref[few, cols] = pooled.astype(BF)

    sent_out.append(copies.start(slope_ref, slope_hbm))
    sent_out.append(copies.start(pooled_ref, pooled_hbm))
    wait_all(outer)
    sent_out.append(copies.start(all_out_ref, all_out_hbm))
    partial = dot(pooled_ref[...], all_out_ref[...])
    partial = jnp.concatenate([partial[0:16] + hidden_sum_ref[...], partial[16:64]], axis=0)
    partial = (partial * length_ref[:, 0:1]).astype(BF)
    outgoing_ref[...] = (dot_t(route_ref[...], partial) + relations).astype(BF)
    sent_out.append(copies.start(outgoing_ref, outgoing_hbm))
    wait_all(sent_out)


def graph_kernel(
    copies,
    where_ref,
    arrived_hbm, own_hot_t_hbm,
    src_hot_hbm, dst_hot_hbm, dst_hot_t_hbm,
    w_msg_hbm, w_self_hbm, d_out_hbm,
    cache_hbm, low_hbm, high_hbm,
    table_out_hbm, graph_out_hbm, aggregate_hbm, nodes_hbm, pre_hbm,
    arrived_ref, own_hot_t_ref,
    src_hot_ref, dst_hot_ref, dst_hot_t_ref,
    w_msg_ref, w_self_ref, d_out_ref,
    table_out_ref, graph_out_ref, aggregate_ref, nodes_ref, pre_ref,
    base_ref, places_ref, row_hot_t_ref, src_row_hot_ref,
    ext_ref, sources_ref, edges_ref, agg_grad_ref, sums_ref, rel_ref, blocks_ref,
):
    scale = (256 / 2048) ** 0.5
    first = [
        copies.start(low_hbm.at[pl.ds(64, 16), pl.ds(0, 128)], places_ref.at[0]),
        copies.start(high_hbm.at[pl.ds(64, 16), pl.ds(0, 128)], places_ref.at[1]),
        copies.start(own_hot_t_hbm, own_hot_t_ref),
        copies.start(arrived_hbm, arrived_ref),
        copies.start(cache_hbm, base_ref.at[pl.ds(16, 240), :]),
        copies.start(low_hbm.at[pl.ds(0, 64), :], base_ref.at[pl.ds(256, 64), :]),
        copies.start(high_hbm.at[pl.ds(0, 64), :], base_ref.at[pl.ds(320, 64), :]),
        copies.start(src_hot_hbm, src_hot_ref),
    ]
    second = [copies.start(dst_hot_t_hbm, dst_hot_t_ref)]
    third = [
        copies.start(w_msg_hbm, w_msg_ref),
        copies.start(w_self_hbm, w_self_ref),
        copies.start(d_out_hbm, d_out_ref),
    ]
    fourth = [copies.start(dst_hot_hbm, dst_hot_ref)]
    base_ref[0:16, :] = jnp.zeros((16, 1024), BF)
    wait_all(first)
    to = lanes((128, 128)) - sublanes((128, 128))
    inside = sublanes((128, 128)) < 64
    low_move = ((to == 0) & inside).astype(F32).astype(BF)
    high_move = ((to == 64) & inside).astype(F32).astype(BF)
    places = (dot(places_ref[0], low_move) + dot(places_ref[1], high_move))[0:1].astype(I32)
    upper = (lax.broadcasted_iota(I32, (1, 128), 1) >= 64).astype(I32)
    table_row = jnp.where(places < 16, (places % 4) * 16 + upper * 8 + places // 4, -1)
    row_hot_t_ref[:, 0:256] = own_hot_t_ref[...]
    row_hot_t_ref[:, 256:384] = (sublanes((64, 128)) == table_row).astype(F32).astype(BF)
    src_row_hot_ref[...] = dot_bt(row_hot_t_ref[...], src_hot_ref[...]).astype(BF)
    total = arrived_ref[0:64, :].astype(F32)
    for i in range(1, 4):
        total = total + arrived_ref[i * 64 : (i + 1) * 64, :].astype(F32)
    for j in range(16):
        at = j // 4 * 16 + 12 + j % 4
        rel_ref[j] = total[at : at + 1]
    table = total.astype(BF)
    ext_ref[...] = (base_ref[...].astype(F32) + dot_t(row_hot_t_ref[...], table)).astype(BF)
    nodes_ref[...] = ext_ref[0:256, :]
    sent_out = [copies.start(nodes_ref, nodes_hbm)]

    for n in range(4):
        cols = slice(n * 256, (n + 1) * 256)

        @pl.loop(0, 4)
        def _(k):
            rows = pl.ds(pl.multiple_of(k * 512, 512), 512)
            taken = dot(src_hot_ref[rows, :], ext_ref[:, cols])
            taken = taken.astype(BF)
            sources_ref[rows, cols] = taken
            for i in range(4):
                few = pl.ds(pl.multiple_of(k * 512 + i * 128, 128), 128)
                edges_ref[few, cols] = taken[i * 128 : (i + 1) * 128] * rel_ref[k * 4 + i, :, cols].astype(BF)

    wait_all(second)

    @pl.loop(0, 4)
    def _(n):
        cols = pl.ds(pl.multiple_of(n * 256, 256), 256)
        aggregate_ref[:, cols] = (scale * dot(dst_hot_t_ref[...], edges_ref[:, cols])).astype(BF)

    sent_out.append(copies.start(aggregate_ref, aggregate_hbm))
    wait_all(third)

    @pl.loop(0, 4)
    def _(n):
        cols = pl.ds(pl.multiple_of(n * 256, 256), 256)
        out_pre = dot(aggregate_ref[...], w_msg_ref[:, cols]) + dot(nodes_ref[...], w_self_ref[:, cols])
        squashed = jnp.tanh(out_pre)
        graph_out_ref[:, cols] = squashed.astype(BF)
        pre_ref[:, cols] = (d_out_ref[:, cols].astype(F32) * (1.0 - squashed * squashed)).astype(BF)

    sent_out.append(copies.start(graph_out_ref, graph_out_hbm))
    sent_out.append(copies.start(pre_ref, pre_hbm))

    @pl.loop(0, 4)
    def _(n):
        cols = pl.ds(pl.multiple_of(n * 256, 256), 256)
        agg_grad_ref[:, cols] = (scale * dot_bt(pre_ref[...], w_msg_ref[cols, :])).astype(BF)

    wait_all(fourth)

    for n in range(4):
        cols = slice(n * 256, (n + 1) * 256)

        @pl.loop(0, 4)
        def _(k):
            rows = pl.ds(pl.multiple_of(k * 512, 512), 512)
            at_dest = dot(dst_hot_ref[rows, :], agg_grad_ref[:, cols])
            for i in range(4):
                few = pl.ds(pl.multiple_of(k * 512 + i * 128, 128), 128)
                part = at_dest[i * 128 : (i + 1) * 128]
                edges_ref[few, cols] = part.astype(BF) * rel_ref[k * 4 + i, :, cols].astype(BF)
                product = part * sources_ref[few, cols].astype(F32)
                sums_ref[k * 4 + i, :, cols] = jnp.sum(product, axis=0, keepdims=True)

    blocks_ref[...] = jnp.concatenate([sums_ref[j] for j in range(16)], axis=0).astype(BF)
    block = lanes((64, 16))
    block_hot = (sublanes((64, 16)) == block // 4 * 16 + 12 + block % 4).astype(F32).astype(BF)
    own_pre = dot(own_hot_t_ref[...], pre_ref[...]).astype(BF)

    @pl.loop(0, 4)
    def _(n):
        cols = pl.ds(pl.multiple_of(n * 256, 256), 256)
        grad = dot(src_row_hot_ref[...], edges_ref[:, cols]) + dot_bt(own_pre, w_self_ref[cols, :])
        grad = grad + dot(block_hot, blocks_ref[:, cols])
        table_out_ref[:, cols] = grad.astype(BF)

    for x in range(4):
        sent_out.append(copies.start(table_out_ref, table_out_hbm.at[pl.ds(x * 64, 64), :]))
    wait_all(sent_out)


def weight_kernel(
    copies,
    where_ref,
    aggregate_hbm, nodes_hbm, pre_hbm,
    kept_hbm, given_hbm,
    aggregate_ref, nodes_ref, pre_ref,
    kept_ref, given_ref,
):
    core = where_ref[1]
    wait_all(
        [copies.start(aggregate_hbm, aggregate_ref), copies.start(nodes_hbm, nodes_ref), copies.start(pre_hbm, pre_ref)]
    )
    sent_out = []
    for half, chunk_ref, chunk_hbm in ((1 - core, given_ref, given_hbm), (core, kept_ref, kept_hbm)):

        @pl.loop(0, 4)
        def _(z):
            rows = pl.ds(pl.multiple_of(z * 256 + half * 128, 128), 128)
            msg = dot_t(aggregate_ref[:, rows], pre_ref[...])
            own = dot_t(nodes_ref[:, rows], pre_ref[...])
            for x in range(4):
                for y in range(4):
                    at = (x * 4 + y) * 8
                    both = jnp.concatenate([msg[at : at + 8], own[at : at + 8]], axis=0)
                    chunk_ref[x, z * 4 + y] = both.astype(BF)

        sent_out.append(copies.start(chunk_ref, chunk_hbm))
    wait_all(sent_out)


def ring_places(mine):
    places = []
    for at in range(4):
        ahead = lax.rem(at - mine + 4, 4)
        places.append(jnp.where(ahead == 0, 0, jnp.where(ahead == 3, 1, ahead + 1)))
    return places


def back_kernel(
    copies,
    where_ref,
    returned_hbm, route_hbm, length_hbm, rel_hot_hbm, pooled_hbm, all_out_hbm, slope_hbm, normed_t_hbm,
    in_given_hbm, out_given_hbm, in_kept_hbm, out_kept_hbm,
    returned_ref, route_ref, length_ref, rel_hot_ref, pooled_ref, all_out_ref, slope_ref, normed_t_ref,
    in_given_ref, out_given_ref, in_kept_ref, out_kept_ref,
    scaled_ref, grad_ref,
):
    my_z, core, my_y = where_ref[0], where_ref[1], where_ref[3]
    first = [
        copies.start(returned_hbm, returned_ref),
        copies.start(route_hbm, route_ref),
        copies.start(length_hbm, length_ref),
        copies.start(rel_hot_hbm, rel_hot_ref),
        copies.start(pooled_hbm, pooled_ref),
    ]
    second = [copies.start(all_out_hbm, all_out_ref), copies.start(slope_hbm, slope_ref)]
    third = [copies.start(normed_t_hbm, normed_t_ref)]
    places = ring_places(my_z)
    pools = []
    wait_all(first)
    scaled_ref[...] = (dot(route_ref[...], returned_ref[...]) * length_ref[:, 0:1]).astype(BF)
    for s in range(4):
        line = lanes((16, 256))
        length = 1.0 / length_ref[s * 16 : (s + 1) * 16, 0:1]
        inside = (line // 16 == sublanes((16, 256))) & ((line % 16).astype(F32) + 0.5 < length)
        pools.append(inside.astype(F32).astype(BF))
    wait_all(second)

    @pl.loop(0, 4)
    def _(t):
        cols = pl.ds(pl.multiple_of(t * 256, 256), 256)
        upstream = dot_bt(scaled_ref[...], all_out_ref[cols, :]).astype(BF)
        for s in range(4):
            rows = slice(s * 256, (s + 1) * 256)
            at_tokens = dot_t(pools[s], upstream[s * 16 : (s + 1) * 16])
            grad_ref[rows, cols] = (slope_ref[rows, cols].astype(F32) * at_tokens).astype(BF)

    wait_all(third)
    sent_out = []
    for half, in_ref, in_hbm, out_ref, out_hbm in (
        (1 - core, in_given_ref, in_given_hbm, out_given_ref, out_given_hbm),
        (core, in_kept_ref, in_kept_hbm, out_kept_ref, out_kept_hbm),
    ):

        @pl.loop(0, 4)
        def _(t):
            cols = pl.ds(pl.multiple_of(t * 256, 256), 256)
            origin = jnp.where(t == 0, 0, jnp.where(t == 1, 3, t - 1))
            owner = lax.rem(my_y + origin, 4)
            units = pl.ds(pl.multiple_of(t * 256 + half * 128, 128), 128)
            out = dot_t(pooled_ref[:, units], scaled_ref[...]).astype(BF)
            rel_rows = pl.ds(pl.multiple_of(owner * 128 + half * 64, 64), 64)
            rel = dot(rel_hot_ref[rel_rows, :], returned_ref[...]).astype(BF)
            inner = dot(normed_t_ref[pl.ds(pl.multiple_of(half * 512, 512), 512), :], grad_ref[:, cols]).astype(BF)
            for z in range(4):
                out_ref[t, places[z], 0:32, :] = out[z * 32 : (z + 1) * 32]
                out_ref[t, places[z], 32:48, :] = rel[z * 16 : (z + 1) * 16]
                for i in range(4):
                    piece = inner[z * 128 + i * 32 : z * 128 + (i + 1) * 32]
                    in_ref[places[z], t, :, i * 256 : (i + 1) * 256] = piece

        sent_out.append(copies.start(in_ref, in_hbm))
        sent_out.append(copies.start(out_ref, out_hbm))
    wait_all(sent_out)


def place_kernel(
    copies,
    where_ref,
    h0, h1, h2, h3, h4, h5, h6, h7,
    in_hbm, out_hbm, rel_hbm,
    a0, a1, a2, a3, c0, c1, c2, c3,
    in_ref, out_ref, owned_ref, rel_ref,
):
    sources = (h0, h1, h2, h3, h4, h5, h6, h7)
    targets = (a0, a1, a2, a3, c0, c1, c2, c3)
    wait_all([copies.start(source, target) for source, target in zip(sources, targets)])
    my_z, core = where_ref[0], where_ref[1]
    for pieces, half in (((a0, a1, a2, a3), core), ((c0, c1, c2, c3), 1 - core)):
        for piece, origin in zip(pieces, ORIGINS):
            z = lax.rem(my_z + origin, 4)
            values = piece[...].astype(F32)
            for i in range(4):
                rows = pl.ds(pl.multiple_of(half * 512 + z * 128 + i * 32, 32), 32)
                in_ref[rows, :] = values[0:32, i * 256 : (i + 1) * 256]
            out_ref[pl.ds(pl.multiple_of(half * 128 + z * 32, 32), 32), :] = values[32:64]
            rel_ref[pl.ds(pl.multiple_of(half * 32 + z * 8, 8), 8), :] = values[64:72]
    owned_ref[...] = rel_ref[0:52, :]
    wait_all([copies.start(in_ref, in_hbm), copies.start(out_ref, out_hbm), copies.start(owned_ref, rel_hbm)])


def shards(
    hidden,
    desc_len,
    w_in,
    w_out,
    send_order,
    place_order,
    cache,
    halo_rows,
    edge_src,
    edge_dst,
    edge_rel,
    rel_table,
    w_msg,
    w_self,
    d_out,
):
    entities, length, width = hidden.shape
    tokens = entities * length
    units = w_in.shape[1]
    my_core = lax.axis_index("core")
    where = jnp.stack([lax.axis_index(name) for name in ("z", "core", "x", "y")]).astype(I32)
    src, dst, rel = edge_src[0], edge_dst[0], edge_rel[0]
    shard_rows = rel_table.shape[0]

    numbers = jnp.broadcast_to(rel.reshape(1, 4, 4), (4, 4, 4)).reshape(16, 4)
    numbers = lax.all_to_all(jnp.pad(numbers, ((0, 0), (0, 124))), GROUP, 0, 0, tiled=True)

    rel_pad = jnp.pad(rel_table, ((0, 64 - shard_rows), (0, 0)))
    operands = [hidden.reshape(tokens, width), desc_len[None, :], send_order]
    outs = [((tokens + 16, width), BF), ((entities, width), F32), ((576, 512), BF)]
    block, hidden_sum, weights = local_call(
        norm_kernel,
        outs,
        [where, *operands, w_in, w_out, rel_pad],
        like(operands) + filled(outs),
        copies=14,
    )
    blocks = [block, *gather_ring(block, "x", 128)]
    mine = gather_ring(weights, "y", 256)
    other = [shift_by(part, "core", 1) for part in mine]

    outs = [
        ((256, width), BF),
        ((4 * tokens, width), BF),
        ((4 * tokens, 4 * units), BF),
        ((4 * entities, 4 * units), BF),
        ((4 * units, width), BF),
        ((4 * entities, 256), BF),
        ((4 * entities, 128), F32),
        ((512, 256), BF),
    ]
    outgoing, normed, slope, pooled, all_out, route, inverse, rel_hot = local_call(
        encode_kernel,
        outs,
        [where, *blocks, w_in, w_out, rel_pad, *mine, *other, hidden_sum, numbers],
        filled(outs)
        + [
            pltpu.VMEM((width, 4 * units), BF),
            pltpu.VMEM((4 * entities, tokens), BF),
            pltpu.VMEM((256, width), BF),
            pltpu.VMEM((4, 16, 128), BF),
            pltpu.VMEM((entities, width), F32),
            pltpu.VMEM((16, 128), I32),
        ],
        copies=64,
        flops=2 * 4 * tokens * width * 4 * units,
    )

    halo = halo_rows[0]
    place = place_order[0]
    side = halo.shape[0] // 2
    cache_count = cache.shape[0]
    boundary = dot(one_hot(halo - entities, cache_count), cache).astype(BF)
    halo_hot = halo[:, None] == jnp.arange(entities, dtype=I32)[None, :]
    halo_place = jnp.where(halo < entities, jnp.sum(jnp.where(halo_hot, place[None, :], 0), axis=1), 16)

    def edge_of(rows, places):
        return jnp.concatenate([rows, jnp.pad(row_of(places, width), ((0, 15), (0, 0)))], axis=0)

    to_high, to_low = edge_of(boundary[side:], halo_place[side:]), edge_of(boundary[:side], halo_place[:side])
    to_high, to_low, outgoing = lax.optimization_barrier((to_high, to_low, outgoing))
    from_low = shift_by(to_high, GROUP, 1)
    from_high = shift_by(to_low, GROUP, 15)
    own_row = jnp.concatenate([fresh_row(0, place), jnp.full((cache_count,), -1, I32)])
    node_count = entities + cache_count
    extended_count = node_count + 2 * side
    edge_count = src.shape[0]
    block_count = rel.shape[0]
    src_hot = one_hot(src, extended_count)
    arrived = lax.all_to_all(outgoing.reshape(16, 16, width), GROUP, 0, 0, tiled=True).reshape(256, width)
    arrived, normed_t = lax.optimization_barrier((arrived, normed.T))

    outs = [((256, width), BF)] + [((node_count, width), BF)] * 4
    operands = [
        arrived,
        one_hot_t(own_row, 64),
        src_hot,
        one_hot(dst, node_count),
        one_hot_t(dst, node_count),
        w_msg,
        w_self,
        d_out,
    ]
    grad_table, graph_out, aggregate, nodes, grad_pre = local_call(
        graph_kernel,
        outs,
        [where, *operands, cache, from_low, from_high],
        like(operands)
        + filled([((64, width), BF), *outs[1:]])
        + [
            pltpu.VMEM((extended_count, width), BF),
            pltpu.VMEM((2, 16, 128), BF),
            pltpu.VMEM((64, extended_count), BF),
            pltpu.VMEM((64, edge_count), BF),
            pltpu.VMEM((extended_count, width), BF),
            pltpu.VMEM((edge_count, width), BF),
            pltpu.VMEM((edge_count, width), BF),
            pltpu.VMEM((node_count, width), BF),
            pltpu.VMEM((block_count, 1, width), F32),
            pltpu.VMEM((block_count, 1, width), F32),
            pltpu.VMEM((block_count, width), BF),
        ],
        copies=30,
        flops=6 * 10**9,
    )

    returned = lax.all_to_all(grad_table.reshape(16, 16, width), GROUP, 0, 0, tiled=True).reshape(256, width)

    outs = [((4, 16, 16, width), BF)] * 2
    operands = [aggregate, nodes, grad_pre]
    graph_kept, graph_given = local_call(
        weight_kernel, outs, [where, *operands], like(operands) + filled(outs), flops=10**9
    )
    returned, graph_kept, graph_given = lax.optimization_barrier((returned, graph_kept, graph_given))
    chip = (graph_kept.astype(F32) + shift_by(graph_given, "core", 1).astype(F32)).astype(BF)
    line = lax.all_to_all(chip, "x", 0, 0, tiled=True)
    plane = lax.all_to_all(jnp.sum(line.astype(F32), axis=0).astype(BF), ("z", "y"), 0, 0, tiled=True)
    weight_rows = jnp.sum(plane.astype(F32), axis=0)
    grad_msg, grad_self = weight_rows[:8], weight_rows[8:]

    outs = [((4, 4, 32, width), BF), ((4, 4, 48, width), BF)] * 2
    operands = [returned, route, inverse, rel_hot, pooled, all_out, slope, normed_t]
    in_given, out_given, in_kept, out_kept = local_call(
        back_kernel,
        outs,
        [where, *operands],
        like(operands)
        + filled(outs)
        + [pltpu.VMEM((4 * entities, width), BF), pltpu.VMEM((4 * tokens, 4 * units), BF)],
        copies=14,
        flops=2 * 4 * tokens * width * 4 * units,
    )
    in_chip = (in_kept.astype(F32) + shift_by(in_given, "core", 1).astype(F32)).astype(BF)
    out_chip = (out_kept.astype(F32) + shift_by(out_given, "core", 1).astype(F32)).astype(BF)
    out_part = reduce_ring([out_chip[i].reshape(192, width) for i in range(4)], "y").reshape(4, 48, width)
    in_part = reduce_ring([in_chip[i].reshape(128, width) for i in range(4)], "z").reshape(4, 32, width)
    out_part = reduce_ring([out_part[i] for i in range(4)], "z")
    in_part = reduce_ring([in_part[i] for i in range(4)], "y")
    part = jnp.concatenate([in_part, out_part], axis=0)
    parts = [part] + [shift_by(part, "z", s) for s in SHIFTS]
    others = [shift_by(piece, "core", 1) for piece in parts]
    outs = [((width, units), F32), ((units, width), F32), ((shard_rows, width), F32)]
    operands = [*parts, *others]
    grad_w_in, grad_w_out, grad_rel = local_call(
        place_kernel,
        outs,
        [where, *operands],
        like(operands) + filled(outs) + [pltpu.VMEM((64, width), F32)],
        copies=12,
    )
    return (graph_out, grad_w_in, grad_w_out, grad_rel, grad_msg, grad_self)


def solution(mesh):
    fine = Mesh(mesh.devices.reshape(4, 2, 4, 4), ("z", "core", "x", "y"))
    every = ("z", "core", "x", "y")
    placed = (
        P(every, None, None),
        P(every),
        P(None, GROUP),
        P(GROUP, None),
        P(every, None),
        P(every, None),
        P(every, None),
        P(every, None),
        P(every, None),
        P(every, None),
        P(every, None),
        P(GROUP, None),
        P(),
        P(),
        P(every, None),
    )
    return jax.shard_map(
        shards,
        mesh=fine,
        in_specs=placed,
        out_specs=(
            P(every, None),
            P(None, GROUP),
            P(GROUP, None),
            P(GROUP, None),
            P(every, None),
            P(every, None),
        ),
        check_vma=False,
    )
```

```python
import jax
import jax.numpy as jnp
import numpy as np
from jax import lax
from jax.experimental import pallas as pl
from jax.experimental.pallas import tpu as pltpu
from jax.sharding import Mesh
from jax.sharding import PartitionSpec as P

BF = jnp.bfloat16
F32 = jnp.float32
I32 = jnp.int32
GROUP = ("x", "y")
SHIFTS = (1, 3, 2)
ORIGINS = (0, 3, 1, 2)
GELU_SCALE = float(np.sqrt(2.0 / np.pi))
GELU_CUBE = 0.044715


def shift_by(value, axis, shift):
    count = lax.axis_size(axis)
    return lax.ppermute(value, axis, [(i, (i + shift) % count) for i in range(count)])


def dot(a, b):
    return jnp.dot(a, b, preferred_element_type=F32)


def dot_t(a, b):
    return lax.dot_general(a, b, (((0,), (0,)), ((), ())), preferred_element_type=F32)


def dot_bt(a, b):
    return lax.dot_general(a, b, (((1,), (1,)), ((), ())), preferred_element_type=F32)


def one_hot(index, count):
    return (index[:, None] == jnp.arange(count, dtype=I32)[None, :]).astype(BF)


def one_hot_t(index, count):
    return (index[None, :] == jnp.arange(count, dtype=I32)[:, None]).astype(BF)


def lanes(shape):
    return lax.broadcasted_iota(I32, shape, 1)


def sublanes(shape):
    return lax.broadcasted_iota(I32, shape, 0)


def row_of(values, width):
    return jnp.pad(values.astype(BF), (0, width - values.shape[0]))[None, :]


def gather_ring(value, axis, cut):
    low, high = shift_by(value, axis, 1), shift_by(value, axis, 3)
    return [low, high, shift_by(low[:cut], axis, 1), shift_by(high[cut:], axis, 3)]


def reduce_ring(chunks, axis):
    total = chunks[0].astype(F32)
    for chunk, origin in zip(chunks[1:], ORIGINS[1:]):
        total = total + shift_by(chunk, axis, origin).astype(F32)
    return total.astype(BF)


def fresh_row(side, place):
    return (place % 4) * 16 + (side + 1) * 4 + place // 4


class Copies:
    def __init__(self, sems):
        self.sems, self.used = sems, 0

    def start(self, source, target):
        copy = pltpu.make_async_copy(source, target, self.sems.at[self.used])
        self.used += 1
        copy.start()
        return copy


def local_call(body, outs, operands, scratch=(), copies=8, flops=0, limit=60):
    def kernel(*refs):
        body(Copies(refs[-1]), *refs[:-1])

    return pl.pallas_call(
        kernel,
        out_shape=[jax.ShapeDtypeStruct(shape, kind) for shape, kind in outs],
        in_specs=[pl.BlockSpec(memory_space=pltpu.SMEM)]
        + [pl.BlockSpec(memory_space=pltpu.HBM)] * (len(operands) - 1),
        out_specs=[pl.BlockSpec(memory_space=pltpu.HBM)] * len(outs),
        scratch_shapes=[*scratch, pltpu.SemaphoreType.DMA((copies,))],
        compiler_params=pltpu.CompilerParams(vmem_limit_bytes=limit * 1024 * 1024),
        cost_estimate=pl.CostEstimate(flops=flops, bytes_accessed=1024 * 1024, transcendentals=0),
    )(*operands)


def like(arrays):
    return [pltpu.VMEM(array.shape, array.dtype) for array in arrays]


def filled(outs):
    return [pltpu.VMEM(shape, kind) for shape, kind in outs]


def wait_all(copies):
    for copy in copies:
        copy.wait()


def length_column(meta):
    shape = meta.shape
    return jnp.sum(jnp.where(lanes(shape) == sublanes(shape), meta, 0.0), axis=1, keepdims=True)


def pool_rows(length, tokens):
    shape = (16, tokens)
    line = lanes(shape)
    inside = (line // 16 == sublanes(shape)) & ((line % 16).astype(F32) < length)
    return inside.astype(F32).astype(BF)


def norm_kernel(
    copies,
    where_ref,
    hidden_hbm, lens_hbm, order_hbm, table_hbm, in_hbm, out_hbm,
    block_hbm, sum_hbm, weights_hbm, padded_hbm,
    hidden_ref, lens_ref, order_ref, table_ref,
    block_ref, sum_ref, weights_ref, padded_ref,
):
    core = where_ref[1]
    table = copies.start(table_hbm, table_ref)
    packed = []
    for i in range(2):
        cols, wide = pl.ds(i * 256, 256), pl.ds(i * 512, 512)
        source = in_hbm.at[pl.ds(pl.multiple_of(core * 512 + i * 256, 256), 256), :]
        packed.append(copies.start(source, weights_ref.at[pl.ds(0, 256), cols]))
        source = out_hbm.at[pl.ds(pl.multiple_of(core * 128, 128), 128), wide]
        packed.append(copies.start(source, weights_ref.at[pl.ds(256 + i * 128, 128), :]))
    first = [
        copies.start(hidden_hbm, hidden_ref),
        copies.start(lens_hbm, lens_ref),
        copies.start(order_hbm, order_ref),
    ]
    table.wait()
    spread = (lanes((64, 52)) == sublanes((64, 52))).astype(F32).astype(BF)
    padded_ref[...] = dot(spread, table_ref[...]).astype(BF)
    own = padded_ref[pl.ds(pl.multiple_of(core * 32, 32), 32), :]
    weights_ref[512:544, :] = own[:, 0:512]
    weights_ref[544:576, :] = own[:, 512:1024]
    wait_all(packed)
    later = [copies.start(weights_ref, weights_hbm), copies.start(padded_ref, padded_hbm)]
    wait_all(first)
    meta = jnp.zeros((16, 128), F32)
    for i, row in enumerate((lens_ref[...], order_ref[...])):
        values = jnp.broadcast_to(row.astype(F32), (16, 16)).astype(BF)
        select = (lanes((16, 128)) == sublanes((16, 128)) + 16 * i).astype(F32).astype(BF)
        meta = meta + dot(values, select)
    values = hidden_ref[...].astype(F32)
    center = values - jnp.mean(values, axis=-1, keepdims=True)
    spread = jnp.mean(center * center, axis=-1, keepdims=True)
    tokens = values.shape[0]
    block_ref[0:tokens, :] = (center * lax.rsqrt(spread + 1e-05)).astype(BF)
    block_ref[tokens : tokens + 16, :] = jnp.zeros((16, values.shape[1]), BF)
    block_ref[tokens : tokens + 16, 0:128] = meta.astype(BF)
    later.append(copies.start(block_ref, block_hbm))
    sum_ref[...] = dot(pool_rows(length_column(meta), tokens), hidden_ref[...])
    later.append(copies.start(sum_ref, sum_hbm))
    wait_all(later)


def encode_kernel(
    copies,
    where_ref,
    b0, b1, b2, b3_top, b3_rest,
    own_in, own_out, own_rel,
    m1, m2, m3_in, m3_rest,
    o1, o2, o3_in, o3_rest,
    hidden_sum_hbm, numbers_hbm,
    outgoing_hbm, normed_hbm, slope_hbm, pooled_hbm, all_out_hbm, route_hbm, length_hbm, rel_hot_hbm,
    outgoing_ref, normed_ref, slope_ref, pooled_ref, all_out_ref, route_ref, length_ref, rel_hot_ref,
    in_ref, pool_ref, rel_ref, meta_ref, hidden_sum_ref, numbers_ref,
):
    core, my_x, my_y = where_ref[1], where_ref[2], where_ref[3]
    metas, tokens, weights, tables = [], [], [[], [], [], []], []
    for s, (block, row) in enumerate(((b0, 256), (b1, 256), (b2, 256), (b3_rest, 128))):
        metas.append(copies.start(block.at[pl.ds(row, 16), pl.ds(0, 128)], meta_ref.at[s]))
    tables.append(copies.start(own_rel, rel_ref.at[pl.ds(0, 64), :]))
    tables.append(copies.start(numbers_hbm, numbers_ref))
    pieces = []
    for t, (mine, other) in enumerate(
        (((m1, m1, 256), (o1, o1, 256)), ((m2, m2, 256), (o2, o2, 256)), ((m3_in, m3_rest, 0), (o3_in, o3_rest, 0))), 1
    ):
        for (inner, rest, at), half in ((mine, core), (other, 1 - core)):
            pieces.append((t, inner, rest, at, half))
            for i in range(2):
                rows = pl.ds(pl.multiple_of(t * 64 + half * 32, 32), 32)
                target = rel_ref.at[rows, pl.ds(i * 512, 512)]
                tables.append(copies.start(rest.at[pl.ds(at + 256 + i * 32, 32), :], target))
    for s, (block, row, count) in enumerate(((b0, 0, 256), (b1, 256, 256), (b2, 512, 256), (b3_top, 768, 128), (b3_rest, 896, 128))):
        tokens.append(copies.start(block.at[pl.ds(0, count), :], normed_ref.at[pl.ds(row, count), :]))
    weights[0].append(copies.start(own_in, in_ref.at[:, pl.ds(0, 256)]))
    for t, inner, rest, at, half in pieces:
        for i in range(2):
            rows = pl.ds(pl.multiple_of(half * 512 + i * 256, 256), 256)
            target = in_ref.at[rows, pl.ds(t * 256, 256)]
            weights[t].append(copies.start(inner.at[pl.ds(0, 256), pl.ds(i * 256, 256)], target))
    outer = [
        copies.start(own_out, all_out_ref.at[pl.ds(0, 256), :]),
        copies.start(hidden_sum_hbm, hidden_sum_ref),
    ]
    for t, inner, rest, at, half in pieces:
        for i in range(2):
            rows = pl.ds(pl.multiple_of(t * 256 + half * 128, 128), 128)
            target = all_out_ref.at[rows, pl.ds(i * 512, 512)]
            outer.append(copies.start(rest.at[pl.ds(at + i * 128, 128), :], target))
    wait_all(metas)
    wait_all(tables)

    wide = (16, 256)
    slot = lanes(wide) % 16
    bound = lanes((128, 256))
    bound = (bound // 16 + (bound % 16) // 4 + 15) % 16
    bound_hot = (sublanes((128, 256)) == bound + 16).astype(F32).astype(BF)
    for s in range(4):
        meta = meta_ref[s]
        values = meta.astype(F32)
        length = length_column(values)
        length_ref[s * 16 : (s + 1) * 16, :] = jnp.broadcast_to(1.0 / length, (16, 128))
        pool_ref[s * 16 : (s + 1) * 16, :] = pool_rows(length, 256)
        sent = dot(meta, bound_hot)
        encoder = lax.rem(my_x + ORIGINS[s], 4)
        chosen = (sent == sublanes(wide).astype(F32)) & (slot % 4 == encoder) & (slot < 12)
        route_ref[s * 16 : (s + 1) * 16, :] = chosen.astype(F32).astype(BF)

    high = numbers_ref[...] // 32
    digits = (high.astype(F32).astype(BF), (numbers_ref[...] - 32 * high).astype(F32).astype(BF))
    tall, flat = (256, 128), (16, 256)
    chosen = lanes(tall) == sublanes(tall) % 16 - 12
    source_hot = (sublanes((256, 16)) // 16 == lanes((256, 16))).astype(F32).astype(BF)
    column = [jnp.sum(jnp.where(chosen, dot(source_hot, part), 0.0), axis=1, keepdims=True) for part in digits]
    line = lanes((256, 256))
    owner_y = (my_y + jnp.where(line < 64, 0, jnp.where(line < 128, 3, line // 64 - 1))) % 4
    name = ((my_x * 4 + owner_y) * 52 + line % 64).astype(F32)
    served = (name == 32.0 * column[0] + column[1]) & (line % 64 < 52) & (sublanes((256, 256)) % 16 >= 12)
    slot_hot = (sublanes((128, 256)) == lanes((128, 256)) % 16 - 12).astype(F32).astype(BF)
    own = sublanes(flat) == lanes(flat) // 16
    row = [jnp.sum(jnp.where(own, dot(part, slot_hot), 0.0), axis=0, keepdims=True) for part in digits]
    line = sublanes((512, 256))
    local = (line // 64) % 2 * 32 + (line // 16) % 4 * 8 + line % 16
    name = ((my_x * 4 + line // 128) * 52 + local).astype(F32)
    good = (line % 16 < 8) & (local < 52) & (lanes((512, 256)) % 16 >= 12)
    rel_hot_ref[...] = ((name == 32.0 * row[0] + row[1]) & good).astype(F32).astype(BF)
    relations = dot(served.astype(F32).astype(BF), rel_ref[...])

    sent_out = [
        copies.start(route_ref, route_hbm),
        copies.start(length_ref, length_hbm),
        copies.start(rel_hot_ref, rel_hot_hbm),
    ]
    wait_all(tokens)
    sent_out.append(copies.start(normed_ref, normed_hbm))
    for t in range(4):
        cols = slice(t * 256, (t + 1) * 256)
        wait_all(weights[t])

        @pl.loop(0, 2)
        def _(s):
            rows = pl.ds(pl.multiple_of(s * 512, 512), 512)
            pre = dot(normed_ref[rows, :], in_ref[:, cols])
            square = pre * pre
            tanh = jnp.tanh(GELU_SCALE * pre * (1.0 + GELU_CUBE * square))
            upper = 0.5 + 0.5 * tanh
            slope = upper + (0.5 * GELU_SCALE) * pre * (1.0 - tanh * tanh) * (1.0 + 3.0 * GELU_CUBE * square)
            slope_ref[rows, cols] = slope.astype(BF)
            activation = (pre * upper).astype(BF)
            for i in range(2):
                few = pl.ds(pl.multiple_of(s * 32 + i * 16, 16), 16)
                pooled = dot(pool_ref[few, :], activation[i * 256 : (i + 1) * 256])
                pooled_ref[few, cols] = pooled.astype(BF)

    sent_out.append(copies.start(slope_ref, slope_hbm))
    sent_out.append(copies.start(pooled_ref, pooled_hbm))
    wait_all(outer)
    sent_out.append(copies.start(all_out_ref, all_out_hbm))
    partial = dot(pooled_ref[...], all_out_ref[...])
    partial = jnp.concatenate([partial[0:16] + hidden_sum_ref[...], partial[16:64]], axis=0)
    partial = (partial * length_ref[:, 0:1]).astype(BF)
    outgoing_ref[...] = (dot_t(route_ref[...], partial) + relations).astype(BF)
    sent_out.append(copies.start(outgoing_ref, outgoing_hbm))
    wait_all(sent_out)


def graph_kernel(
    copies,
    where_ref,
    arrived_hbm, own_hot_t_hbm,
    src_hot_hbm, dst_hot_hbm, dst_hot_t_hbm,
    w_msg_hbm, w_self_hbm, d_out_hbm,
    cache_hbm, low_hbm, high_hbm,
    table_out_hbm, graph_out_hbm, aggregate_hbm, nodes_hbm, pre_hbm,
    arrived_ref, own_hot_t_ref,
    src_hot_ref, dst_hot_ref, dst_hot_t_ref,
    w_msg_ref, w_self_ref, d_out_ref,
    table_out_ref, graph_out_ref, aggregate_ref, nodes_ref, pre_ref,
    base_ref, places_ref, row_hot_t_ref, src_row_hot_ref,
    ext_ref, sources_ref, edges_ref, agg_grad_ref, sums_ref, rel_ref, blocks_ref,
):
    scale = (256 / 2048) ** 0.5
    first = [
        copies.start(low_hbm.at[pl.ds(64, 16), pl.ds(0, 128)], places_ref.at[0]),
        copies.start(high_hbm.at[pl.ds(64, 16), pl.ds(0, 128)], places_ref.at[1]),
        copies.start(own_hot_t_hbm, own_hot_t_ref),
        copies.start(arrived_hbm, arrived_ref),
        copies.start(cache_hbm, base_ref.at[pl.ds(16, 240), :]),
        copies.start(low_hbm.at[pl.ds(0, 64), :], base_ref.at[pl.ds(256, 64), :]),
        copies.start(high_hbm.at[pl.ds(0, 64), :], base_ref.at[pl.ds(320, 64), :]),
        copies.start(src_hot_hbm, src_hot_ref),
    ]
    second = [copies.start(dst_hot_t_hbm, dst_hot_t_ref)]
    third = [
        copies.start(w_msg_hbm, w_msg_ref),
        copies.start(w_self_hbm, w_self_ref),
        copies.start(d_out_hbm, d_out_ref),
    ]
    fourth = [copies.start(dst_hot_hbm, dst_hot_ref)]
    base_ref[0:16, :] = jnp.zeros((16, 1024), BF)
    wait_all(first)
    to = lanes((128, 128)) - sublanes((128, 128))
    inside = sublanes((128, 128)) < 64
    low_move = ((to == 0) & inside).astype(F32).astype(BF)
    high_move = ((to == 64) & inside).astype(F32).astype(BF)
    places = (dot(places_ref[0], low_move) + dot(places_ref[1], high_move))[0:1].astype(I32)
    upper = (lax.broadcasted_iota(I32, (1, 128), 1) >= 64).astype(I32)
    table_row = jnp.where(places < 16, (places % 4) * 16 + upper * 8 + places // 4, -1)
    row_hot_t_ref[:, 0:256] = own_hot_t_ref[...]
    row_hot_t_ref[:, 256:384] = (sublanes((64, 128)) == table_row).astype(F32).astype(BF)
    src_row_hot_ref[...] = dot_bt(row_hot_t_ref[...], src_hot_ref[...]).astype(BF)
    total = arrived_ref[0:64, :].astype(F32)
    for i in range(1, 4):
        total = total + arrived_ref[i * 64 : (i + 1) * 64, :].astype(F32)
    for j in range(16):
        at = j // 4 * 16 + 12 + j % 4
        rel_ref[j] = total[at : at + 1]
    table = total.astype(BF)
    ext_ref[...] = (base_ref[...].astype(F32) + dot_t(row_hot_t_ref[...], table)).astype(BF)
    nodes_ref[...] = ext_ref[0:256, :]
    sent_out = [copies.start(nodes_ref, nodes_hbm)]

    for n in range(4):
        cols = slice(n * 256, (n + 1) * 256)

        @pl.loop(0, 4)
        def _(k):
            rows = pl.ds(pl.multiple_of(k * 512, 512), 512)
            taken = dot(src_hot_ref[rows, :], ext_ref[:, cols])
            taken = taken.astype(BF)
            sources_ref[rows, cols] = taken
            for i in range(4):
                few = pl.ds(pl.multiple_of(k * 512 + i * 128, 128), 128)
                edges_ref[few, cols] = taken[i * 128 : (i + 1) * 128] * rel_ref[k * 4 + i, :, cols].astype(BF)

    wait_all(second)

    @pl.loop(0, 4)
    def _(n):
        cols = pl.ds(pl.multiple_of(n * 256, 256), 256)
        aggregate_ref[:, cols] = (scale * dot(dst_hot_t_ref[...], edges_ref[:, cols])).astype(BF)

    sent_out.append(copies.start(aggregate_ref, aggregate_hbm))
    wait_all(third)

    @pl.loop(0, 4)
    def _(n):
        cols = pl.ds(pl.multiple_of(n * 256, 256), 256)
        out_pre = dot(aggregate_ref[...], w_msg_ref[:, cols]) + dot(nodes_ref[...], w_self_ref[:, cols])
        squashed = jnp.tanh(out_pre)
        graph_out_ref[:, cols] = squashed.astype(BF)
        pre_ref[:, cols] = (d_out_ref[:, cols].astype(F32) * (1.0 - squashed * squashed)).astype(BF)

    sent_out.append(copies.start(graph_out_ref, graph_out_hbm))
    sent_out.append(copies.start(pre_ref, pre_hbm))

    @pl.loop(0, 4)
    def _(n):
        cols = pl.ds(pl.multiple_of(n * 256, 256), 256)
        agg_grad_ref[:, cols] = (scale * dot_bt(pre_ref[...], w_msg_ref[cols, :])).astype(BF)

    wait_all(fourth)

    for n in range(4):
        cols = slice(n * 256, (n + 1) * 256)

        @pl.loop(0, 4)
        def _(k):
            rows = pl.ds(pl.multiple_of(k * 512, 512), 512)
            at_dest = dot(dst_hot_ref[rows, :], agg_grad_ref[:, cols])
            for i in range(4):
                few = pl.ds(pl.multiple_of(k * 512 + i * 128, 128), 128)
                part = at_dest[i * 128 : (i + 1) * 128]
                edges_ref[few, cols] = part.astype(BF) * rel_ref[k * 4 + i, :, cols].astype(BF)
                product = part * sources_ref[few, cols].astype(F32)
                sums_ref[k * 4 + i, :, cols] = jnp.sum(product, axis=0, keepdims=True)

    blocks_ref[...] = jnp.concatenate([sums_ref[j] for j in range(16)], axis=0).astype(BF)
    block = lanes((64, 16))
    block_hot = (sublanes((64, 16)) == block // 4 * 16 + 12 + block % 4).astype(F32).astype(BF)
    own_pre = dot(own_hot_t_ref[...], pre_ref[...]).astype(BF)

    @pl.loop(0, 4)
    def _(n):
        cols = pl.ds(pl.multiple_of(n * 256, 256), 256)
        grad = dot(src_row_hot_ref[...], edges_ref[:, cols]) + dot_bt(own_pre, w_self_ref[cols, :])
        grad = grad + dot(block_hot, blocks_ref[:, cols])
        table_out_ref[:, cols] = grad.astype(BF)

    for x in range(4):
        sent_out.append(copies.start(table_out_ref, table_out_hbm.at[pl.ds(x * 64, 64), :]))
    wait_all(sent_out)


def weight_kernel(
    copies,
    where_ref,
    aggregate_hbm, nodes_hbm, pre_hbm,
    kept_hbm, given_hbm,
    aggregate_ref, nodes_ref, pre_ref,
    kept_ref, given_ref,
):
    core = where_ref[1]
    wait_all(
        [copies.start(aggregate_hbm, aggregate_ref), copies.start(nodes_hbm, nodes_ref), copies.start(pre_hbm, pre_ref)]
    )
    sent_out = []
    for half, chunk_ref, chunk_hbm in ((1 - core, given_ref, given_hbm), (core, kept_ref, kept_hbm)):

        @pl.loop(0, 4)
        def _(z):
            rows = pl.ds(pl.multiple_of(z * 256 + half * 128, 128), 128)
            msg = dot_t(aggregate_ref[:, rows], pre_ref[...])
            own = dot_t(nodes_ref[:, rows], pre_ref[...])
            for x in range(4):
                for y in range(4):
                    at = (x * 4 + y) * 8
                    both = jnp.concatenate([msg[at : at + 8], own[at : at + 8]], axis=0)
                    chunk_ref[x, z * 4 + y] = both.astype(BF)

        sent_out.append(copies.start(chunk_ref, chunk_hbm))
    wait_all(sent_out)


def ring_places(mine):
    places = []
    for at in range(4):
        ahead = lax.rem(at - mine + 4, 4)
        places.append(jnp.where(ahead == 0, 0, jnp.where(ahead == 3, 1, ahead + 1)))
    return places


def back_kernel(
    copies,
    where_ref,
    returned_hbm, route_hbm, length_hbm, rel_hot_hbm, pooled_hbm, all_out_hbm, slope_hbm, normed_t_hbm,
    in_given_hbm, out_given_hbm, in_kept_hbm, out_kept_hbm,
    returned_ref, route_ref, length_ref, rel_hot_ref, pooled_ref, all_out_ref, slope_ref, normed_t_ref,
    in_given_ref, out_given_ref, in_kept_ref, out_kept_ref,
    scaled_ref, grad_ref,
):
    my_z, core, my_y = where_ref[0], where_ref[1], where_ref[3]
    first = [
        copies.start(returned_hbm, returned_ref),
        copies.start(route_hbm, route_ref),
        copies.start(length_hbm, length_ref),
        copies.start(rel_hot_hbm, rel_hot_ref),
        copies.start(pooled_hbm, pooled_ref),
    ]
    second = [copies.start(all_out_hbm, all_out_ref), copies.start(slope_hbm, slope_ref)]
    third = [copies.start(normed_t_hbm, normed_t_ref)]
    places = ring_places(my_z)
    pools = []
    wait_all(first)
    scaled_ref[...] = (dot(route_ref[...], returned_ref[...]) * length_ref[:, 0:1]).astype(BF)
    for s in range(4):
        line = lanes((16, 256))
        length = 1.0 / length_ref[s * 16 : (s + 1) * 16, 0:1]
        inside = (line // 16 == sublanes((16, 256))) & ((line % 16).astype(F32) + 0.5 < length)
        pools.append(inside.astype(F32).astype(BF))
    wait_all(second)

    @pl.loop(0, 4)
    def _(t):
        cols = pl.ds(pl.multiple_of(t * 256, 256), 256)
        upstream = dot_bt(scaled_ref[...], all_out_ref[cols, :]).astype(BF)
        for s in range(4):
            rows = slice(s * 256, (s + 1) * 256)
            at_tokens = dot_t(pools[s], upstream[s * 16 : (s + 1) * 16])
            grad_ref[rows, cols] = (slope_ref[rows, cols].astype(F32) * at_tokens).astype(BF)

    wait_all(third)
    sent_out = []
    for half, in_ref, in_hbm, out_ref, out_hbm in (
        (1 - core, in_given_ref, in_given_hbm, out_given_ref, out_given_hbm),
        (core, in_kept_ref, in_kept_hbm, out_kept_ref, out_kept_hbm),
    ):

        @pl.loop(0, 4)
        def _(t):
            cols = pl.ds(pl.multiple_of(t * 256, 256), 256)
            origin = jnp.where(t == 0, 0, jnp.where(t == 1, 3, t - 1))
            owner = lax.rem(my_y + origin, 4)
            units = pl.ds(pl.multiple_of(t * 256 + half * 128, 128), 128)
            out = dot_t(pooled_ref[:, units], scaled_ref[...]).astype(BF)
            rel_rows = pl.ds(pl.multiple_of(owner * 128 + half * 64, 64), 64)
            rel = dot(rel_hot_ref[rel_rows, :], returned_ref[...]).astype(BF)
            inner = dot(normed_t_ref[pl.ds(pl.multiple_of(half * 512, 512), 512), :], grad_ref[:, cols]).astype(BF)
            for z in range(4):
                out_ref[t, places[z], :, :] = out[z * 32 : (z + 1) * 32]
                in_ref[places[z], t, 32:48, :] = rel[z * 16 : (z + 1) * 16]
                for i in range(4):
                    piece = inner[z * 128 + i * 32 : z * 128 + (i + 1) * 32]
                    in_ref[places[z], t, 0:32, i * 256 : (i + 1) * 256] = piece

        sent_out.append(copies.start(in_ref, in_hbm))
        sent_out.append(copies.start(out_ref, out_hbm))
    wait_all(sent_out)


def place_kernel(
    copies,
    where_ref,
    h0, h1, h2, h3, h4, h5, h6, h7,
    in_hbm, out_hbm, rel_hbm,
    a0, a1, a2, a3, c0, c1, c2, c3,
    in_ref, out_ref, owned_ref, rel_ref,
):
    sources = (h0, h1, h2, h3, h4, h5, h6, h7)
    targets = (a0, a1, a2, a3, c0, c1, c2, c3)
    wait_all([copies.start(source, target) for source, target in zip(sources, targets)])
    my_z, core = where_ref[0], where_ref[1]
    for pieces, half in (((a0, a1, a2, a3), core), ((c0, c1, c2, c3), 1 - core)):
        for piece, origin in zip(pieces, ORIGINS):
            z = lax.rem(my_z + origin, 4)
            values = piece[...].astype(F32)
            for i in range(4):
                rows = pl.ds(pl.multiple_of(half * 512 + z * 128 + i * 32, 32), 32)
                in_ref[rows, :] = values[0:32, i * 256 : (i + 1) * 256]
            out_ref[pl.ds(pl.multiple_of(half * 128 + z * 32, 32), 32), :] = values[48:80]
            rel_ref[pl.ds(pl.multiple_of(half * 32 + z * 8, 8), 8), :] = values[32:40]
    owned_ref[...] = rel_ref[0:52, :]
    wait_all([copies.start(in_ref, in_hbm), copies.start(out_ref, out_hbm), copies.start(owned_ref, rel_hbm)])


def shards(
    hidden,
    desc_len,
    w_in,
    w_out,
    send_order,
    place_order,
    cache,
    halo_rows,
    edge_src,
    edge_dst,
    edge_rel,
    rel_table,
    w_msg,
    w_self,
    d_out,
):
    entities, length, width = hidden.shape
    tokens = entities * length
    units = w_in.shape[1]
    my_core = lax.axis_index("core")
    where = jnp.stack([lax.axis_index(name) for name in ("z", "core", "x", "y")]).astype(I32)
    src, dst, rel = edge_src[0], edge_dst[0], edge_rel[0]
    shard_rows = rel_table.shape[0]

    numbers = jnp.broadcast_to(rel.reshape(1, 4, 4), (4, 4, 4)).reshape(16, 4)
    numbers = lax.all_to_all(jnp.pad(numbers, ((0, 0), (0, 124))), GROUP, 0, 0, tiled=True)

    operands = [hidden.reshape(tokens, width), desc_len[None, :], send_order, rel_table]
    outs = [((tokens + 16, width), BF), ((entities, width), F32), ((576, 512), BF), ((64, width), BF)]
    block, hidden_sum, weights, rel_pad = local_call(
        norm_kernel,
        outs,
        [where, *operands, w_in, w_out],
        like(operands) + filled(outs),
        copies=14,
    )
    blocks = [block, *gather_ring(block, "x", 128)]
    mine = gather_ring(weights, "y", 256)
    other = [shift_by(part, "core", 1) for part in mine]

    outs = [
        ((256, width), BF),
        ((4 * tokens, width), BF),
        ((4 * tokens, 4 * units), BF),
        ((4 * entities, 4 * units), BF),
        ((4 * units, width), BF),
        ((4 * entities, 256), BF),
        ((4 * entities, 128), F32),
        ((512, 256), BF),
    ]
    outgoing, normed, slope, pooled, all_out, route, inverse, rel_hot = local_call(
        encode_kernel,
        outs,
        [where, *blocks, w_in, w_out, rel_pad, *mine, *other, hidden_sum, numbers],
        filled(outs)
        + [
            pltpu.VMEM((width, 4 * units), BF),
            pltpu.VMEM((4 * entities, tokens), BF),
            pltpu.VMEM((256, width), BF),
            pltpu.VMEM((4, 16, 128), BF),
            pltpu.VMEM((entities, width), F32),
            pltpu.VMEM((16, 128), I32),
        ],
        copies=64,
        flops=2 * 4 * tokens * width * 4 * units,
    )

    halo = halo_rows[0]
    place = place_order[0]
    side = halo.shape[0] // 2
    cache_count = cache.shape[0]
    boundary = dot(one_hot(halo - entities, cache_count), cache).astype(BF)
    halo_hot = halo[:, None] == jnp.arange(entities, dtype=I32)[None, :]
    halo_place = jnp.where(halo < entities, jnp.sum(jnp.where(halo_hot, place[None, :], 0), axis=1), 16)

    def edge_of(rows, places):
        return jnp.concatenate([rows, jnp.pad(row_of(places, width), ((0, 15), (0, 0)))], axis=0)

    to_high, to_low = edge_of(boundary[side:], halo_place[side:]), edge_of(boundary[:side], halo_place[:side])
    to_high, to_low, outgoing = lax.optimization_barrier((to_high, to_low, outgoing))
    from_low = shift_by(to_high, GROUP, 1)
    from_high = shift_by(to_low, GROUP, 15)
    own_row = jnp.concatenate([fresh_row(0, place), jnp.full((cache_count,), -1, I32)])
    node_count = entities + cache_count
    extended_count = node_count + 2 * side
    edge_count = src.shape[0]
    block_count = rel.shape[0]
    src_hot = one_hot(src, extended_count)
    arrived = lax.all_to_all(outgoing.reshape(16, 16, width), GROUP, 0, 0, tiled=True).reshape(256, width)
    arrived, normed_t = lax.optimization_barrier((arrived, normed.T))

    outs = [((256, width), BF)] + [((node_count, width), BF)] * 4
    operands = [
        arrived,
        one_hot_t(own_row, 64),
        src_hot,
        one_hot(dst, node_count),
        one_hot_t(dst, node_count),
        w_msg,
        w_self,
        d_out,
    ]
    grad_table, graph_out, aggregate, nodes, grad_pre = local_call(
        graph_kernel,
        outs,
        [where, *operands, cache, from_low, from_high],
        like(operands)
        + filled([((64, width), BF), *outs[1:]])
        + [
            pltpu.VMEM((extended_count, width), BF),
            pltpu.VMEM((2, 16, 128), BF),
            pltpu.VMEM((64, extended_count), BF),
            pltpu.VMEM((64, edge_count), BF),
            pltpu.VMEM((extended_count, width), BF),
            pltpu.VMEM((edge_count, width), BF),
            pltpu.VMEM((edge_count, width), BF),
            pltpu.VMEM((node_count, width), BF),
            pltpu.VMEM((block_count, 1, width), F32),
            pltpu.VMEM((block_count, 1, width), F32),
            pltpu.VMEM((block_count, width), BF),
        ],
        copies=30,
        flops=6 * 10**9,
    )

    returned = lax.all_to_all(grad_table.reshape(16, 16, width), GROUP, 0, 0, tiled=True).reshape(256, width)

    outs = [((4, 16, 16, width), BF)] * 2
    operands = [aggregate, nodes, grad_pre]
    graph_kept, graph_given = local_call(
        weight_kernel, outs, [where, *operands], like(operands) + filled(outs), flops=10**9
    )
    returned, graph_kept, graph_given = lax.optimization_barrier((returned, graph_kept, graph_given))
    chip = (graph_kept.astype(F32) + shift_by(graph_given, "core", 1).astype(F32)).astype(BF)

    outs = [((4, 4, 48, width), BF), ((4, 4, 32, width), BF)] * 2
    operands = [returned, route, inverse, rel_hot, pooled, all_out, slope, normed_t]
    in_given, out_given, in_kept, out_kept = local_call(
        back_kernel,
        outs,
        [where, *operands],
        like(operands)
        + filled(outs)
        + [pltpu.VMEM((4 * entities, width), BF), pltpu.VMEM((4 * tokens, 4 * units), BF)],
        copies=14,
        flops=2 * 4 * tokens * width * 4 * units,
    )
    in_other, chip = lax.optimization_barrier((shift_by(in_given, "core", 1), chip))
    line = lax.all_to_all(chip, "x", 0, 0, tiled=True)
    plane = lax.all_to_all(jnp.sum(line.astype(F32), axis=0).astype(BF), ("z", "y"), 0, 0, tiled=True)
    weight_rows = jnp.sum(plane.astype(F32), axis=0)
    grad_msg, grad_self = weight_rows[:8], weight_rows[8:]
    in_chip = (in_kept.astype(F32) + in_other.astype(F32)).astype(BF)
    in_chip, out_given = lax.optimization_barrier((in_chip, out_given))
    out_chip = (out_kept.astype(F32) + shift_by(out_given, "core", 1).astype(F32)).astype(BF)
    out_part = reduce_ring([out_chip[i].reshape(128, width) for i in range(4)], "y").reshape(4, 32, width)
    in_part = reduce_ring([in_chip[i].reshape(192, width) for i in range(4)], "z").reshape(4, 48, width)
    out_part = reduce_ring([out_part[i] for i in range(4)], "z")
    in_part = reduce_ring([in_part[i] for i in range(4)], "y")
    part = jnp.concatenate([in_part, out_part], axis=0)
    parts = [part] + [shift_by(part, "z", s) for s in SHIFTS]
    others = [shift_by(piece, "core", 1) for piece in parts]
    outs = [((width, units), F32), ((units, width), F32), ((shard_rows, width), F32)]
    operands = [*parts, *others]
    grad_w_in, grad_w_out, grad_rel = local_call(
        place_kernel,
        outs,
        [where, *operands],
        like(operands) + filled(outs) + [pltpu.VMEM((64, width), F32)],
        copies=12,
    )
    return (graph_out, grad_w_in, grad_w_out, grad_rel, grad_msg, grad_self)


def solution(mesh):
    fine = Mesh(mesh.devices.reshape(4, 2, 4, 4), ("z", "core", "x", "y"))
    every = ("z", "core", "x", "y")
    placed = (
        P(every, None, None),
        P(every),
        P(None, GROUP),
        P(GROUP, None),
        P(every, None),
        P(every, None),
        P(every, None),
        P(every, None),
        P(every, None),
        P(every, None),
        P(every, None),
        P(GROUP, None),
        P(),
        P(),
        P(every, None),
    )
    return jax.shard_map(
        shards,
        mesh=fine,
        in_specs=placed,
        out_specs=(
            P(every, None),
            P(None, GROUP),
            P(GROUP, None),
            P(GROUP, None),
            P(every, None),
            P(every, None),
        ),
        check_vma=False,
    )
```

```python
import jax
import jax.numpy as jnp
import numpy as np
from jax import lax
from jax.experimental import pallas as pl
from jax.experimental.pallas import tpu as pltpu
from jax.sharding import Mesh
from jax.sharding import PartitionSpec as P

BF = jnp.bfloat16
F32 = jnp.float32
I32 = jnp.int32
GROUP = ("x", "y")
SHIFTS = (1, 3, 2)
ORIGINS = (0, 3, 1, 2)
GELU_SCALE = float(np.sqrt(2.0 / np.pi))
GELU_CUBE = 0.044715


def shift_by(value, axis, shift):
    count = lax.axis_size(axis)
    return lax.ppermute(value, axis, [(i, (i + shift) % count) for i in range(count)])


def dot(a, b):
    return jnp.dot(a, b, preferred_element_type=F32)


def dot_t(a, b):
    return lax.dot_general(a, b, (((0,), (0,)), ((), ())), preferred_element_type=F32)


def dot_bt(a, b):
    return lax.dot_general(a, b, (((1,), (1,)), ((), ())), preferred_element_type=F32)


def one_hot(index, count):
    return (index[:, None] == jnp.arange(count, dtype=I32)[None, :]).astype(BF)


def one_hot_t(index, count):
    return (index[None, :] == jnp.arange(count, dtype=I32)[:, None]).astype(BF)


def lanes(shape):
    return lax.broadcasted_iota(I32, shape, 1)


def sublanes(shape):
    return lax.broadcasted_iota(I32, shape, 0)


def row_of(values, width):
    return jnp.pad(values.astype(BF), (0, width - values.shape[0]))[None, :]


def gather_ring(value, axis, cut):
    low, high = shift_by(value, axis, 1), shift_by(value, axis, 3)
    return [low, high, shift_by(low[:cut], axis, 1), shift_by(high[cut:], axis, 3)]


def reduce_ring(chunks, axis):
    total = chunks[0].astype(F32)
    for chunk, origin in zip(chunks[1:], ORIGINS[1:]):
        total = total + shift_by(chunk, axis, origin).astype(F32)
    return total.astype(BF)


def fresh_row(side, place):
    return (place % 4) * 16 + (side + 1) * 4 + place // 4


class Copies:
    def __init__(self, sems):
        self.sems, self.used = sems, 0

    def start(self, source, target):
        copy = pltpu.make_async_copy(source, target, self.sems.at[self.used])
        self.used += 1
        copy.start()
        return copy


def local_call(body, outs, operands, scratch=(), copies=8, flops=0, limit=60):
    def kernel(*refs):
        body(Copies(refs[-1]), *refs[:-1])

    return pl.pallas_call(
        kernel,
        out_shape=[jax.ShapeDtypeStruct(shape, kind) for shape, kind in outs],
        in_specs=[pl.BlockSpec(memory_space=pltpu.SMEM)]
        + [pl.BlockSpec(memory_space=pltpu.HBM)] * (len(operands) - 1),
        out_specs=[pl.BlockSpec(memory_space=pltpu.HBM)] * len(outs),
        scratch_shapes=[*scratch, pltpu.SemaphoreType.DMA((copies,))],
        compiler_params=pltpu.CompilerParams(vmem_limit_bytes=limit * 1024 * 1024),
        cost_estimate=pl.CostEstimate(flops=flops, bytes_accessed=1024 * 1024, transcendentals=0),
    )(*operands)


def like(arrays):
    return [pltpu.VMEM(array.shape, array.dtype) for array in arrays]


def filled(outs):
    return [pltpu.VMEM(shape, kind) for shape, kind in outs]


def wait_all(copies):
    for copy in copies:
        copy.wait()


def length_column(meta):
    shape = meta.shape
    return jnp.sum(jnp.where(lanes(shape) == sublanes(shape), meta, 0.0), axis=1, keepdims=True)


def pool_rows(length, tokens):
    shape = (16, tokens)
    line = lanes(shape)
    inside = (line // 16 == sublanes(shape)) & ((line % 16).astype(F32) < length)
    return inside.astype(F32).astype(BF)


def norm_kernel(
    copies,
    where_ref,
    hidden_hbm, lens_hbm, order_hbm, table_hbm, in_hbm, out_hbm,
    block_hbm, sum_hbm, weights_hbm, padded_hbm,
    hidden_ref, lens_ref, order_ref, table_ref,
    block_ref, sum_ref, weights_ref, padded_ref,
):
    core = where_ref[1]
    table = copies.start(table_hbm, table_ref)
    packed = []
    for i in range(2):
        cols, wide = pl.ds(i * 256, 256), pl.ds(i * 512, 512)
        source = in_hbm.at[pl.ds(pl.multiple_of(core * 512 + i * 256, 256), 256), :]
        packed.append(copies.start(source, weights_ref.at[pl.ds(0, 256), cols]))
        source = out_hbm.at[pl.ds(pl.multiple_of(core * 128, 128), 128), wide]
        packed.append(copies.start(source, weights_ref.at[pl.ds(256 + i * 128, 128), :]))
    first = [
        copies.start(hidden_hbm, hidden_ref),
        copies.start(lens_hbm, lens_ref),
        copies.start(order_hbm, order_ref),
    ]
    table.wait()
    spread = (lanes((64, 52)) == sublanes((64, 52))).astype(F32).astype(BF)
    padded_ref[...] = dot(spread, table_ref[...]).astype(BF)
    own = padded_ref[pl.ds(pl.multiple_of(core * 32, 32), 32), :]
    weights_ref[512:544, :] = own[:, 0:512]
    weights_ref[544:576, :] = own[:, 512:1024]
    wait_all(packed)
    later = [copies.start(weights_ref, weights_hbm), copies.start(padded_ref, padded_hbm)]
    wait_all(first)
    meta = jnp.zeros((16, 128), F32)
    for i, row in enumerate((lens_ref[...], order_ref[...])):
        values = jnp.broadcast_to(row.astype(F32), (16, 16)).astype(BF)
        select = (lanes((16, 128)) == sublanes((16, 128)) + 16 * i).astype(F32).astype(BF)
        meta = meta + dot(values, select)
    values = hidden_ref[...].astype(F32)
    center = values - jnp.mean(values, axis=-1, keepdims=True)
    spread = jnp.mean(center * center, axis=-1, keepdims=True)
    tokens = values.shape[0]
    block_ref[0:tokens, :] = (center * lax.rsqrt(spread + 1e-05)).astype(BF)
    block_ref[tokens : tokens + 16, :] = jnp.zeros((16, values.shape[1]), BF)
    block_ref[tokens : tokens + 16, 0:128] = meta.astype(BF)
    later.append(copies.start(block_ref, block_hbm))
    sum_ref[...] = dot(pool_rows(length_column(meta), tokens), hidden_ref[...])
    later.append(copies.start(sum_ref, sum_hbm))
    wait_all(later)


def encode_kernel(
    copies,
    where_ref,
    b0, b1, b2, b3_top, b3_rest,
    own_in, own_out, own_rel,
    m1, m2, m3_in, m3_rest,
    o1, o2, o3_in, o3_rest,
    hidden_sum_hbm, numbers_hbm,
    outgoing_hbm, normed_hbm, slope_hbm, pooled_hbm, all_out_hbm, route_hbm, length_hbm, rel_hot_hbm,
    outgoing_ref, normed_ref, slope_ref, pooled_ref, all_out_ref, route_ref, length_ref, rel_hot_ref,
    in_ref, pool_ref, rel_ref, meta_ref, hidden_sum_ref, numbers_ref,
):
    core, my_x, my_y = where_ref[1], where_ref[2], where_ref[3]
    metas, tokens, weights, tables = [], [], [[], [], [], []], []
    for s, (block, row) in enumerate(((b0, 256), (b1, 256), (b2, 256), (b3_rest, 128))):
        metas.append(copies.start(block.at[pl.ds(row, 16), pl.ds(0, 128)], meta_ref.at[s]))
    tables.append(copies.start(own_rel, rel_ref.at[pl.ds(0, 64), :]))
    tables.append(copies.start(numbers_hbm, numbers_ref))
    pieces = []
    for t, (mine, other) in enumerate(
        (((m1, m1, 256), (o1, o1, 256)), ((m2, m2, 256), (o2, o2, 256)), ((m3_in, m3_rest, 0), (o3_in, o3_rest, 0))), 1
    ):
        for (inner, rest, at), half in ((mine, core), (other, 1 - core)):
            pieces.append((t, inner, rest, at, half))
            for i in range(2):
                rows = pl.ds(pl.multiple_of(t * 64 + half * 32, 32), 32)
                target = rel_ref.at[rows, pl.ds(i * 512, 512)]
                tables.append(copies.start(rest.at[pl.ds(at + 256 + i * 32, 32), :], target))
    for s, (block, row, count) in enumerate(((b0, 0, 256), (b1, 256, 256), (b2, 512, 256), (b3_top, 768, 128), (b3_rest, 896, 128))):
        tokens.append(copies.start(block.at[pl.ds(0, count), :], normed_ref.at[pl.ds(row, count), :]))
    weights[0].append(copies.start(own_in, in_ref.at[:, pl.ds(0, 256)]))
    for t, inner, rest, at, half in pieces:
        for i in range(2):
            rows = pl.ds(pl.multiple_of(half * 512 + i * 256, 256), 256)
            target = in_ref.at[rows, pl.ds(t * 256, 256)]
            weights[t].append(copies.start(inner.at[pl.ds(0, 256), pl.ds(i * 256, 256)], target))
    outer = [
        copies.start(own_out, all_out_ref.at[pl.ds(0, 256), :]),
        copies.start(hidden_sum_hbm, hidden_sum_ref),
    ]
    for t, inner, rest, at, half in pieces:
        for i in range(2):
            rows = pl.ds(pl.multiple_of(t * 256 + half * 128, 128), 128)
            target = all_out_ref.at[rows, pl.ds(i * 512, 512)]
            outer.append(copies.start(rest.at[pl.ds(at + i * 128, 128), :], target))
    wait_all(metas)
    wait_all(tables)

    wide = (16, 256)
    slot = lanes(wide) % 16
    bound = lanes((128, 256))
    bound = (bound // 16 + (bound % 16) // 4 + 15) % 16
    bound_hot = (sublanes((128, 256)) == bound + 16).astype(F32).astype(BF)
    for s in range(4):
        meta = meta_ref[s]
        values = meta.astype(F32)
        length = length_column(values)
        length_ref[s * 16 : (s + 1) * 16, :] = jnp.broadcast_to(1.0 / length, (16, 128))
        pool_ref[s * 16 : (s + 1) * 16, :] = pool_rows(length, 256)
        sent = dot(meta, bound_hot)
        encoder = lax.rem(my_x + ORIGINS[s], 4)
        chosen = (sent == sublanes(wide).astype(F32)) & (slot % 4 == encoder) & (slot < 12)
        route_ref[s * 16 : (s + 1) * 16, :] = chosen.astype(F32).astype(BF)

    high = numbers_ref[...] // 32
    digits = (high.astype(F32).astype(BF), (numbers_ref[...] - 32 * high).astype(F32).astype(BF))
    tall, flat = (256, 128), (16, 256)
    chosen = lanes(tall) == sublanes(tall) % 16 - 12
    source_hot = (sublanes((256, 16)) // 16 == lanes((256, 16))).astype(F32).astype(BF)
    column = [jnp.sum(jnp.where(chosen, dot(source_hot, part), 0.0), axis=1, keepdims=True) for part in digits]
    line = lanes((256, 256))
    owner_y = (my_y + jnp.where(line < 64, 0, jnp.where(line < 128, 3, line // 64 - 1))) % 4
    name = ((my_x * 4 + owner_y) * 52 + line % 64).astype(F32)
    served = (name == 32.0 * column[0] + column[1]) & (line % 64 < 52) & (sublanes((256, 256)) % 16 >= 12)
    slot_hot = (sublanes((128, 256)) == lanes((128, 256)) % 16 - 12).astype(F32).astype(BF)
    own = sublanes(flat) == lanes(flat) // 16
    row = [jnp.sum(jnp.where(own, dot(part, slot_hot), 0.0), axis=0, keepdims=True) for part in digits]
    line = sublanes((512, 256))
    local = (line // 64) % 2 * 32 + (line // 16) % 4 * 8 + line % 16
    name = ((my_x * 4 + line // 128) * 52 + local).astype(F32)
    good = (line % 16 < 8) & (local < 52) & (lanes((512, 256)) % 16 >= 12)
    rel_hot_ref[...] = ((name == 32.0 * row[0] + row[1]) & good).astype(F32).astype(BF)
    relations = dot(served.astype(F32).astype(BF), rel_ref[...])

    sent_out = [
        copies.start(route_ref, route_hbm),
        copies.start(length_ref, length_hbm),
        copies.start(rel_hot_ref, rel_hot_hbm),
    ]
    wait_all(tokens)
    sent_out.append(copies.start(normed_ref, normed_hbm))
    for t in range(4):
        cols = slice(t * 256, (t + 1) * 256)
        wait_all(weights[t])

        @pl.loop(0, 2)
        def _(s):
            rows = pl.ds(pl.multiple_of(s * 512, 512), 512)
            pre = dot(normed_ref[rows, :], in_ref[:, cols])
            square = pre * pre
            tanh = jnp.tanh(GELU_SCALE * pre * (1.0 + GELU_CUBE * square))
            upper = 0.5 + 0.5 * tanh
            slope = upper + (0.5 * GELU_SCALE) * pre * (1.0 - tanh * tanh) * (1.0 + 3.0 * GELU_CUBE * square)
            slope_ref[rows, cols] = slope.astype(BF)
            activation = (pre * upper).astype(BF)
            for i in range(2):
                few = pl.ds(pl.multiple_of(s * 32 + i * 16, 16), 16)
                pooled = dot(pool_ref[few, :], activation[i * 256 : (i + 1) * 256])
                pooled_ref[few, cols] = pooled.astype(BF)

    sent_out.append(copies.start(slope_ref, slope_hbm))
    sent_out.append(copies.start(pooled_ref, pooled_hbm))
    wait_all(outer)
    sent_out.append(copies.start(all_out_ref, all_out_hbm))
    partial = dot(pooled_ref[...], all_out_ref[...])
    partial = jnp.concatenate([partial[0:16] + hidden_sum_ref[...], partial[16:64]], axis=0)
    partial = (partial * length_ref[:, 0:1]).astype(BF)
    outgoing_ref[...] = (dot_t(route_ref[...], partial) + relations).astype(BF)
    sent_out.append(copies.start(outgoing_ref, outgoing_hbm))
    wait_all(sent_out)


def graph_kernel(
    copies,
    where_ref,
    arrived_hbm, own_hot_t_hbm,
    src_hot_hbm, dst_hot_hbm, dst_hot_t_hbm,
    w_msg_hbm, w_self_hbm, d_out_hbm,
    cache_hbm, low_hbm, high_hbm,
    table_out_hbm, graph_out_hbm, aggregate_hbm, nodes_hbm, pre_hbm,
    arrived_ref, own_hot_t_ref,
    src_hot_ref, dst_hot_ref, dst_hot_t_ref,
    w_msg_ref, w_self_ref, d_out_ref,
    table_out_ref, graph_out_ref, aggregate_ref, nodes_ref, pre_ref,
    base_ref, places_ref, row_hot_t_ref, src_row_hot_ref,
    ext_ref, sources_ref, edges_ref, agg_grad_ref, sums_ref, rel_ref, blocks_ref,
):
    scale = (256 / 2048) ** 0.5
    first = [
        copies.start(low_hbm.at[pl.ds(64, 16), pl.ds(0, 128)], places_ref.at[0]),
        copies.start(high_hbm.at[pl.ds(64, 16), pl.ds(0, 128)], places_ref.at[1]),
        copies.start(own_hot_t_hbm, own_hot_t_ref),
        copies.start(arrived_hbm, arrived_ref),
        copies.start(cache_hbm, base_ref.at[pl.ds(16, 240), :]),
        copies.start(low_hbm.at[pl.ds(0, 64), :], base_ref.at[pl.ds(256, 64), :]),
        copies.start(high_hbm.at[pl.ds(0, 64), :], base_ref.at[pl.ds(320, 64), :]),
        copies.start(src_hot_hbm, src_hot_ref),
    ]
    second = [copies.start(dst_hot_t_hbm, dst_hot_t_ref)]
    third = [
        copies.start(w_msg_hbm, w_msg_ref),
        copies.start(w_self_hbm, w_self_ref),
        copies.start(d_out_hbm, d_out_ref),
    ]
    fourth = [copies.start(dst_hot_hbm, dst_hot_ref)]
    base_ref[0:16, :] = jnp.zeros((16, 1024), BF)
    wait_all(first)
    to = lanes((128, 128)) - sublanes((128, 128))
    inside = sublanes((128, 128)) < 64
    low_move = ((to == 0) & inside).astype(F32).astype(BF)
    high_move = ((to == 64) & inside).astype(F32).astype(BF)
    places = (dot(places_ref[0], low_move) + dot(places_ref[1], high_move))[0:1].astype(I32)
    upper = (lax.broadcasted_iota(I32, (1, 128), 1) >= 64).astype(I32)
    table_row = jnp.where(places < 16, (places % 4) * 16 + upper * 8 + places // 4, -1)
    row_hot_t_ref[:, 0:256] = own_hot_t_ref[...]
    row_hot_t_ref[:, 256:384] = (sublanes((64, 128)) == table_row).astype(F32).astype(BF)
    src_row_hot_ref[...] = dot_bt(row_hot_t_ref[...], src_hot_ref[...]).astype(BF)
    total = arrived_ref[0:64, :].astype(F32)
    for i in range(1, 4):
        total = total + arrived_ref[i * 64 : (i + 1) * 64, :].astype(F32)
    for j in range(16):
        at = j // 4 * 16 + 12 + j % 4
        rel_ref[j] = total[at : at + 1]
    table = total.astype(BF)
    ext_ref[...] = (base_ref[...].astype(F32) + dot_t(row_hot_t_ref[...], table)).astype(BF)
    nodes_ref[...] = ext_ref[0:256, :]
    sent_out = [copies.start(nodes_ref, nodes_hbm)]

    for n in range(4):
        cols = slice(n * 256, (n + 1) * 256)

        @pl.loop(0, 4)
        def _(k):
            rows = pl.ds(pl.multiple_of(k * 512, 512), 512)
            taken = dot(src_hot_ref[rows, :], ext_ref[:, cols])
            taken = taken.astype(BF)
            sources_ref[rows, cols] = taken
            for i in range(4):
                few = pl.ds(pl.multiple_of(k * 512 + i * 128, 128), 128)
                edges_ref[few, cols] = taken[i * 128 : (i + 1) * 128] * rel_ref[k * 4 + i, :, cols].astype(BF)

    wait_all(second)

    @pl.loop(0, 4)
    def _(n):
        cols = pl.ds(pl.multiple_of(n * 256, 256), 256)
        aggregate_ref[:, cols] = (scale * dot(dst_hot_t_ref[...], edges_ref[:, cols])).astype(BF)

    sent_out.append(copies.start(aggregate_ref, aggregate_hbm))
    wait_all(third)

    @pl.loop(0, 4)
    def _(n):
        cols = pl.ds(pl.multiple_of(n * 256, 256), 256)
        out_pre = dot(aggregate_ref[...], w_msg_ref[:, cols]) + dot(nodes_ref[...], w_self_ref[:, cols])
        squashed = jnp.tanh(out_pre)
        graph_out_ref[:, cols] = squashed.astype(BF)
        pre_ref[:, cols] = (d_out_ref[:, cols].astype(F32) * (1.0 - squashed * squashed)).astype(BF)

    sent_out.append(copies.start(graph_out_ref, graph_out_hbm))
    sent_out.append(copies.start(pre_ref, pre_hbm))

    @pl.loop(0, 4)
    def _(n):
        cols = pl.ds(pl.multiple_of(n * 256, 256), 256)
        agg_grad_ref[:, cols] = (scale * dot_bt(pre_ref[...], w_msg_ref[cols, :])).astype(BF)

    wait_all(fourth)

    for n in range(4):
        cols = slice(n * 256, (n + 1) * 256)

        @pl.loop(0, 4)
        def _(k):
            rows = pl.ds(pl.multiple_of(k * 512, 512), 512)
            at_dest = dot(dst_hot_ref[rows, :], agg_grad_ref[:, cols])
            for i in range(4):
                few = pl.ds(pl.multiple_of(k * 512 + i * 128, 128), 128)
                part = at_dest[i * 128 : (i + 1) * 128]
                edges_ref[few, cols] = part.astype(BF) * rel_ref[k * 4 + i, :, cols].astype(BF)
                product = part * sources_ref[few, cols].astype(F32)
                sums_ref[k * 4 + i, :, cols] = jnp.sum(product, axis=0, keepdims=True)

    blocks_ref[...] = jnp.concatenate([sums_ref[j] for j in range(16)], axis=0).astype(BF)
    block = lanes((64, 16))
    block_hot = (sublanes((64, 16)) == block // 4 * 16 + 12 + block % 4).astype(F32).astype(BF)
    own_pre = dot(own_hot_t_ref[...], pre_ref[...]).astype(BF)

    @pl.loop(0, 4)
    def _(n):
        cols = pl.ds(pl.multiple_of(n * 256, 256), 256)
        grad = dot(src_row_hot_ref[...], edges_ref[:, cols]) + dot_bt(own_pre, w_self_ref[cols, :])
        grad = grad + dot(block_hot, blocks_ref[:, cols])
        table_out_ref[:, cols] = grad.astype(BF)

    for x in range(4):
        sent_out.append(copies.start(table_out_ref, table_out_hbm.at[pl.ds(x * 64, 64), :]))
    wait_all(sent_out)


def weight_kernel(
    copies,
    where_ref,
    aggregate_hbm, nodes_hbm, pre_hbm,
    kept_hbm, given_hbm,
    aggregate_ref, nodes_ref, pre_ref,
    kept_ref, given_ref,
):
    core = where_ref[1]
    wait_all(
        [copies.start(aggregate_hbm, aggregate_ref), copies.start(nodes_hbm, nodes_ref), copies.start(pre_hbm, pre_ref)]
    )
    sent_out = []
    for half, chunk_ref, chunk_hbm in ((1 - core, given_ref, given_hbm), (core, kept_ref, kept_hbm)):

        @pl.loop(0, 4)
        def _(z):
            rows = pl.ds(pl.multiple_of(z * 256 + half * 128, 128), 128)
            msg = dot_t(aggregate_ref[:, rows], pre_ref[...])
            own = dot_t(nodes_ref[:, rows], pre_ref[...])
            for x in range(4):
                for y in range(4):
                    at = (x * 4 + y) * 8
                    both = jnp.concatenate([msg[at : at + 8], own[at : at + 8]], axis=0)
                    chunk_ref[x, z * 4 + y] = both.astype(BF)

        sent_out.append(copies.start(chunk_ref, chunk_hbm))
    wait_all(sent_out)


def ring_places(mine):
    places = []
    for at in range(4):
        ahead = lax.rem(at - mine + 4, 4)
        places.append(jnp.where(ahead == 0, 0, jnp.where(ahead == 3, 1, ahead + 1)))
    return places


def back_kernel(
    copies,
    where_ref,
    returned_hbm, route_hbm, length_hbm, rel_hot_hbm, pooled_hbm, all_out_hbm, slope_hbm, normed_t_hbm,
    in_given_hbm, out_given_hbm, in_kept_hbm, out_kept_hbm,
    returned_ref, route_ref, length_ref, rel_hot_ref, pooled_ref, all_out_ref, slope_ref, normed_t_ref,
    in_given_ref, out_given_ref, in_kept_ref, out_kept_ref,
    scaled_ref, grad_ref,
):
    my_z, core, my_y = where_ref[0], where_ref[1], where_ref[3]
    first = [
        copies.start(returned_hbm, returned_ref),
        copies.start(route_hbm, route_ref),
        copies.start(length_hbm, length_ref),
        copies.start(rel_hot_hbm, rel_hot_ref),
        copies.start(pooled_hbm, pooled_ref),
    ]
    second = [copies.start(all_out_hbm, all_out_ref), copies.start(slope_hbm, slope_ref)]
    third = [copies.start(normed_t_hbm, normed_t_ref)]
    places = ring_places(my_z)
    pools = []
    wait_all(first)
    scaled_ref[...] = (dot(route_ref[...], returned_ref[...]) * length_ref[:, 0:1]).astype(BF)
    for s in range(4):
        line = lanes((16, 256))
        length = 1.0 / length_ref[s * 16 : (s + 1) * 16, 0:1]
        inside = (line // 16 == sublanes((16, 256))) & ((line % 16).astype(F32) + 0.5 < length)
        pools.append(inside.astype(F32).astype(BF))
    wait_all(second)

    @pl.loop(0, 4)
    def _(t):
        cols = pl.ds(pl.multiple_of(t * 256, 256), 256)
        upstream = dot_bt(scaled_ref[...], all_out_ref[cols, :]).astype(BF)
        for s in range(4):
            rows = slice(s * 256, (s + 1) * 256)
            at_tokens = dot_t(pools[s], upstream[s * 16 : (s + 1) * 16])
            grad_ref[rows, cols] = (slope_ref[rows, cols].astype(F32) * at_tokens).astype(BF)

    wait_all(third)
    sent_out = []
    for half, in_ref, in_hbm, out_ref, out_hbm in (
        (1 - core, in_given_ref, in_given_hbm, out_given_ref, out_given_hbm),
        (core, in_kept_ref, in_kept_hbm, out_kept_ref, out_kept_hbm),
    ):

        @pl.loop(0, 4)
        def _(t):
            cols = pl.ds(pl.multiple_of(t * 256, 256), 256)
            origin = jnp.where(t == 0, 0, jnp.where(t == 1, 3, t - 1))
            owner = lax.rem(my_y + origin, 4)
            units = pl.ds(pl.multiple_of(t * 256 + half * 128, 128), 128)
            out = dot_t(pooled_ref[:, units], scaled_ref[...]).astype(BF)
            rel_rows = pl.ds(pl.multiple_of(owner * 128 + half * 64, 64), 64)
            rel = dot(rel_hot_ref[rel_rows, :], returned_ref[...]).astype(BF)
            inner = dot(normed_t_ref[pl.ds(pl.multiple_of(half * 512, 512), 512), :], grad_ref[:, cols]).astype(BF)
            for z in range(4):
                out_ref[t, places[z], :, :] = out[z * 32 : (z + 1) * 32]
                in_ref[places[z], t, 32:48, :] = rel[z * 16 : (z + 1) * 16]
                for i in range(4):
                    piece = inner[z * 128 + i * 32 : z * 128 + (i + 1) * 32]
                    in_ref[places[z], t, 0:32, i * 256 : (i + 1) * 256] = piece

        sent_out.append(copies.start(in_ref, in_hbm))
        sent_out.append(copies.start(out_ref, out_hbm))
    wait_all(sent_out)


def place_kernel(
    copies,
    where_ref,
    h0, h1, h2, h3, h4, h5, h6, h7,
    in_hbm, out_hbm, rel_hbm,
    a0, a1, a2, a3, c0, c1, c2, c3,
    in_ref, out_ref, owned_ref, rel_ref,
):
    sources = (h0, h1, h2, h3, h4, h5, h6, h7)
    targets = (a0, a1, a2, a3, c0, c1, c2, c3)
    wait_all([copies.start(source, target) for source, target in zip(sources, targets)])
    my_z, core = where_ref[0], where_ref[1]
    for pieces, half in (((a0, a1, a2, a3), core), ((c0, c1, c2, c3), 1 - core)):
        for piece, origin in zip(pieces, ORIGINS):
            z = lax.rem(my_z + origin, 4)
            values = piece[...].astype(F32)
            for i in range(4):
                rows = pl.ds(pl.multiple_of(half * 512 + z * 128 + i * 32, 32), 32)
                in_ref[rows, :] = values[0:32, i * 256 : (i + 1) * 256]
            out_ref[pl.ds(pl.multiple_of(half * 128 + z * 32, 32), 32), :] = values[48:80]
            rel_ref[pl.ds(pl.multiple_of(half * 32 + z * 8, 8), 8), :] = values[32:40]
    owned_ref[...] = rel_ref[0:52, :]
    wait_all([copies.start(in_ref, in_hbm), copies.start(out_ref, out_hbm), copies.start(owned_ref, rel_hbm)])


def shards(
    hidden,
    desc_len,
    w_in,
    w_out,
    send_order,
    place_order,
    cache,
    halo_rows,
    edge_src,
    edge_dst,
    edge_rel,
    rel_table,
    w_msg,
    w_self,
    d_out,
):
    entities, length, width = hidden.shape
    tokens = entities * length
    units = w_in.shape[1]
    my_core = lax.axis_index("core")
    where = jnp.stack([lax.axis_index(name) for name in ("z", "core", "x", "y")]).astype(I32)
    src, dst, rel = edge_src[0], edge_dst[0], edge_rel[0]
    shard_rows = rel_table.shape[0]

    numbers = jnp.broadcast_to(rel.reshape(1, 4, 4), (4, 4, 4)).reshape(16, 4)
    numbers = lax.all_to_all(jnp.pad(numbers, ((0, 0), (0, 124))), GROUP, 0, 0, tiled=True)

    operands = [hidden.reshape(tokens, width), desc_len[None, :], send_order, rel_table]
    outs = [((tokens + 16, width), BF), ((entities, width), F32), ((576, 512), BF), ((64, width), BF)]
    block, hidden_sum, weights, rel_pad = local_call(
        norm_kernel,
        outs,
        [where, *operands, w_in, w_out],
        like(operands) + filled(outs),
        copies=14,
    )
    blocks = [block, *gather_ring(block, "x", 128)]
    mine = gather_ring(weights, "y", 256)
    other = [shift_by(part, "core", 1) for part in mine]

    halo = halo_rows[0]
    place = place_order[0]
    side = halo.shape[0] // 2
    cache_count = cache.shape[0]
    boundary = dot(one_hot(halo - entities, cache_count), cache).astype(BF)
    halo_hot = halo[:, None] == jnp.arange(entities, dtype=I32)[None, :]
    halo_place = jnp.where(halo < entities, jnp.sum(jnp.where(halo_hot, place[None, :], 0), axis=1), 16)

    def edge_of(rows, places):
        return jnp.concatenate([rows, jnp.pad(row_of(places, width), ((0, 15), (0, 0)))], axis=0)

    to_high, to_low = edge_of(boundary[side:], halo_place[side:]), edge_of(boundary[:side], halo_place[:side])
    from_low = shift_by(to_high, GROUP, 1)
    from_high = shift_by(to_low, GROUP, 15)
    mine[2], from_low, from_high = lax.optimization_barrier((mine[2], from_low, from_high))

    outs = [
        ((256, width), BF),
        ((4 * tokens, width), BF),
        ((4 * tokens, 4 * units), BF),
        ((4 * entities, 4 * units), BF),
        ((4 * units, width), BF),
        ((4 * entities, 256), BF),
        ((4 * entities, 128), F32),
        ((512, 256), BF),
    ]
    outgoing, normed, slope, pooled, all_out, route, inverse, rel_hot = local_call(
        encode_kernel,
        outs,
        [where, *blocks, w_in, w_out, rel_pad, *mine, *other, hidden_sum, numbers],
        filled(outs)
        + [
            pltpu.VMEM((width, 4 * units), BF),
            pltpu.VMEM((4 * entities, tokens), BF),
            pltpu.VMEM((256, width), BF),
            pltpu.VMEM((4, 16, 128), BF),
            pltpu.VMEM((entities, width), F32),
            pltpu.VMEM((16, 128), I32),
        ],
        copies=64,
        flops=2 * 4 * tokens * width * 4 * units,
    )

    own_row = jnp.concatenate([fresh_row(0, place), jnp.full((cache_count,), -1, I32)])
    node_count = entities + cache_count
    extended_count = node_count + 2 * side
    edge_count = src.shape[0]
    block_count = rel.shape[0]
    src_hot = one_hot(src, extended_count)
    arrived = lax.all_to_all(outgoing.reshape(16, 16, width), GROUP, 0, 0, tiled=True).reshape(256, width)
    arrived, normed_t = lax.optimization_barrier((arrived, normed.T))

    outs = [((256, width), BF)] + [((node_count, width), BF)] * 4
    operands = [
        arrived,
        one_hot_t(own_row, 64),
        src_hot,
        one_hot(dst, node_count),
        one_hot_t(dst, node_count),
        w_msg,
        w_self,
        d_out,
    ]
    grad_table, graph_out, aggregate, nodes, grad_pre = local_call(
        graph_kernel,
        outs,
        [where, *operands, cache, from_low, from_high],
        like(operands)
        + filled([((64, width), BF), *outs[1:]])
        + [
            pltpu.VMEM((extended_count, width), BF),
            pltpu.VMEM((2, 16, 128), BF),
            pltpu.VMEM((64, extended_count), BF),
            pltpu.VMEM((64, edge_count), BF),
            pltpu.VMEM((extended_count, width), BF),
            pltpu.VMEM((edge_count, width), BF),
            pltpu.VMEM((edge_count, width), BF),
            pltpu.VMEM((node_count, width), BF),
            pltpu.VMEM((block_count, 1, width), F32),
            pltpu.VMEM((block_count, 1, width), F32),
            pltpu.VMEM((block_count, width), BF),
        ],
        copies=30,
        flops=6 * 10**9,
    )

    returned = lax.all_to_all(grad_table.reshape(16, 16, width), GROUP, 0, 0, tiled=True).reshape(256, width)

    outs = [((4, 16, 16, width), BF)] * 2
    operands = [aggregate, nodes, grad_pre]
    graph_kept, graph_given = local_call(
        weight_kernel, outs, [where, *operands], like(operands) + filled(outs), flops=10**9
    )
    returned, graph_kept, graph_given = lax.optimization_barrier((returned, graph_kept, graph_given))
    chip = (graph_kept.astype(F32) + shift_by(graph_given, "core", 1).astype(F32)).astype(BF)

    outs = [((4, 4, 48, width), BF), ((4, 4, 32, width), BF)] * 2
    operands = [returned, route, inverse, rel_hot, pooled, all_out, slope, normed_t]
    in_given, out_given, in_kept, out_kept = local_call(
        back_kernel,
        outs,
        [where, *operands],
        like(operands)
        + filled(outs)
        + [pltpu.VMEM((4 * entities, width), BF), pltpu.VMEM((4 * tokens, 4 * units), BF)],
        copies=14,
        flops=2 * 4 * tokens * width * 4 * units,
    )
    in_other, chip = lax.optimization_barrier((shift_by(in_given, "core", 1), chip))
    line = lax.all_to_all(chip, "x", 0, 0, tiled=True)
    plane = lax.all_to_all(jnp.sum(line.astype(F32), axis=0).astype(BF), ("z", "y"), 0, 0, tiled=True)
    weight_rows = jnp.sum(plane.astype(F32), axis=0)
    grad_msg, grad_self = weight_rows[:8], weight_rows[8:]
    in_chip = (in_kept.astype(F32) + in_other.astype(F32)).astype(BF)
    in_chip, out_given = lax.optimization_barrier((in_chip, out_given))
    out_chip = (out_kept.astype(F32) + shift_by(out_given, "core", 1).astype(F32)).astype(BF)
    out_part = reduce_ring([out_chip[i].reshape(128, width) for i in range(4)], "y").reshape(4, 32, width)
    in_part = reduce_ring([in_chip[i].reshape(192, width) for i in range(4)], "z").reshape(4, 48, width)
    out_part = reduce_ring([out_part[i] for i in range(4)], "z")
    in_part = reduce_ring([in_part[i] for i in range(4)], "y")
    part = jnp.concatenate([in_part, out_part], axis=0)
    parts = [part] + [shift_by(part, "z", s) for s in SHIFTS]
    others = [shift_by(piece, "core", 1) for piece in parts]
    outs = [((width, units), F32), ((units, width), F32), ((shard_rows, width), F32)]
    operands = [*parts, *others]
    grad_w_in, grad_w_out, grad_rel = local_call(
        place_kernel,
        outs,
        [where, *operands],
        like(operands) + filled(outs) + [pltpu.VMEM((64, width), F32)],
        copies=12,
    )
    return (graph_out, grad_w_in, grad_w_out, grad_rel, grad_msg, grad_self)


def solution(mesh):
    fine = Mesh(mesh.devices.reshape(4, 2, 4, 4), ("z", "core", "x", "y"))
    every = ("z", "core", "x", "y")
    placed = (
        P(every, None, None),
        P(every),
        P(None, GROUP),
        P(GROUP, None),
        P(every, None),
        P(every, None),
        P(every, None),
        P(every, None),
        P(every, None),
        P(every, None),
        P(every, None),
        P(GROUP, None),
        P(),
        P(),
        P(every, None),
    )
    return jax.shard_map(
        shards,
        mesh=fine,
        in_specs=placed,
        out_specs=(
            P(every, None),
            P(None, GROUP),
            P(GROUP, None),
            P(GROUP, None),
            P(every, None),
            P(every, None),
        ),
        check_vma=False,
    )
```

```python
import jax
import jax.numpy as jnp
import numpy as np
from jax import lax
from jax.experimental import pallas as pl
from jax.experimental.pallas import tpu as pltpu
from jax.sharding import Mesh
from jax.sharding import PartitionSpec as P

BF = jnp.bfloat16
F32 = jnp.float32
I32 = jnp.int32
GROUP = ("x", "y")
SHIFTS = (1, 3, 2)
ORIGINS = (0, 3, 1, 2)
GELU_SCALE = float(np.sqrt(2.0 / np.pi))
GELU_CUBE = 0.044715


def shift_by(value, axis, shift):
    count = lax.axis_size(axis)
    return lax.ppermute(value, axis, [(i, (i + shift) % count) for i in range(count)])


def dot(a, b):
    return jnp.dot(a, b, preferred_element_type=F32)


def dot_t(a, b):
    return lax.dot_general(a, b, (((0,), (0,)), ((), ())), preferred_element_type=F32)


def dot_bt(a, b):
    return lax.dot_general(a, b, (((1,), (1,)), ((), ())), preferred_element_type=F32)


def one_hot(index, count):
    return (index[:, None] == jnp.arange(count, dtype=I32)[None, :]).astype(BF)


def one_hot_t(index, count):
    return (index[None, :] == jnp.arange(count, dtype=I32)[:, None]).astype(BF)


def lanes(shape):
    return lax.broadcasted_iota(I32, shape, 1)


def sublanes(shape):
    return lax.broadcasted_iota(I32, shape, 0)


def row_of(values, width):
    return jnp.pad(values.astype(BF), (0, width - values.shape[0]))[None, :]


def gather_ring(value, axis, cut):
    low, high = shift_by(value, axis, 1), shift_by(value, axis, 3)
    return [low, high, shift_by(low[:cut], axis, 1), shift_by(high[cut:], axis, 3)]


def reduce_ring(chunks, axis):
    total = chunks[0].astype(F32)
    for chunk, origin in zip(chunks[1:], ORIGINS[1:]):
        total = total + shift_by(chunk, axis, origin).astype(F32)
    return total.astype(BF)


def fresh_row(side, place):
    return (place % 4) * 16 + (side + 1) * 4 + place // 4


class Copies:
    def __init__(self, sems):
        self.sems, self.used = sems, 0

    def start(self, source, target):
        copy = pltpu.make_async_copy(source, target, self.sems.at[self.used])
        self.used += 1
        copy.start()
        return copy


def local_call(body, outs, operands, scratch=(), copies=8, flops=0, limit=60):
    def kernel(*refs):
        body(Copies(refs[-1]), *refs[:-1])

    return pl.pallas_call(
        kernel,
        out_shape=[jax.ShapeDtypeStruct(shape, kind) for shape, kind in outs],
        in_specs=[pl.BlockSpec(memory_space=pltpu.SMEM)]
        + [pl.BlockSpec(memory_space=pltpu.HBM)] * (len(operands) - 1),
        out_specs=[pl.BlockSpec(memory_space=pltpu.HBM)] * len(outs),
        scratch_shapes=[*scratch, pltpu.SemaphoreType.DMA((copies,))],
        compiler_params=pltpu.CompilerParams(vmem_limit_bytes=limit * 1024 * 1024),
        cost_estimate=pl.CostEstimate(flops=flops, bytes_accessed=1024 * 1024, transcendentals=0),
    )(*operands)


def like(arrays):
    return [pltpu.VMEM(array.shape, array.dtype) for array in arrays]


def filled(outs):
    return [pltpu.VMEM(shape, kind) for shape, kind in outs]


def wait_all(copies):
    for copy in copies:
        copy.wait()


def length_column(meta):
    shape = meta.shape
    return jnp.sum(jnp.where(lanes(shape) == sublanes(shape), meta, 0.0), axis=1, keepdims=True)


def pool_rows(length, tokens):
    shape = (16, tokens)
    line = lanes(shape)
    inside = (line // 16 == sublanes(shape)) & ((line % 16).astype(F32) < length)
    return inside.astype(F32).astype(BF)


def norm_kernel(
    copies,
    where_ref,
    hidden_hbm, lens_hbm, order_hbm, table_hbm, in_hbm, out_hbm,
    block_hbm, sum_hbm, weights_hbm, padded_hbm,
    hidden_ref, lens_ref, order_ref, table_ref,
    block_ref, sum_ref, weights_ref, padded_ref,
):
    core = where_ref[1]
    table = copies.start(table_hbm, table_ref)
    packed = []
    for i in range(2):
        cols, wide = pl.ds(i * 256, 256), pl.ds(i * 512, 512)
        source = in_hbm.at[pl.ds(pl.multiple_of(core * 512 + i * 256, 256), 256), :]
        packed.append(copies.start(source, weights_ref.at[pl.ds(0, 256), cols]))
        source = out_hbm.at[pl.ds(pl.multiple_of(core * 128, 128), 128), wide]
        packed.append(copies.start(source, weights_ref.at[pl.ds(256 + i * 128, 128), :]))
    first = [
        copies.start(hidden_hbm, hidden_ref),
        copies.start(lens_hbm, lens_ref),
        copies.start(order_hbm, order_ref),
    ]
    table.wait()
    spread = (lanes((64, 52)) == sublanes((64, 52))).astype(F32).astype(BF)
    padded_ref[...] = dot(spread, table_ref[...]).astype(BF)
    own = padded_ref[pl.ds(pl.multiple_of(core * 32, 32), 32), :]
    weights_ref[512:544, :] = own[:, 0:512]
    weights_ref[544:576, :] = own[:, 512:1024]
    wait_all(packed)
    later = [copies.start(weights_ref, weights_hbm), copies.start(padded_ref, padded_hbm)]
    wait_all(first)
    meta = jnp.zeros((16, 128), F32)
    for i, row in enumerate((lens_ref[...], order_ref[...])):
        values = jnp.broadcast_to(row.astype(F32), (16, 16)).astype(BF)
        select = (lanes((16, 128)) == sublanes((16, 128)) + 16 * i).astype(F32).astype(BF)
        meta = meta + dot(values, select)
    values = hidden_ref[...].astype(F32)
    center = values - jnp.mean(values, axis=-1, keepdims=True)
    spread = jnp.mean(center * center, axis=-1, keepdims=True)
    tokens = values.shape[0]
    block_ref[0:tokens, :] = (center * lax.rsqrt(spread + 1e-05)).astype(BF)
    block_ref[tokens : tokens + 16, :] = jnp.zeros((16, values.shape[1]), BF)
    block_ref[tokens : tokens + 16, 0:128] = meta.astype(BF)
    later.append(copies.start(block_ref, block_hbm))
    sum_ref[...] = dot(pool_rows(length_column(meta), tokens), hidden_ref[...])
    later.append(copies.start(sum_ref, sum_hbm))
    wait_all(later)


def encode_kernel(
    copies,
    where_ref,
    b0, b1, b2, b3_top, b3_rest,
    own_in, own_out, own_rel,
    m1, m2, m3_in, m3_rest,
    o1, o2, o3_in, o3_rest,
    hidden_sum_hbm, numbers_hbm,
    outgoing_hbm, normed_hbm, slope_hbm, pooled_hbm, all_out_hbm, route_hbm, length_hbm, rel_hot_hbm,
    outgoing_ref, normed_ref, slope_ref, pooled_ref, all_out_ref, route_ref, length_ref, rel_hot_ref,
    in_ref, pool_ref, rel_ref, meta_ref, hidden_sum_ref, numbers_ref,
):
    core, my_x, my_y = where_ref[1], where_ref[2], where_ref[3]
    metas, tokens, weights, tables = [], [], [[], [], [], []], []
    for s, (block, row) in enumerate(((b0, 256), (b1, 256), (b2, 256), (b3_rest, 128))):
        metas.append(copies.start(block.at[pl.ds(row, 16), pl.ds(0, 128)], meta_ref.at[s]))
    tables.append(copies.start(own_rel, rel_ref.at[pl.ds(0, 64), :]))
    tables.append(copies.start(numbers_hbm, numbers_ref))
    pieces = []
    for t, (mine, other) in enumerate(
        (((m1, m1, 256), (o1, o1, 256)), ((m2, m2, 256), (o2, o2, 256)), ((m3_in, m3_rest, 0), (o3_in, o3_rest, 0))), 1
    ):
        for (inner, rest, at), half in ((mine, core), (other, 1 - core)):
            pieces.append((t, inner, rest, at, half))
            for i in range(2):
                rows = pl.ds(pl.multiple_of(t * 64 + half * 32, 32), 32)
                target = rel_ref.at[rows, pl.ds(i * 512, 512)]
                tables.append(copies.start(rest.at[pl.ds(at + 256 + i * 32, 32), :], target))
    for s, (block, row, count) in enumerate(((b0, 0, 256), (b1, 256, 256), (b2, 512, 256), (b3_top, 768, 128), (b3_rest, 896, 128))):
        tokens.append(copies.start(block.at[pl.ds(0, count), :], normed_ref.at[pl.ds(row, count), :]))
    weights[0].append(copies.start(own_in, in_ref.at[:, pl.ds(0, 256)]))
    for t, inner, rest, at, half in pieces:
        for i in range(2):
            rows = pl.ds(pl.multiple_of(half * 512 + i * 256, 256), 256)
            target = in_ref.at[rows, pl.ds(t * 256, 256)]
            weights[t].append(copies.start(inner.at[pl.ds(0, 256), pl.ds(i * 256, 256)], target))
    outer = [
        copies.start(own_out, all_out_ref.at[pl.ds(0, 256), :]),
        copies.start(hidden_sum_hbm, hidden_sum_ref),
    ]
    for t, inner, rest, at, half in pieces:
        for i in range(2):
            rows = pl.ds(pl.multiple_of(t * 256 + half * 128, 128), 128)
            target = all_out_ref.at[rows, pl.ds(i * 512, 512)]
            outer.append(copies.start(rest.at[pl.ds(at + i * 128, 128), :], target))
    wait_all(metas)
    wait_all(tables)

    wide = (16, 256)
    slot = lanes(wide) % 16
    bound = lanes((128, 256))
    bound = (bound // 16 + (bound % 16) // 4 + 15) % 16
    bound_hot = (sublanes((128, 256)) == bound + 16).astype(F32).astype(BF)
    for s in range(4):
        meta = meta_ref[s]
        values = meta.astype(F32)
        length = length_column(values)
        length_ref[s * 16 : (s + 1) * 16, :] = jnp.broadcast_to(1.0 / length, (16, 128))
        pool_ref[s * 16 : (s + 1) * 16, :] = pool_rows(length, 256)
        sent = dot(meta, bound_hot)
        encoder = lax.rem(my_x + ORIGINS[s], 4)
        chosen = (sent == sublanes(wide).astype(F32)) & (slot % 4 == encoder) & (slot < 12)
        route_ref[s * 16 : (s + 1) * 16, :] = chosen.astype(F32).astype(BF)

    high = numbers_ref[...] // 32
    digits = (high.astype(F32).astype(BF), (numbers_ref[...] - 32 * high).astype(F32).astype(BF))
    tall, flat = (256, 128), (16, 256)
    chosen = lanes(tall) == sublanes(tall) % 16 - 12
    source_hot = (sublanes((256, 16)) // 16 == lanes((256, 16))).astype(F32).astype(BF)
    column = [jnp.sum(jnp.where(chosen, dot(source_hot, part), 0.0), axis=1, keepdims=True) for part in digits]
    line = lanes((256, 256))
    owner_y = (my_y + jnp.where(line < 64, 0, jnp.where(line < 128, 3, line // 64 - 1))) % 4
    name = ((my_x * 4 + owner_y) * 52 + line % 64).astype(F32)
    served = (name == 32.0 * column[0] + column[1]) & (line % 64 < 52) & (sublanes((256, 256)) % 16 >= 12)
    slot_hot = (sublanes((128, 256)) == lanes((128, 256)) % 16 - 12).astype(F32).astype(BF)
    own = sublanes(flat) == lanes(flat) // 16
    row = [jnp.sum(jnp.where(own, dot(part, slot_hot), 0.0), axis=0, keepdims=True) for part in digits]
    line = sublanes((512, 256))
    local = (line // 64) % 2 * 32 + (line // 16) % 4 * 8 + line % 16
    name = ((my_x * 4 + line // 128) * 52 + local).astype(F32)
    good = (line % 16 < 8) & (local < 52) & (lanes((512, 256)) % 16 >= 12)
    rel_hot_ref[...] = ((name == 32.0 * row[0] + row[1]) & good).astype(F32).astype(BF)
    relations = dot(served.astype(F32).astype(BF), rel_ref[...])

    sent_out = [
        copies.start(route_ref, route_hbm),
        copies.start(length_ref, length_hbm),
        copies.start(rel_hot_ref, rel_hot_hbm),
    ]
    wait_all(tokens)
    sent_out.append(copies.start(normed_ref, normed_hbm))
    for t in range(4):
        cols = slice(t * 256, (t + 1) * 256)
        wait_all(weights[t])

        @pl.loop(0, 2)
        def _(s):
            rows = pl.ds(pl.multiple_of(s * 512, 512), 512)
            pre = dot(normed_ref[rows, :], in_ref[:, cols])
            square = pre * pre
            tanh = jnp.tanh(GELU_SCALE * pre * (1.0 + GELU_CUBE * square))
            upper = 0.5 + 0.5 * tanh
            slope = upper + (0.5 * GELU_SCALE) * pre * (1.0 - tanh * tanh) * (1.0 + 3.0 * GELU_CUBE * square)
            slope_ref[rows, cols] = slope.astype(BF)
            activation = (pre * upper).astype(BF)
            for i in range(2):
                few = pl.ds(pl.multiple_of(s * 32 + i * 16, 16), 16)
                pooled = dot(pool_ref[few, :], activation[i * 256 : (i + 1) * 256])
                pooled_ref[few, cols] = pooled.astype(BF)

    sent_out.append(copies.start(slope_ref, slope_hbm))
    sent_out.append(copies.start(pooled_ref, pooled_hbm))
    wait_all(outer)
    sent_out.append(copies.start(all_out_ref, all_out_hbm))
    partial = dot(pooled_ref[...], all_out_ref[...])
    partial = jnp.concatenate([partial[0:16] + hidden_sum_ref[...], partial[16:64]], axis=0)
    partial = (partial * length_ref[:, 0:1]).astype(BF)
    outgoing_ref[...] = (dot_t(route_ref[...], partial) + relations).astype(BF)
    sent_out.append(copies.start(outgoing_ref, outgoing_hbm))
    wait_all(sent_out)


def graph_kernel(
    copies,
    where_ref,
    arrived_hbm, own_hot_t_hbm,
    src_hot_hbm, dst_hot_hbm, dst_hot_t_hbm,
    w_msg_hbm, w_self_hbm, d_out_hbm,
    cache_hbm, low_hbm, high_hbm,
    table_out_hbm, graph_out_hbm, aggregate_hbm, nodes_hbm, pre_hbm,
    arrived_ref, own_hot_t_ref,
    src_hot_ref, dst_hot_ref, dst_hot_t_ref,
    w_msg_ref, w_self_ref, d_out_ref,
    table_out_ref, graph_out_ref, aggregate_ref, nodes_ref, pre_ref,
    base_ref, places_ref, row_hot_t_ref, src_row_hot_ref,
    ext_ref, sources_ref, edges_ref, agg_grad_ref, sums_ref, rel_ref, blocks_ref,
):
    scale = (256 / 2048) ** 0.5
    first = [
        copies.start(low_hbm.at[pl.ds(64, 16), pl.ds(0, 128)], places_ref.at[0]),
        copies.start(high_hbm.at[pl.ds(64, 16), pl.ds(0, 128)], places_ref.at[1]),
        copies.start(own_hot_t_hbm, own_hot_t_ref),
        copies.start(arrived_hbm, arrived_ref),
        copies.start(cache_hbm, base_ref.at[pl.ds(16, 240), :]),
        copies.start(low_hbm.at[pl.ds(0, 64), :], base_ref.at[pl.ds(256, 64), :]),
        copies.start(high_hbm.at[pl.ds(0, 64), :], base_ref.at[pl.ds(320, 64), :]),
        copies.start(src_hot_hbm, src_hot_ref),
    ]
    second = [copies.start(dst_hot_t_hbm, dst_hot_t_ref)]
    third = [
        copies.start(w_msg_hbm, w_msg_ref),
        copies.start(w_self_hbm, w_self_ref),
        copies.start(d_out_hbm, d_out_ref),
    ]
    fourth = [copies.start(dst_hot_hbm, dst_hot_ref)]
    base_ref[0:16, :] = jnp.zeros((16, 1024), BF)
    wait_all(first)
    to = lanes((128, 128)) - sublanes((128, 128))
    inside = sublanes((128, 128)) < 64
    low_move = ((to == 0) & inside).astype(F32).astype(BF)
    high_move = ((to == 64) & inside).astype(F32).astype(BF)
    places = (dot(places_ref[0], low_move) + dot(places_ref[1], high_move))[0:1].astype(I32)
    upper = (lax.broadcasted_iota(I32, (1, 128), 1) >= 64).astype(I32)
    table_row = jnp.where(places < 16, (places % 4) * 16 + upper * 8 + places // 4, -1)
    row_hot_t_ref[:, 0:256] = own_hot_t_ref[...]
    row_hot_t_ref[:, 256:384] = (sublanes((64, 128)) == table_row).astype(F32).astype(BF)
    src_row_hot_ref[...] = dot_bt(row_hot_t_ref[...], src_hot_ref[...]).astype(BF)
    total = arrived_ref[0:64, :].astype(F32)
    for i in range(1, 4):
        total = total + arrived_ref[i * 64 : (i + 1) * 64, :].astype(F32)
    for j in range(16):
        at = j // 4 * 16 + 12 + j % 4
        rel_ref[j] = total[at : at + 1]
    table = total.astype(BF)
    ext_ref[...] = (base_ref[...].astype(F32) + dot_t(row_hot_t_ref[...], table)).astype(BF)
    nodes_ref[...] = ext_ref[0:256, :]
    sent_out = [copies.start(nodes_ref, nodes_hbm)]

    for n in range(4):
        cols = slice(n * 256, (n + 1) * 256)

        @pl.loop(0, 4)
        def _(k):
            rows = pl.ds(pl.multiple_of(k * 512, 512), 512)
            taken = dot(src_hot_ref[rows, :], ext_ref[:, cols])
            taken = taken.astype(BF)
            sources_ref[rows, cols] = taken
            for i in range(4):
                few = pl.ds(pl.multiple_of(k * 512 + i * 128, 128), 128)
                edges_ref[few, cols] = taken[i * 128 : (i + 1) * 128] * rel_ref[k * 4 + i, :, cols].astype(BF)

    wait_all(second)

    @pl.loop(0, 4)
    def _(n):
        cols = pl.ds(pl.multiple_of(n * 256, 256), 256)
        aggregate_ref[:, cols] = (scale * dot(dst_hot_t_ref[...], edges_ref[:, cols])).astype(BF)

    sent_out.append(copies.start(aggregate_ref, aggregate_hbm))
    wait_all(third)

    @pl.loop(0, 4)
    def _(n):
        cols = pl.ds(pl.multiple_of(n * 256, 256), 256)
        out_pre = dot(aggregate_ref[...], w_msg_ref[:, cols]) + dot(nodes_ref[...], w_self_ref[:, cols])
        squashed = jnp.tanh(out_pre)
        graph_out_ref[:, cols] = squashed.astype(BF)
        pre_ref[:, cols] = (d_out_ref[:, cols].astype(F32) * (1.0 - squashed * squashed)).astype(BF)

    sent_out.append(copies.start(graph_out_ref, graph_out_hbm))
    sent_out.append(copies.start(pre_ref, pre_hbm))

    @pl.loop(0, 4)
    def _(n):
        cols = pl.ds(pl.multiple_of(n * 256, 256), 256)
        agg_grad_ref[:, cols] = (scale * dot_bt(pre_ref[...], w_msg_ref[cols, :])).astype(BF)

    wait_all(fourth)

    for n in range(4):
        cols = slice(n * 256, (n + 1) * 256)

        @pl.loop(0, 4)
        def _(k):
            rows = pl.ds(pl.multiple_of(k * 512, 512), 512)
            at_dest = dot(dst_hot_ref[rows, :], agg_grad_ref[:, cols])
            for i in range(4):
                few = pl.ds(pl.multiple_of(k * 512 + i * 128, 128), 128)
                part = at_dest[i * 128 : (i + 1) * 128]
                edges_ref[few, cols] = part.astype(BF) * rel_ref[k * 4 + i, :, cols].astype(BF)
                product = part * sources_ref[few, cols].astype(F32)
                sums_ref[k * 4 + i, :, cols] = jnp.sum(product, axis=0, keepdims=True)

    blocks_ref[...] = jnp.concatenate([sums_ref[j] for j in range(16)], axis=0).astype(BF)
    block = lanes((64, 16))
    block_hot = (sublanes((64, 16)) == block // 4 * 16 + 12 + block % 4).astype(F32).astype(BF)
    own_pre = dot(own_hot_t_ref[...], pre_ref[...]).astype(BF)

    @pl.loop(0, 4)
    def _(n):
        cols = pl.ds(pl.multiple_of(n * 256, 256), 256)
        grad = dot(src_row_hot_ref[...], edges_ref[:, cols]) + dot_bt(own_pre, w_self_ref[cols, :])
        grad = grad + dot(block_hot, blocks_ref[:, cols])
        table_out_ref[:, cols] = grad.astype(BF)

    for x in range(4):
        sent_out.append(copies.start(table_out_ref, table_out_hbm.at[pl.ds(x * 64, 64), :]))
    wait_all(sent_out)


def weight_kernel(
    copies,
    where_ref,
    aggregate_hbm, nodes_hbm, pre_hbm,
    kept_hbm, given_hbm,
    aggregate_ref, nodes_ref, pre_ref,
    kept_ref, given_ref,
):
    core = where_ref[1]
    wait_all(
        [copies.start(aggregate_hbm, aggregate_ref), copies.start(nodes_hbm, nodes_ref), copies.start(pre_hbm, pre_ref)]
    )
    sent_out = []
    for half, chunk_ref, chunk_hbm in ((1 - core, given_ref, given_hbm), (core, kept_ref, kept_hbm)):

        @pl.loop(0, 4)
        def _(z):
            rows = pl.ds(pl.multiple_of(z * 256 + half * 128, 128), 128)
            msg = dot_t(aggregate_ref[:, rows], pre_ref[...])
            own = dot_t(nodes_ref[:, rows], pre_ref[...])
            for x in range(4):
                for y in range(4):
                    at = (x * 4 + y) * 8
                    both = jnp.concatenate([msg[at : at + 8], own[at : at + 8]], axis=0)
                    chunk_ref[x, z * 4 + y] = both.astype(BF)

        sent_out.append(copies.start(chunk_ref, chunk_hbm))
    wait_all(sent_out)


def ring_places(mine):
    places = []
    for at in range(4):
        ahead = lax.rem(at - mine + 4, 4)
        places.append(jnp.where(ahead == 0, 0, jnp.where(ahead == 3, 1, ahead + 1)))
    return places


def back_kernel(
    copies,
    where_ref,
    returned_hbm, route_hbm, length_hbm, rel_hot_hbm, pooled_hbm, all_out_hbm, slope_hbm, normed_t_hbm,
    in_given_hbm, out_given_hbm, in_kept_hbm, out_kept_hbm,
    returned_ref, route_ref, length_ref, rel_hot_ref, pooled_ref, all_out_ref, slope_ref, normed_t_ref,
    in_given_ref, out_given_ref, in_kept_ref, out_kept_ref,
    scaled_ref, grad_ref,
):
    my_z, core, my_y = where_ref[0], where_ref[1], where_ref[3]
    first = [
        copies.start(returned_hbm, returned_ref),
        copies.start(route_hbm, route_ref),
        copies.start(length_hbm, length_ref),
        copies.start(rel_hot_hbm, rel_hot_ref),
        copies.start(pooled_hbm, pooled_ref),
    ]
    second = [copies.start(all_out_hbm, all_out_ref), copies.start(slope_hbm, slope_ref)]
    third = [copies.start(normed_t_hbm, normed_t_ref)]
    places = ring_places(my_z)
    pools = []
    wait_all(first)
    scaled_ref[...] = (dot(route_ref[...], returned_ref[...]) * length_ref[:, 0:1]).astype(BF)
    for s in range(4):
        line = lanes((16, 256))
        length = 1.0 / length_ref[s * 16 : (s + 1) * 16, 0:1]
        inside = (line // 16 == sublanes((16, 256))) & ((line % 16).astype(F32) + 0.5 < length)
        pools.append(inside.astype(F32).astype(BF))
    wait_all(second)

    @pl.loop(0, 4)
    def _(t):
        cols = pl.ds(pl.multiple_of(t * 256, 256), 256)
        upstream = dot_bt(scaled_ref[...], all_out_ref[cols, :]).astype(BF)
        for s in range(4):
            rows = slice(s * 256, (s + 1) * 256)
            at_tokens = dot_t(pools[s], upstream[s * 16 : (s + 1) * 16])
            grad_ref[rows, cols] = (slope_ref[rows, cols].astype(F32) * at_tokens).astype(BF)

    wait_all(third)
    sent_out = []
    for half, in_ref, in_hbm, out_ref, out_hbm in (
        (1 - core, in_given_ref, in_given_hbm, out_given_ref, out_given_hbm),
        (core, in_kept_ref, in_kept_hbm, out_kept_ref, out_kept_hbm),
    ):

        @pl.loop(0, 4)
        def _(t):
            cols = pl.ds(pl.multiple_of(t * 256, 256), 256)
            origin = jnp.where(t == 0, 0, jnp.where(t == 1, 3, t - 1))
            owner = lax.rem(my_y + origin, 4)
            units = pl.ds(pl.multiple_of(t * 256 + half * 128, 128), 128)
            out = dot_t(pooled_ref[:, units], scaled_ref[...]).astype(BF)
            rel_rows = pl.ds(pl.multiple_of(owner * 128 + half * 64, 64), 64)
            rel = dot(rel_hot_ref[rel_rows, :], returned_ref[...]).astype(BF)
            inner = dot(normed_t_ref[pl.ds(pl.multiple_of(half * 512, 512), 512), :], grad_ref[:, cols]).astype(BF)
            for z in range(4):
                out_ref[t, places[z], :, :] = out[z * 32 : (z + 1) * 32]
                in_ref[places[z], t, 32:48, :] = rel[z * 16 : (z + 1) * 16]
                for i in range(4):
                    piece = inner[z * 128 + i * 32 : z * 128 + (i + 1) * 32]
                    in_ref[places[z], t, 0:32, i * 256 : (i + 1) * 256] = piece

        sent_out.append(copies.start(in_ref, in_hbm))
        sent_out.append(copies.start(out_ref, out_hbm))
    wait_all(sent_out)


def place_kernel(
    copies,
    where_ref,
    h0, h1, h2, h3, h4, h5, h6, h7,
    in_hbm, out_hbm, rel_hbm,
    a0, a1, a2, a3, c0, c1, c2, c3,
    in_ref, out_ref, owned_ref, rel_ref,
):
    sources = (h0, h1, h2, h3, h4, h5, h6, h7)
    targets = (a0, a1, a2, a3, c0, c1, c2, c3)
    wait_all([copies.start(source, target) for source, target in zip(sources, targets)])
    my_z, core = where_ref[0], where_ref[1]
    for pieces, half in (((a0, a1, a2, a3), core), ((c0, c1, c2, c3), 1 - core)):
        for piece, origin in zip(pieces, ORIGINS):
            z = lax.rem(my_z + origin, 4)
            values = piece[...].astype(F32)
            for i in range(4):
                rows = pl.ds(pl.multiple_of(half * 512 + z * 128 + i * 32, 32), 32)
                in_ref[rows, :] = values[0:32, i * 256 : (i + 1) * 256]
            out_ref[pl.ds(pl.multiple_of(half * 128 + z * 32, 32), 32), :] = values[48:80]
            rel_ref[pl.ds(pl.multiple_of(half * 32 + z * 8, 8), 8), :] = values[32:40]
    owned_ref[...] = rel_ref[0:52, :]
    wait_all([copies.start(in_ref, in_hbm), copies.start(out_ref, out_hbm), copies.start(owned_ref, rel_hbm)])


def shards(
    hidden,
    desc_len,
    w_in,
    w_out,
    send_order,
    place_order,
    cache,
    halo_rows,
    edge_src,
    edge_dst,
    edge_rel,
    rel_table,
    w_msg,
    w_self,
    d_out,
):
    entities, length, width = hidden.shape
    tokens = entities * length
    units = w_in.shape[1]
    my_core = lax.axis_index("core")
    where = jnp.stack([lax.axis_index(name) for name in ("z", "core", "x", "y")]).astype(I32)
    src, dst, rel = edge_src[0], edge_dst[0], edge_rel[0]
    shard_rows = rel_table.shape[0]

    numbers = jnp.broadcast_to(rel.reshape(1, 4, 4), (4, 4, 4)).reshape(16, 4)
    numbers = lax.all_to_all(jnp.pad(numbers, ((0, 0), (0, 124))), GROUP, 0, 0, tiled=True)

    operands = [hidden.reshape(tokens, width), desc_len[None, :], send_order, rel_table]
    outs = [((tokens + 16, width), BF), ((entities, width), F32), ((576, 512), BF), ((64, width), BF)]
    block, hidden_sum, weights, rel_pad = local_call(
        norm_kernel,
        outs,
        [where, *operands, w_in, w_out],
        like(operands) + filled(outs),
        copies=14,
    )
    blocks = [block, *gather_ring(block, "x", 128)]
    mine = gather_ring(weights, "y", 256)
    other = [shift_by(part, "core", 1) for part in mine]

    halo = halo_rows[0]
    place = place_order[0]
    side = halo.shape[0] // 2
    cache_count = cache.shape[0]
    boundary = dot(one_hot(halo - entities, cache_count), cache).astype(BF)
    halo_hot = halo[:, None] == jnp.arange(entities, dtype=I32)[None, :]
    halo_place = jnp.where(halo < entities, jnp.sum(jnp.where(halo_hot, place[None, :], 0), axis=1), 16)

    def edge_of(rows, places):
        return jnp.concatenate([rows, jnp.pad(row_of(places, width), ((0, 15), (0, 0)))], axis=0)

    to_high, to_low = edge_of(boundary[side:], halo_place[side:]), edge_of(boundary[:side], halo_place[:side])
    from_low = shift_by(to_high, GROUP, 1)
    mine[2], from_low = lax.optimization_barrier((mine[2], from_low))

    outs = [
        ((256, width), BF),
        ((4 * tokens, width), BF),
        ((4 * tokens, 4 * units), BF),
        ((4 * entities, 4 * units), BF),
        ((4 * units, width), BF),
        ((4 * entities, 256), BF),
        ((4 * entities, 128), F32),
        ((512, 256), BF),
    ]
    outgoing, normed, slope, pooled, all_out, route, inverse, rel_hot = local_call(
        encode_kernel,
        outs,
        [where, *blocks, w_in, w_out, rel_pad, *mine, *other, hidden_sum, numbers],
        filled(outs)
        + [
            pltpu.VMEM((width, 4 * units), BF),
            pltpu.VMEM((4 * entities, tokens), BF),
            pltpu.VMEM((256, width), BF),
            pltpu.VMEM((4, 16, 128), BF),
            pltpu.VMEM((entities, width), F32),
            pltpu.VMEM((16, 128), I32),
        ],
        copies=64,
        flops=2 * 4 * tokens * width * 4 * units,
    )

    to_low, outgoing = lax.optimization_barrier((to_low, outgoing))
    from_high = shift_by(to_low, GROUP, 15)
    own_row = jnp.concatenate([fresh_row(0, place), jnp.full((cache_count,), -1, I32)])
    node_count = entities + cache_count
    extended_count = node_count + 2 * side
    edge_count = src.shape[0]
    block_count = rel.shape[0]
    src_hot = one_hot(src, extended_count)
    arrived = lax.all_to_all(outgoing.reshape(16, 16, width), GROUP, 0, 0, tiled=True).reshape(256, width)
    arrived, normed_t = lax.optimization_barrier((arrived, normed.T))

    outs = [((256, width), BF)] + [((node_count, width), BF)] * 4
    operands = [
        arrived,
        one_hot_t(own_row, 64),
        src_hot,
        one_hot(dst, node_count),
        one_hot_t(dst, node_count),
        w_msg,
        w_self,
        d_out,
    ]
    grad_table, graph_out, aggregate, nodes, grad_pre = local_call(
        graph_kernel,
        outs,
        [where, *operands, cache, from_low, from_high],
        like(operands)
        + filled([((64, width), BF), *outs[1:]])
        + [
            pltpu.VMEM((extended_count, width), BF),
            pltpu.VMEM((2, 16, 128), BF),
            pltpu.VMEM((64, extended_count), BF),
            pltpu.VMEM((64, edge_count), BF),
            pltpu.VMEM((extended_count, width), BF),
            pltpu.VMEM((edge_count, width), BF),
            pltpu.VMEM((edge_count, width), BF),
            pltpu.VMEM((node_count, width), BF),
            pltpu.VMEM((block_count, 1, width), F32),
            pltpu.VMEM((block_count, 1, width), F32),
            pltpu.VMEM((block_count, width), BF),
        ],
        copies=30,
        flops=6 * 10**9,
    )

    returned = lax.all_to_all(grad_table.reshape(16, 16, width), GROUP, 0, 0, tiled=True).reshape(256, width)

    outs = [((4, 16, 16, width), BF)] * 2
    operands = [aggregate, nodes, grad_pre]
    graph_kept, graph_given = local_call(
        weight_kernel, outs, [where, *operands], like(operands) + filled(outs), flops=10**9
    )
    returned, graph_kept, graph_given = lax.optimization_barrier((returned, graph_kept, graph_given))
    chip = (graph_kept.astype(F32) + shift_by(graph_given, "core", 1).astype(F32)).astype(BF)

    outs = [((4, 4, 48, width), BF), ((4, 4, 32, width), BF)] * 2
    operands = [returned, route, inverse, rel_hot, pooled, all_out, slope, normed_t]
    in_given, out_given, in_kept, out_kept = local_call(
        back_kernel,
        outs,
        [where, *operands],
        like(operands)
        + filled(outs)
        + [pltpu.VMEM((4 * entities, width), BF), pltpu.VMEM((4 * tokens, 4 * units), BF)],
        copies=14,
        flops=2 * 4 * tokens * width * 4 * units,
    )
    in_other, chip = lax.optimization_barrier((shift_by(in_given, "core", 1), chip))
    line = lax.all_to_all(chip, "x", 0, 0, tiled=True)
    plane = lax.all_to_all(jnp.sum(line.astype(F32), axis=0).astype(BF), ("z", "y"), 0, 0, tiled=True)
    weight_rows = jnp.sum(plane.astype(F32), axis=0)
    grad_msg, grad_self = weight_rows[:8], weight_rows[8:]
    in_chip = (in_kept.astype(F32) + in_other.astype(F32)).astype(BF)
    in_chip, out_given = lax.optimization_barrier((in_chip, out_given))
    out_chip = (out_kept.astype(F32) + shift_by(out_given, "core", 1).astype(F32)).astype(BF)
    out_part = reduce_ring([out_chip[i].reshape(128, width) for i in range(4)], "y").reshape(4, 32, width)
    in_part = reduce_ring([in_chip[i].reshape(192, width) for i in range(4)], "z").reshape(4, 48, width)
    out_part = reduce_ring([out_part[i] for i in range(4)], "z")
    in_part = reduce_ring([in_part[i] for i in range(4)], "y")
    part = jnp.concatenate([in_part, out_part], axis=0)
    parts = [part] + [shift_by(part, "z", s) for s in SHIFTS]
    others = [shift_by(piece, "core", 1) for piece in parts]
    outs = [((width, units), F32), ((units, width), F32), ((shard_rows, width), F32)]
    operands = [*parts, *others]
    grad_w_in, grad_w_out, grad_rel = local_call(
        place_kernel,
        outs,
        [where, *operands],
        like(operands) + filled(outs) + [pltpu.VMEM((64, width), F32)],
        copies=12,
    )
    return (graph_out, grad_w_in, grad_w_out, grad_rel, grad_msg, grad_self)


def solution(mesh):
    fine = Mesh(mesh.devices.reshape(4, 2, 4, 4), ("z", "core", "x", "y"))
    every = ("z", "core", "x", "y")
    placed = (
        P(every, None, None),
        P(every),
        P(None, GROUP),
        P(GROUP, None),
        P(every, None),
        P(every, None),
        P(every, None),
        P(every, None),
        P(every, None),
        P(every, None),
        P(every, None),
        P(GROUP, None),
        P(),
        P(),
        P(every, None),
    )
    return jax.shard_map(
        shards,
        mesh=fine,
        in_specs=placed,
        out_specs=(
            P(every, None),
            P(None, GROUP),
            P(GROUP, None),
            P(GROUP, None),
            P(every, None),
            P(every, None),
        ),
        check_vma=False,
    )
```
